32 devices in a mesh: dom: 2 (over y), atoms: 4 (over z), modes: 2 (over x), sub: 2 (over core).
Axes of the slice: x: 2, y: 2, z: 4, core: 2. Of those that a mesh axis runs over, the one named last changes fastest.
Arguments:
- mode_panel: bfloat16 [3, 6144, 512], P(None, ('dom', 'atoms'), ('modes', 'sub')), parts along dimension 1, may hold values from -6 to 6
- partners: bfloat16 [3, 6144, 2560], P(None, ('dom', 'atoms'), ('modes', 'sub')), parts along dimension 1, may hold values from -6 to 6
- bond_blocks: float32 [9, 6144, 16], P(None, ('dom', 'atoms')), parts along dimension 1, may hold values from -1.5 to 1.5
- neighbors: int32 [6144, 16], P(('dom', 'atoms')), parts along dimension 0, may hold values from 0 to 3071, as said below
- bond_count: int32 [6144], P(('dom', 'atoms')), parts along dimension 0, may hold values from 4 to 16
- panel_freq: float32 [1024], P('dom'), parts along dimension 0, may hold values from 1 to 2
- partner_freq: float32 [5120], P(('dom', 'modes', 'sub')), parts along dimension 0, may hold values from 1 to 2
- win_start: int32 [1024], P('dom'), parts along dimension 0, may hold values from 0 to 1535, as said below
- win_len: int32 [1024], P('dom'), parts along dimension 0, may hold values from 1024 to 2048, as said below
Outputs:
- elements: float32 [1024, 2560], P(('dom', 'atoms'), ('modes', 'sub')), parts along dimension 0
- diffusivity: float32 [1024], P(('dom', 'atoms')), parts along dimension 0
The draws below stay inside these ranges and needn't reach their ends.
There are 2 independent parts, one for each index of `dom`. The reference program is written for one: setup_inputs(seed, part) draws one part's arguments, and reference() takes and returns one part's arrays. A program takes and returns all parts, laid end to end along the dimension named above; each array names one. Nothing has to cross between parts.
Inputs may be any that keep to these rules, and one draw needn't show every extreme that they name: `neighbors`: every neighbor lies within 96 atoms of its own atom in atom order, and some bonds reach exactly 96. Slots k >= bond_count[a] of atom a are padding. Each window lies inside the partner modes: win_start[j] + win_len[j] <= 2560. `win_len`: some panel mode has exactly 2048 partners.
All inputs are finite; a program needn't handle non-finite values.
Results may differ from the reference program's by a relative error of at most 0.003.
Values may be sent and summed in bfloat16 or wider, within the bound.
No kernel may reach another device: no remote copies, remote signals or barrier semaphores. Data moves between devices by JAX's collectives and lax.ppermute only.
A program may use at most 64 MiB of HBM per device.

```python
import math
import jax
import jax.numpy as jnp
from jax import lax

ATOMS = 3072
HALO = 96
BONDS = 16
PANEL = 512
WINDOW = 2048
PARTNERS = 2560


def window_draw(key):
    base = jax.random.fold_in(key, 50)
    key_len, key_pos, key_shift = jax.random.split(base, 3)
    row_ids = jnp.arange(PANEL)
    lengths = jax.random.randint(key_len, (PANEL,), WINDOW // 2, WINDOW + 1)
    chosen = jax.random.randint(key_pos, (), 1, PANEL - 1)
    lengths = jnp.where(row_ids == chosen, WINDOW, lengths)
    lengths = jnp.where(row_ids == PANEL - 1, WINDOW // 2, lengths)
    shifts = jax.random.randint(key_shift, (PANEL,), 0, WINDOW - lengths + 1)
    shifts = jnp.where(row_ids == 0, 0, shifts)
    shifts = jnp.where(row_ids == PANEL - 1, WINDOW - WINDOW // 2, shifts)
    return (row_ids + shifts, lengths)


def draw_win_start(key, part):
    return window_draw(key)[0].astype(jnp.int32)


def draw_win_len(key, part):
    return window_draw(key)[1].astype(jnp.int32)


def draw_neighbors(key, part):
    key = jax.random.fold_in(key, 3)
    key_off, key_sign = jax.random.split(key, 2)
    atom_ids = jnp.arange(ATOMS)[:, None]
    slot_ids = jnp.arange(BONDS)[None, :]
    offsets = jax.random.randint(key_off, (ATOMS, BONDS), 1, HALO + 1)
    offsets = jnp.where((atom_ids + slot_ids) % 97 == 0, HALO, offsets)
    signs = jax.random.randint(key_sign, (ATOMS, BONDS), 0, 2) * 2 - 1
    return jnp.clip(atom_ids + signs * offsets, 0, ATOMS - 1).astype(jnp.int32)


def touch_ends(entries, own_key, least, high):
    dims = entries.shape
    spot = [jax.random.randint(jax.random.fold_in(own_key, axis), (), 0, dims[axis]) for axis in range(len(dims))]
    entries = entries.at[tuple(spot)].set(least)
    longest = dims.index(max(dims))
    spot[longest] = (spot[longest] + 1) % dims[longest]
    return entries.at[tuple(spot)].set(high)


def block_levels(own_key, shape, cuts, low, top_value):
    loudness, own = 1.0, jax.random.fold_in(own_key, 6)
    for dim, blocks in cuts:
        steps = jnp.exp(jax.random.uniform(jax.random.fold_in(own, dim), (blocks,), jnp.float32, low / len(cuts), top_value / len(cuts)))
        loudness = loudness * jnp.repeat(steps, shape[dim] // blocks).reshape([-1 if axis == dim else 1 for axis in range(len(shape))])
    return loudness


def normal_values(own_key, dims, scale, most, cuts=(), kind=jnp.bfloat16):
    drawn = jax.random.normal(own_key, dims, jnp.float32) * scale
    if len(cuts) > 0:
        drawn = block_levels(own_key, dims, cuts, -0.22, 0.18) * drawn
    return jnp.clip(drawn, min=-most, max=most).astype(kind)


def setup_inputs(seed: int = 0, part: int = 0) -> dict:
    keys = jax.random.split(jax.random.key(seed), 10)
    part_splits = jax.random.split(jax.random.fold_in(keys[9], part), 10)
    mode_panel = normal_values(part_splits[0], (3, ATOMS, PANEL), 1.0, 6.0, ((1, 4), (2, 4)))
    partners = normal_values(part_splits[1], (3, ATOMS, PARTNERS), 1.0, 6.0, ((1, 4), (2, 4)))
    bond_blocks = normal_values(part_splits[2], (9, ATOMS, BONDS), 0.25, 1.5, ((1, 4),), jnp.float32)
    neighbors = draw_neighbors(jax.random.fold_in(jax.random.fold_in(keys[9], part), 71), part)
    bond_count = touch_ends(jax.random.randint(part_splits[4], (ATOMS,), BONDS // 4, BONDS + 1), jax.random.fold_in(part_splits[4], 1), BONDS // 4, BONDS).astype(jnp.int32)
    panel_freq = jnp.clip(jnp.exp(jax.random.uniform(part_splits[5], (PANEL,), jnp.float32, math.log(1.0), math.log(2.0))), 1.0, 2.0)
    partner_freq = jnp.clip(jnp.exp(math.log(2.0) - 0.6931472 * jax.random.uniform(part_splits[6], (PARTNERS,), jnp.float32) ** block_levels(part_splits[6], (PARTNERS,), ((0, 4),), -0.2, 0.2)), 1.0, 2.0)
    win_start = draw_win_start(jax.random.fold_in(jax.random.fold_in(keys[9], part), 71), part)
    win_len = draw_win_len(jax.random.fold_in(jax.random.fold_in(keys[9], part), 71), part)
    return dict(mode_panel=mode_panel, partners=partners, bond_blocks=bond_blocks, neighbors=neighbors, bond_count=bond_count, panel_freq=panel_freq, partner_freq=partner_freq, win_start=win_start, win_len=win_len)


lorentz_width = 0.05

def reference(mode_panel, partners, bond_blocks, neighbors, bond_count, panel_freq, partner_freq, win_start, win_len):
    slot_ids = jnp.arange(BONDS, dtype=jnp.int32)
    live_slot = (slot_ids[None, :] < bond_count[:, None]).astype(jnp.float32)
    coefficient = bond_blocks * live_slot[None]

    def slot_step(slot_index, summed):
        target = lax.dynamic_index_in_dim(neighbors, slot_index, 1, keepdims=False)
        gathered = jnp.take(mode_panel, target, axis=1)
        coef_slot = lax.dynamic_index_in_dim(coefficient, slot_index, 2, keepdims=False).reshape(3, 3, ATOMS)
        for d in range(3):
            summed = summed + coef_slot[:, d, :, None] * gathered[d][None]
        return summed
    summed = lax.fori_loop(0, BONDS, slot_step, jnp.zeros((3, ATOMS, PANEL), jnp.float32))
    images = summed.astype(jnp.bfloat16)
    products = jnp.dot(images.reshape(3 * ATOMS, PANEL).T, partners.reshape(3 * ATOMS, PARTNERS), preferred_element_type=jnp.float32)
    columns = jnp.arange(PARTNERS, dtype=jnp.int32)
    inside = (columns[None, :] >= win_start[:, None]) & (columns[None, :] < win_start[:, None] + win_len[:, None])
    norm_scale = 1.0 / math.sqrt(3 * ATOMS)
    elements = jnp.where(inside, products * norm_scale, 0.0)
    offset_freq = panel_freq[:, None] - partner_freq[None, :]
    lorentz = lorentz_width / (math.pi * (offset_freq * offset_freq + lorentz_width * lorentz_width))
    weight = jnp.where(inside, lorentz, 0.0)
    numerator = lax.optimization_barrier(jnp.sum(weight * elements * elements, axis=1))
    diffusivity = math.pi / 3.0 * numerator / (panel_freq * panel_freq)
    return (elements, diffusivity)
```

```python
import math

import jax
import jax.numpy as jnp
from jax import lax
from jax.experimental import pallas as pl
from jax.experimental.pallas import tpu as pltpu
from jax.sharding import PartitionSpec as P

HALO = 96
BONDS = 16
LANES = 128
SPAN = LANES + 2 * HALO
GROUP = 32
VMEM_BYTES = 40 * 1024 * 1024

lorentz_width = 0.05


def build_block(first, base, nbr_ref, coef_ref, count_ref, slot_ref, entry_ref, dense_ref):
    lanes = pl.ds(first, LANES)
    target = nbr_ref[:, lanes] - (base + (first - HALO))
    slot_ids = lax.broadcasted_iota(jnp.int32, (BONDS, LANES), 0)
    live = slot_ids < count_ref[:, lanes]
    coefs = [jnp.where(live, coef_ref[e, :, lanes], 0.0) for e in range(9)]
    merged = [jnp.zeros((BONDS, LANES), jnp.float32) for _ in range(9)]
    for k in range(BONDS):
        same = (target == target[k : k + 1]) & (slot_ids >= k)
        for e in range(9):
            merged[e] = merged[e] + jnp.where(same, coefs[e][k : k + 1], 0.0)
    for k in range(BONDS):
        slot_ref[k] = jnp.broadcast_to(target[k : k + 1], (8, LANES))
        for e in range(9):
            entry_ref[e * BONDS + k] = jnp.broadcast_to(merged[e][k : k + 1], (8, LANES))
    tiles = GROUP // 8
    rows = lax.broadcasted_iota(jnp.int32, (tiles, 8, LANES), 0) * 8 + lax.broadcasted_iota(
        jnp.int32, (tiles, 8, LANES), 1
    )

    def group_step(g, carry):
        here = rows + g * GROUP
        cells = [jnp.zeros((tiles, 8, LANES), jnp.float32) for _ in range(9)]
        for k in range(BONDS):
            hit = slot_ref[k][None] == here
            for e in range(9):
                cells[e] = jnp.where(hit, entry_ref[e * BONDS + k][None], cells[e])
        for r in range(3):
            for c in range(3):
                value = cells[3 * r + c].reshape(GROUP, LANES)
                high = value.astype(jnp.bfloat16)
                low = (value - high.astype(jnp.float32)).astype(jnp.bfloat16)
                at = pl.ds(pl.multiple_of(c * SPAN + g * GROUP, GROUP), GROUP)
                dense_ref[at, 2 * r * LANES : (2 * r + 1) * LANES] = high
                dense_ref[at, (2 * r + 1) * LANES : (2 * r + 2) * LANES] = low
        return carry

    lax.fori_loop(0, SPAN // GROUP, group_step, 0)


def window(first, rows, c, panel_ref, low_ref, high_ref):
    begin, end = first - HALO, first - HALO + SPAN
    if begin < 0:
        return jnp.concatenate([low_ref[c, HALO + begin :], panel_ref[c, :end]], axis=0)
    if end > rows:
        return jnp.concatenate([panel_ref[c, begin:], high_ref[c, : end - rows]], axis=0)
    return panel_ref[c, begin:end]


def image_kernel(blocks, rows, has_halo, *refs):
    if has_halo:
        base_ref, panel_ref, low_ref, high_ref, nbr_ref, coef_ref, count_ref = refs[:7]
    else:
        base_ref, panel_ref, nbr_ref, coef_ref, count_ref = refs[:5]
        low_ref = high_ref = None
    out_ref, slot_ref, entry_ref, dense_ref = refs[-4:]
    width = len(blocks) * LANES
    for place, block in enumerate(blocks):
        first = block * LANES
        build_block(first, base_ref[0], nbr_ref, coef_ref, count_ref, slot_ref, entry_ref, dense_ref)
        cells = jnp.concatenate(
            [window(first, rows, c, panel_ref, low_ref, high_ref) for c in range(3)], axis=0
        )
        both = lax.dot_general(
            cells, dense_ref[...], (((0,), (0,)), ((), ())), preferred_element_type=jnp.float32
        )
        for r in range(3):
            image = both[:, 2 * r * LANES : (2 * r + 1) * LANES] + both[:, (2 * r + 1) * LANES : (2 * r + 2) * LANES]
            at = r * width + place * LANES
            out_ref[:, at : at + LANES] = image.astype(jnp.bfloat16)


def images_of(blocks, base, panel, halos, nbr, coef, count):
    rows, cols = panel.shape[1:]
    vmem = pl.BlockSpec(memory_space=pltpu.VMEM)
    operands = [base, panel, *halos, nbr, coef, count]

    def kernel(*refs):
        image_kernel(blocks, rows, len(halos) > 0, *refs)

    return pl.pallas_call(
        kernel,
        in_specs=[pl.BlockSpec(memory_space=pltpu.SMEM)] + [vmem] * (len(operands) - 1),
        out_specs=vmem,
        out_shape=jax.ShapeDtypeStruct((cols, 3 * LANES * len(blocks)), jnp.bfloat16),
        scratch_shapes=[
            pltpu.VMEM((BONDS, 8, LANES), jnp.int32),
            pltpu.VMEM((9 * BONDS, 8, LANES), jnp.float32),
            pltpu.VMEM((3 * SPAN, 6 * LANES), jnp.bfloat16),
        ],
        compiler_params=pltpu.CompilerParams(vmem_limit_bytes=VMEM_BYTES),
        name="images",
    )(*operands)


def runs_of(blocks):
    runs = []
    for place, block in enumerate(blocks):
        if runs and runs[-1][1] + runs[-1][2] == block:
            runs[-1][2] += 1
        else:
            runs.append([place, block, 1])
    return runs


def product_kernel(chunks, half_ref, partners_ref, *refs):
    out_ref = refs[-1]
    count = len(chunks)
    for who in range(2):
        total = None
        for blocks, image_ref in zip(chunks, refs[who * count : (who + 1) * count]):
            width = len(blocks) * LANES
            for r in range(3):
                for place, block, length in runs_of(blocks):
                    at = r * width + place * LANES
                    part = jnp.dot(
                        image_ref[:, at : at + length * LANES],
                        partners_ref[r, block * LANES : (block + length) * LANES, :],
                        preferred_element_type=jnp.float32,
                    )
                    total = part if total is None else total + part
        half = half_ref[0] if who == 0 else 1 - half_ref[0]
        out_ref[half] = total


def products_of(chunks, half, partners, mine, theirs):
    vmem = pl.BlockSpec(memory_space=pltpu.VMEM)
    modes, cols = mine[0].shape[0], partners.shape[2]

    def kernel(*refs):
        product_kernel(chunks, *refs)

    return pl.pallas_call(
        kernel,
        in_specs=[pl.BlockSpec(memory_space=pltpu.SMEM)] + [vmem] * (1 + 2 * len(chunks)),
        out_specs=vmem,
        out_shape=jax.ShapeDtypeStruct((2, modes, cols), jnp.float32),
        compiler_params=pltpu.CompilerParams(vmem_limit_bytes=VMEM_BYTES),
        name="products",
    )(half, partners, *mine, *theirs)


def reduced(group, shift, rows_dev):
    groups, depth = lax.axis_size("modes"), lax.axis_size("atoms")
    place = lax.axis_index("atoms")
    cells = group.reshape(-1, rows_dev, group.shape[-1])
    bit = 0
    while cells.shape[0] > 1:
        pairs = cells.reshape(cells.shape[0] // 2, 2, rows_dev, -1)
        own = (place >> bit) & 1
        keep = lax.dynamic_index_in_dim(pairs, own, 1, keepdims=False)
        send = lax.dynamic_index_in_dim(pairs, 1 - own, 1, keepdims=False)
        step = 1 << bit
        got = lax.ppermute(send.astype(jnp.bfloat16), "atoms", [(z, z ^ step) for z in range(depth)])
        cells = keep + got.astype(jnp.float32)
        bit += 1
    cells = cells[0]
    low, level = bit, 0
    while (1 << level) < groups:
        moves = []
        for z in range(depth):
            for m in range(groups):
                goal = (m + shift) % groups
                settled = all(((z >> (low + u)) ^ (goal >> u)) & 1 == 0 for u in range(level))
                if settled and ((z >> (low + level)) ^ (goal >> level)) & 1:
                    moves.append((z * groups + m, (z ^ (1 << (low + level))) * groups + m))
        got = lax.ppermute(cells.astype(jnp.bfloat16), ("atoms", "modes"), moves)
        cells = cells + got.astype(jnp.float32)
        level += 1
    return cells


def body(
    mode_panel,
    partners,
    bond_blocks,
    neighbors,
    bond_count,
    panel_freq,
    partner_freq,
    win_start,
    win_len,
):
    atom_rows = mode_panel.shape[1]
    atom_index = lax.axis_index("atoms")
    atom_count = lax.axis_size("atoms")
    groups = lax.axis_size("modes")
    group_index = lax.axis_index("modes")
    half_index = lax.axis_index("sub")
    column_index = lax.axis_index(("modes", "sub"))
    part_cols = partners.shape[2]
    panel_total = win_start.shape[0]
    rows_dev = panel_total // atom_count

    up = [(z, z + 1) for z in range(atom_count - 1)]
    down = [(z + 1, z) for z in range(atom_count - 1)]
    low_halo = lax.ppermute(mode_panel[:, atom_rows - HALO :], "atoms", up)
    high_halo = lax.ppermute(mode_panel[:, :HALO], "atoms", down)

    nbr = neighbors.T
    coef = bond_blocks.transpose(0, 2, 1)
    count = bond_count[None, :]
    base = (atom_index * atom_rows).astype(jnp.int32)[None]
    half = half_index.astype(jnp.int32)[None]

    last = atom_rows // LANES - 1
    middle = list(range(1, last))
    cut = (last + 1) // 2
    chunks = [middle[:cut], middle[cut:] + [last, 0]]
    own = []
    for blocks in chunks:
        edge = 0 in blocks or last in blocks
        own.append(images_of(blocks, base, mode_panel, (low_halo, high_halo) if edge else (), nbr, coef, count))

    swap = [(0, 1), (1, 0)]
    far, sibling, far_sibling = {}, [], {}
    for chunk in own:
        for shift in range(1, groups):
            moves = [((m + shift) % groups, m) for m in range(groups)]
            got = lax.ppermute(chunk, "modes", moves)
            far.setdefault(shift, []).append(got)
        sibling.append(lax.ppermute(chunk, "sub", swap))
    for shift in range(1, groups):
        far_sibling[shift] = [lax.ppermute(got, "sub", swap) for got in far[shift]]

    goal = atom_index * groups // atom_count
    products = None
    for shift in range(groups):
        mine = own if shift == 0 else far[shift]
        theirs = sibling if shift == 0 else far_sibling[shift]
        total = reduced(products_of(chunks, half, partners, mine, theirs), shift, rows_dev)
        if products is None:
            products = total
        else:
            products = jnp.where((group_index + shift) % groups == goal, total, products)

    first_col = column_index * part_cols
    norm_scale = 1.0 / math.sqrt(3 * atom_rows * atom_count)
    my_start = lax.dynamic_slice_in_dim(win_start, atom_index * rows_dev, rows_dev, 0)
    my_length = lax.dynamic_slice_in_dim(win_len, atom_index * rows_dev, rows_dev, 0)
    my_freq = lax.dynamic_slice_in_dim(panel_freq, atom_index * rows_dev, rows_dev, 0)
    columns = first_col + jnp.arange(part_cols, dtype=jnp.int32)
    inside = (columns[None, :] >= my_start[:, None]) & (
        columns[None, :] < my_start[:, None] + my_length[:, None]
    )
    elements = jnp.where(inside, products * norm_scale, 0.0)
    offset_freq = my_freq[:, None] - partner_freq[None, :]
    lorentz = lorentz_width / (
        math.pi * (offset_freq * offset_freq + lorentz_width * lorentz_width)
    )
    weight = jnp.where(inside, lorentz, 0.0)
    numerator = lax.psum(jnp.sum(weight * elements * elements, axis=1), ("modes", "sub"))
    diffusivity = math.pi / 3.0 * numerator / (my_freq * my_freq)
    return (elements, diffusivity)


def solution(mesh):
    return jax.shard_map(
        body,
        mesh=mesh,
        in_specs=(
            P(None, ("dom", "atoms"), ("modes", "sub")),
            P(None, ("dom", "atoms"), ("modes", "sub")),
            P(None, ("dom", "atoms"), None),
            P(("dom", "atoms"), None),
            P(("dom", "atoms")),
            P("dom"),
            P(("dom", "modes", "sub")),
            P("dom"),
            P("dom"),
        ),
        out_specs=(P(("dom", "atoms"), ("modes", "sub")), P(("dom", "atoms"))),
        check_vma=False,
    )
```

```python
import math

import jax
import jax.numpy as jnp
from jax import lax
from jax.experimental import pallas as pl
from jax.experimental.pallas import tpu as pltpu
from jax.sharding import PartitionSpec as P

HALO = 96
BONDS = 16
LANES = 128
SPAN = LANES + 2 * HALO
GROUP = 16
VMEM_BYTES = 40 * 1024 * 1024

lorentz_width = 0.05

HBM = pl.BlockSpec(memory_space=pl.ANY)
VMEM = pl.BlockSpec(memory_space=pltpu.VMEM)
SMEM = pl.BlockSpec(memory_space=pltpu.SMEM)


def call(kernel, name, in_specs, out_specs, out_shape, operands, busy_us, scratch=()):
    return pl.pallas_call(
        kernel,
        in_specs=in_specs,
        out_specs=out_specs,
        out_shape=out_shape,
        scratch_shapes=list(scratch),
        compiler_params=pltpu.CompilerParams(vmem_limit_bytes=VMEM_BYTES),
        cost_estimate=pl.CostEstimate(
            flops=int(busy_us * 1.1e9), bytes_accessed=int(busy_us * 1e5), transcendentals=0
        ),
        name=name,
    )(*operands)


def runs_of(blocks):
    runs = []
    for place, block in enumerate(blocks):
        if runs and runs[-1][1] + runs[-1][2] == block:
            runs[-1][2] += 1
        else:
            runs.append([place, block, 1])
    return runs


def build_block(first, base, nbr_ref, coef_ref, count_ref, dense_ref):
    lanes = pl.ds(first, LANES)
    target = nbr_ref[:, lanes] - (base + (first - HALO))
    slot_ids = lax.broadcasted_iota(jnp.int32, (BONDS, LANES), 0)
    live = slot_ids < count_ref[lanes].reshape(1, LANES)
    coefs = [jnp.where(live, coef_ref[e, :, lanes], 0.0) for e in range(9)]
    halves = [(target[h : h + 8], slot_ids[h : h + 8]) for h in (0, 8)]
    merged = [[jnp.zeros((8, LANES), jnp.float32) for _ in range(9)] for _ in range(2)]
    named = [jnp.broadcast_to(target[k : k + 1], (8, LANES)) for k in range(BONDS)]
    for k in range(BONDS):
        rows = [jnp.broadcast_to(coefs[e][k : k + 1], (8, LANES)) for e in range(9)]
        for h in range(k // 8, 2):
            same = (halves[h][0] == named[k]) & (halves[h][1] >= k)
            for e in range(9):
                merged[h][e] = merged[h][e] + jnp.where(same, rows[e], 0.0)
    row_ids = lax.broadcasted_iota(jnp.int32, (8, LANES), 0)

    def group_step(g, carry):
        cells = [[] for _ in range(9)]
        for tile in range(GROUP // 8):
            here = row_ids + (g * GROUP + tile * 8)
            slot = jnp.full((8, LANES), -1, jnp.int32)
            for k in range(BONDS):
                slot = jnp.where(named[k] == here, k, slot)
            place = slot & 7
            early, live_cell = slot < 8, slot >= 0
            for e in range(9):
                picks = [
                    jnp.take_along_axis(merged[h][e], place, axis=0, mode="promise_in_bounds")
                    for h in range(2)
                ]
                cells[e].append(jnp.where(live_cell, jnp.where(early, picks[0], picks[1]), 0.0))
        for r in range(3):
            for c in range(3):
                value = jnp.concatenate(cells[3 * r + c], axis=0)
                high = value.astype(jnp.bfloat16)
                low = (value - high.astype(jnp.float32)).astype(jnp.bfloat16)
                at = pl.ds(pl.multiple_of(c * SPAN + g * GROUP, GROUP), GROUP)
                dense_ref[at, 2 * r * LANES : (2 * r + 1) * LANES] = high
                dense_ref[at, (2 * r + 1) * LANES : (2 * r + 2) * LANES] = low
        return carry

    lax.fori_loop(0, SPAN // GROUP, group_step, 0)


def window(first, rows, c, panel_ref, low_ref, high_ref):
    begin, end = first - HALO, first - HALO + SPAN
    if begin < 0:
        return jnp.concatenate([low_ref[c, HALO + begin :], panel_ref[c, :end]], axis=0)
    if end > rows:
        return jnp.concatenate([panel_ref[c, begin:], high_ref[c, : end - rows]], axis=0)
    return panel_ref[c, begin:end]


def images_of(blocks, base, panel, nbr, coef, count, halos=(), before=None, edges=False, parts=0):
    rows, modes = panel.shape[1:]
    before_blocks = before.shape[1] // (3 * LANES) if parts else 0
    width = (len(blocks) + before_blocks) * LANES
    operands = [base, nbr, count, coef, panel, *halos]
    in_specs = [SMEM] + [HBM] * (len(operands) - 1)
    if before is not None:
        operands.append(before)
        in_specs.append(VMEM if parts else HBM)
    out_shape = [jax.ShapeDtypeStruct((modes, 3 * width), jnp.bfloat16)]
    out_specs = [VMEM]
    if edges:
        out_shape += [jax.ShapeDtypeStruct((3, HALO, modes), jnp.bfloat16)] * 2
        out_specs += [HBM] * 2
    out_shape += [jax.ShapeDtypeStruct((modes // parts, 3 * width), jnp.bfloat16)] * parts if parts > 1 else []
    out_specs += [VMEM] * parts if parts > 1 else []
    n_in, n_out = len(operands), len(out_shape)

    def kernel(*refs):
        base_ref, nbr_hbm, count_hbm, coef_hbm, panel_hbm = refs[:5]
        outs = refs[n_in : n_in + n_out]
        nbr_ref, count_ref, coef_ref, panel_ref, low_ref, high_ref, dense_ref, sems = refs[n_in + n_out :]
        copies, panel_copies = [], []

        def start(source, target, kept):
            copy = pltpu.make_async_copy(source, target, sems.at[len(copies) + len(panel_copies)])
            copy.start()
            kept.append(copy)

        start(nbr_hbm, nbr_ref, copies)
        start(count_hbm, count_ref, copies)
        for _, block, length in runs_of(blocks):
            at = pl.ds(block * LANES, length * LANES)
            start(coef_hbm.at[:, :, at], coef_ref.at[:, :, at], copies)
        for _, block, length in runs_of(blocks):
            begin = max(block * LANES - HALO, 0)
            end = min((block + length) * LANES + HALO, rows)
            at = pl.ds(begin, end - begin)
            start(panel_hbm.at[:, at], panel_ref.at[:, at], panel_copies)
        if halos:
            start(refs[5], low_ref, panel_copies)
            start(refs[6], high_ref, panel_copies)
        if edges:
            start(panel_hbm.at[:, pl.ds(0, HALO)], outs[1], panel_copies)
            start(panel_hbm.at[:, pl.ds(rows - HALO, HALO)], outs[2], panel_copies)
        for copy in copies:
            copy.wait()
        for place, block in enumerate(blocks):
            first = block * LANES
            build_block(first, base_ref[0], nbr_ref, coef_ref, count_ref, dense_ref)
            if place == 0:
                for copy in panel_copies:
                    copy.wait()
            cells = jnp.concatenate(
                [window(first, rows, c, panel_ref, low_ref, high_ref) for c in range(3)], axis=0
            )
            both = lax.dot_general(
                cells, dense_ref[...], (((0,), (0,)), ((), ())), preferred_element_type=jnp.float32
            )
            for r in range(3):
                image = both[:, 2 * r * LANES : (2 * r + 1) * LANES]
                image = image + both[:, (2 * r + 1) * LANES : (2 * r + 2) * LANES]
                at = r * width + (before_blocks + place) * LANES
                outs[0][:, at : at + LANES] = image.astype(jnp.bfloat16)
        if parts:
            old = before_blocks * LANES
            for r in range(3):
                outs[0][:, r * width : r * width + old] = refs[n_in - 1][:, r * old : (r + 1) * old]
            for part, out in enumerate(outs[-parts:] if parts > 1 else []):
                span = modes // parts
                out[...] = outs[0][part * span : (part + 1) * span, :]

    copies_most = 2 + 2 * len(runs_of(blocks)) + 4
    scratch = [
        pltpu.VMEM((BONDS, rows), jnp.int32),
        pltpu.VMEM((rows,), jnp.int32),
        pltpu.VMEM((9, BONDS, rows), jnp.float32),
        pltpu.VMEM((3, rows, modes), jnp.bfloat16),
        pltpu.VMEM((3, HALO, modes), jnp.bfloat16),
        pltpu.VMEM((3, HALO, modes), jnp.bfloat16),
        pltpu.VMEM((3 * SPAN, 6 * LANES), jnp.bfloat16),
        pltpu.SemaphoreType.DMA((copies_most,)),
    ]
    return call(kernel, "images", in_specs, out_specs, out_shape, operands, 1.0 + len(blocks), scratch)


def products_of(chunks, place, partners, mine, theirs, rows_from, rows):
    cols = partners.shape[2]
    count = len(chunks)

    def kernel(place_ref, partners_ref, *refs):
        keep_ref, send_ref = refs[-2:]

        def half(who):
            total = None
            for i, blocks in enumerate(chunks):
                image_ref = refs[who * count + i]
                at_rows = slice(rows_from[i], rows_from[i] + rows)
                width = len(blocks) * LANES
                for r in range(3):
                    for spot, block, length in runs_of(blocks):
                        at = r * width + spot * LANES
                        part = jnp.dot(
                            image_ref[at_rows, at : at + length * LANES],
                            partners_ref[r, block * LANES : (block + length) * LANES, :],
                            preferred_element_type=jnp.float32,
                        )
                        total = part if total is None else total + part
            return total

        first, second = half(0), half(1)
        kept = place_ref[0] == place_ref[1]
        keep_ref[...] = jnp.where(kept, first, second)
        send_ref[...] = jnp.where(kept, second, first).astype(jnp.bfloat16)

    return call(
        kernel,
        "products",
        [SMEM] + [VMEM] * (1 + 2 * count),
        [VMEM, VMEM],
        [jax.ShapeDtypeStruct((rows, cols), jnp.float32), jax.ShapeDtypeStruct((rows, cols), jnp.bfloat16)],
        (place, partners, *mine, *theirs),
        2.5,
    )


def all_products(chunks, half, partners, mine, theirs):
    modes, cols = mine[0].shape[0], partners.shape[2]
    place = jnp.stack([half, jnp.zeros((), jnp.int32)])
    low = products_of(chunks, place, partners, mine, theirs, [0] * len(chunks), modes)[0]
    high = products_of(chunks, place + jnp.array([0, 1], jnp.int32), partners, mine, theirs, [0] * len(chunks), modes)[0]
    return jnp.stack([low, high])


def settle(cells, bit, rows_dev):
    depth = lax.axis_size("atoms")
    place = lax.axis_index("atoms")
    while cells.shape[0] > 1:
        pairs = cells.reshape(cells.shape[0] // 2, 2, rows_dev, -1)
        own = (place >> bit) & 1
        keep = lax.dynamic_index_in_dim(pairs, own, 1, keepdims=False)
        send = lax.dynamic_index_in_dim(pairs, 1 - own, 1, keepdims=False)
        step = 1 << bit
        got = lax.ppermute(send.astype(jnp.bfloat16), "atoms", [(z, z ^ step) for z in range(depth)])
        cells = keep + got.astype(jnp.float32)
        bit += 1
    return cells[0], bit


def collected(terms, bit, shift):
    groups, depth = lax.axis_size("modes"), lax.axis_size("atoms")
    level = 0
    while (1 << level) < groups:
        moves = []
        for z in range(depth):
            for m in range(groups):
                goal = m ^ shift
                settled = all(((z >> (bit + u)) ^ (goal >> u)) & 1 == 0 for u in range(level))
                if settled and ((z >> (bit + level)) ^ (goal >> level)) & 1:
                    moves.append((z * groups + m, (z ^ (1 << (bit + level))) * groups + m))
        sent = sum(term.astype(jnp.float32) for term in terms).astype(jnp.bfloat16)
        terms = terms + [lax.ppermute(sent, ("atoms", "modes"), moves)]
        level += 1
    return terms


def finish(flag, early, late, my_start, my_length, my_freq, partner_freq, first_col, norm_scale):
    rows, cols = early[0].shape
    n_early, parts, n_late = len(early), len(late), len(late[0])
    operands = [flag, my_start, my_length, my_freq, partner_freq, *early, *[t for part in late for t in part]]

    def kernel(flag_ref, start_ref, length_ref, freq_ref, partner_ref, *refs):
        out_ref, sum_ref = refs[-2:]
        span = rows // parts

        def sums(some):
            total = some[0][...]
            for ref in some[1:]:
                total = total + ref[...].astype(jnp.float32)
            return total

        @pl.when(flag_ref[0] == 1)
        def _():
            out_ref[...] = sums(refs[:n_early])

        @pl.when(flag_ref[0] == 0)
        def _():
            for part in range(parts):
                at = n_early + part * n_late
                out_ref[part * span : (part + 1) * span, :] = sums(refs[at : at + n_late])

        columns = lax.broadcasted_iota(jnp.int32, (rows, cols), 1) + flag_ref[1]
        start = start_ref[...]
        inside = (columns >= start) & (columns < start + length_ref[...])
        elements = jnp.where(inside, out_ref[...] * norm_scale, 0.0)
        out_ref[...] = elements
        offset = freq_ref[...] - partner_ref[...]
        lorentz = lorentz_width / (math.pi * (offset * offset + lorentz_width * lorentz_width))
        weighted = jnp.where(inside, lorentz, 0.0) * elements * elements
        folded = weighted[:, :LANES]
        for at in range(LANES, cols, LANES):
            folded = folded + weighted[:, at : at + LANES]
        if rows < LANES:
            folded = jnp.concatenate([folded, jnp.zeros((LANES - rows, LANES), jnp.float32)], axis=0)
        sum_ref[...] = jnp.sum(folded.T, axis=0, keepdims=True)

    return call(
        kernel,
        "finish",
        [SMEM] + [VMEM] * (len(operands) - 1),
        [VMEM, VMEM],
        [jax.ShapeDtypeStruct((rows, cols), jnp.float32), jax.ShapeDtypeStruct((1, LANES), jnp.float32)],
        operands,
        2.0,
    )


def body(
    mode_panel,
    partners,
    bond_blocks,
    neighbors,
    bond_count,
    panel_freq,
    partner_freq,
    win_start,
    win_len,
):
    atom_rows, modes = mode_panel.shape[1:]
    atom_index = lax.axis_index("atoms")
    atom_count = lax.axis_size("atoms")
    groups = lax.axis_size("modes")
    group_index = lax.axis_index("modes")
    half_index = lax.axis_index("sub")
    column_index = lax.axis_index(("modes", "sub"))
    part_cols = partners.shape[2]
    panel_total = win_start.shape[0]
    rows_dev = panel_total // atom_count
    whole_halves = rows_dev == modes

    nbr = neighbors.T
    coef = bond_blocks.transpose(0, 2, 1)
    base = (atom_index * atom_rows).astype(jnp.int32)[None]

    last = atom_rows // LANES - 1
    middle = list(range(1, last))
    cut = len(middle) // 2
    shared = (base, mode_panel, nbr, coef, bond_count)
    first_images, head, tail = images_of(middle[:cut], *shared, edges=True)
    low_halo = lax.ppermute(tail, "atoms", [(z, z + 1) for z in range(atom_count - 1)])
    high_halo = lax.ppermute(head, "atoms", [(z + 1, z) for z in range(atom_count - 1)])
    (middle_images,) = images_of(middle[cut:], *shared, before=first_images)
    parts = 2 if whole_halves else 1
    rest, *pieces = images_of(
        [last, 0], *shared, halos=(low_halo, high_halo), before=middle_images, parts=parts
    )
    pieces = pieces or [rest]
    chunks = [middle[:cut], middle[cut:] + [last, 0]]

    swap = [(0, 1), (1, 0)]

    def from_group(cells, shift):
        return lax.ppermute(cells, "modes", [(m ^ shift, m) for m in range(groups)])

    def from_sibling(cells):
        return lax.ppermute(cells, "sub", swap)

    mine = [first_images, rest]
    theirs = [from_sibling(first_images), from_sibling(rest)]
    half = half_index.astype(jnp.int32)
    place = jnp.stack([half, (atom_index & 1).astype(jnp.int32)])
    goal = atom_index * groups // atom_count

    if whole_halves:
        def level_zero(chunk_mine, chunk_theirs, rows_from, rows):
            keep, send = products_of(chunks, place, partners, chunk_mine, chunk_theirs, rows_from, rows)
            got = lax.ppermute(send, "atoms", [(z, z ^ 1) for z in range(atom_count)])
            return [keep, got]

        early = collected(level_zero(mine, theirs, [0, 0], modes), 1, 0)
    else:
        cells, bit = settle(all_products(chunks, half, partners, mine, theirs).reshape(-1, rows_dev, part_cols), 0, rows_dev)
        early = collected([cells], bit, 0)

    late = None
    for shift in range(1, groups):
        far = [from_group(cells, shift) for cells in [first_images] + pieces]
        far_sibling = [from_sibling(cells) for cells in far]
        terms = []
        for part in range(parts):
            pick = [far[0], far[1 + part]]
            pick_sibling = [far_sibling[0], far_sibling[1 + part]]
            if whole_halves:
                span = modes // parts
                found = collected(level_zero(pick, pick_sibling, [part * span, 0], span), 1, shift)
            else:
                cells, bit = settle(
                    all_products(chunks, half, partners, pick, pick_sibling).reshape(-1, rows_dev, part_cols), 0, rows_dev
                )
                found = collected([cells], bit, shift)
            terms.append(found)
        if late is None:
            late = terms
        else:
            here = (group_index ^ shift) == goal
            late = [[jnp.where(here, a, b) for a, b in zip(new, old)] for new, old in zip(terms, late)]

    def my_rows(values):
        return lax.dynamic_slice_in_dim(values, atom_index * rows_dev, rows_dev, 0)

    my_freq = my_rows(panel_freq)
    flag = jnp.stack([(group_index == goal).astype(jnp.int32), (column_index * part_cols).astype(jnp.int32)])
    elements, numerator = finish(
        flag,
        early,
        late,
        my_rows(win_start)[:, None],
        my_rows(win_len)[:, None],
        my_freq[:, None],
        partner_freq[None, :],
        column_index * part_cols,
        1.0 / math.sqrt(3 * atom_rows * atom_count),
    )
    holders = groups * 2
    sums = [numerator] + [
        lax.ppermute(numerator, ("modes", "sub"), [(i, i ^ code) for i in range(holders)])
        for code in range(1, holders)
    ]
    while len(sums) > 1:
        sums = [sums[i] + sums[i + 1] for i in range(0, len(sums), 2)]
    diffusivity = math.pi / 3.0 * sums[0][0, :rows_dev] / (my_freq * my_freq)
    return (elements, diffusivity)


def solution(mesh):
    return jax.shard_map(
        body,
        mesh=mesh,
        in_specs=(
            P(None, ("dom", "atoms"), ("modes", "sub")),
            P(None, ("dom", "atoms"), ("modes", "sub")),
            P(None, ("dom", "atoms"), None),
            P(("dom", "atoms"), None),
            P(("dom", "atoms")),
            P("dom"),
            P(("dom", "modes", "sub")),
            P("dom"),
            P("dom"),
        ),
        out_specs=(P(("dom", "atoms"), ("modes", "sub")), P(("dom", "atoms"))),
        check_vma=False,
    )
```

```python
import math

import jax
import jax.numpy as jnp
from jax import lax
from jax.experimental import pallas as pl
from jax.experimental.pallas import tpu as pltpu
from jax.sharding import PartitionSpec as P

HALO = 96
BONDS = 16
LANES = 128
SPAN = LANES + 2 * HALO
GROUP = 16
VMEM_BYTES = 40 * 1024 * 1024

lorentz_width = 0.05

HBM = pl.BlockSpec(memory_space=pltpu.HBM)
ANY = pl.BlockSpec(memory_space=pl.ANY)
VMEM = pl.BlockSpec(memory_space=pltpu.VMEM)
SMEM = pl.BlockSpec(memory_space=pltpu.SMEM)


def call(kernel, name, in_specs, out_specs, out_shape, operands, busy_us, scratch=()):
    return pl.pallas_call(
        kernel,
        in_specs=in_specs,
        out_specs=out_specs,
        out_shape=out_shape,
        scratch_shapes=list(scratch),
        compiler_params=pltpu.CompilerParams(vmem_limit_bytes=VMEM_BYTES),
        cost_estimate=pl.CostEstimate(
            flops=int(busy_us * 1.1e9), bytes_accessed=int(busy_us * 1e5), transcendentals=0
        ),
        name=name,
    )(*operands)


def runs_of(blocks):
    runs = []
    for place, block in enumerate(blocks):
        if runs and runs[-1][1] + runs[-1][2] == block:
            runs[-1][2] += 1
        else:
            runs.append([place, block, 1])
    return runs


def build_block(first, base, nbr_ref, coef_ref, count_ref, dense_ref):
    lanes = pl.ds(first, LANES)
    target = nbr_ref[:, lanes] - (base + (first - HALO))
    slot_ids = lax.broadcasted_iota(jnp.int32, (BONDS, LANES), 0)
    live = slot_ids < count_ref[lanes].reshape(1, LANES)
    coefs = [jnp.where(live, coef_ref[e, :, lanes], 0.0) for e in range(9)]
    halves = [(target[h : h + 8], slot_ids[h : h + 8]) for h in (0, 8)]
    merged = [[jnp.zeros((8, LANES), jnp.float32) for _ in range(9)] for _ in range(2)]
    named = [jnp.broadcast_to(target[k : k + 1], (8, LANES)) for k in range(BONDS)]
    for k in range(BONDS):
        rows = [jnp.broadcast_to(coefs[e][k : k + 1], (8, LANES)) for e in range(9)]
        for h in range(k // 8, 2):
            same = (halves[h][0] == named[k]) & (halves[h][1] >= k)
            for e in range(9):
                merged[h][e] = merged[h][e] + jnp.where(same, rows[e], 0.0)
    row_ids = lax.broadcasted_iota(jnp.int32, (8, LANES), 0)

    def group_step(g, carry):
        cells = [[] for _ in range(9)]
        for tile in range(GROUP // 8):
            here = row_ids + (g * GROUP + tile * 8)
            slot = jnp.full((8, LANES), -1, jnp.int32)
            for k in range(BONDS):
                slot = jnp.where(named[k] == here, k, slot)
            place = slot & 7
            early, live_cell = slot < 8, slot >= 0
            for e in range(9):
                picks = [
                    jnp.take_along_axis(merged[h][e], place, axis=0, mode="promise_in_bounds")
                    for h in range(2)
                ]
                cells[e].append(jnp.where(live_cell, jnp.where(early, picks[0], picks[1]), 0.0))
        for r in range(3):
            for c in range(3):
                value = jnp.concatenate(cells[3 * r + c], axis=0)
                high = value.astype(jnp.bfloat16)
                low = (value - high.astype(jnp.float32)).astype(jnp.bfloat16)
                at = pl.ds(pl.multiple_of(c * SPAN + g * GROUP, GROUP), GROUP)
                dense_ref[at, 2 * r * LANES : (2 * r + 1) * LANES] = high
                dense_ref[at, (2 * r + 1) * LANES : (2 * r + 2) * LANES] = low
        return carry

    lax.fori_loop(0, SPAN // GROUP, group_step, 0)


def window(first, rows, c, panel_ref, low_ref, high_ref):
    begin, end = first - HALO, first - HALO + SPAN
    if begin < 0:
        return jnp.concatenate([low_ref[c, HALO + begin :], panel_ref[c, :end]], axis=0)
    if end > rows:
        return jnp.concatenate([panel_ref[c, begin:], high_ref[c, : end - rows]], axis=0)
    return panel_ref[c, begin:end]


def images_of(blocks, base, panel, nbr, coef, count, halos=(), before=None, edges=False, halved=False):
    rows, modes = panel.shape[1:]
    width = len(blocks) * LANES
    operands = [base, *[pltpu.with_memory_space_constraint(x, pltpu.HBM) for x in (nbr, count, coef, panel)], *halos]
    in_specs = [SMEM] + [HBM] * 4 + [ANY] * len(halos)
    old = 0
    if before is not None:
        operands.append(before)
        in_specs.append(VMEM)
        old = before.shape[1] // 3
    out_shape = [jax.ShapeDtypeStruct((modes, 3 * width), jnp.bfloat16)]
    out_specs = [VMEM]
    if edges:
        out_shape += [jax.ShapeDtypeStruct((3, HALO, modes), jnp.bfloat16)] * 2
        out_specs += [ANY] * 2
    if halved:
        out_shape.append(jax.ShapeDtypeStruct((modes // 2, 3 * width), jnp.bfloat16))
        out_specs.append(VMEM)
        if before is not None:
            out_shape.append(jax.ShapeDtypeStruct((modes // 2, 3 * (old + width)), jnp.bfloat16))
            out_specs.append(VMEM)
    n_in, n_out = len(operands), len(out_shape)

    def kernel(*refs):
        base_ref, nbr_hbm, count_hbm, coef_hbm, panel_hbm = refs[:5]
        outs = refs[n_in : n_in + n_out]
        nbr_ref, count_ref, coef_ref, panel_ref, low_ref, high_ref, dense_ref, sems = refs[n_in + n_out :]
        copies, panel_copies = [], []

        def start(source, target, kept):
            copy = pltpu.make_async_copy(source, target, sems.at[len(copies) + len(panel_copies)])
            copy.start()
            kept.append(copy)

        start(nbr_hbm, nbr_ref, copies)
        start(count_hbm, count_ref, copies)
        for _, block, length in runs_of(blocks):
            at = pl.ds(block * LANES, length * LANES)
            start(coef_hbm.at[:, :, at], coef_ref.at[:, :, at], copies)
        for _, block, length in runs_of(blocks):
            begin = max(block * LANES - HALO, 0)
            end = min((block + length) * LANES + HALO, rows)
            at = pl.ds(begin, end - begin)
            start(panel_hbm.at[:, at], panel_ref.at[:, at], panel_copies)
        if halos:
            start(refs[5], low_ref, panel_copies)
            start(refs[6], high_ref, panel_copies)
        if edges:
            start(panel_hbm.at[:, pl.ds(0, HALO)], outs[1], panel_copies)
            start(panel_hbm.at[:, pl.ds(rows - HALO, HALO)], outs[2], panel_copies)
        for copy in copies:
            copy.wait()
        for place, block in enumerate(blocks):
            first = block * LANES
            build_block(first, base_ref[0], nbr_ref, coef_ref, count_ref, dense_ref)
            if place == 0:
                for copy in panel_copies:
                    copy.wait()
            cells = jnp.concatenate(
                [window(first, rows, c, panel_ref, low_ref, high_ref) for c in range(3)], axis=0
            )
            both = lax.dot_general(
                cells, dense_ref[...], (((0,), (0,)), ((), ())), preferred_element_type=jnp.float32
            )
            for r in range(3):
                image = both[:, 2 * r * LANES : (2 * r + 1) * LANES]
                image = image + both[:, (2 * r + 1) * LANES : (2 * r + 2) * LANES]
                at = r * width + place * LANES
                outs[0][:, at : at + LANES] = image.astype(jnp.bfloat16)
        if halved:
            span = modes // 2
            half_ref = outs[-1] if before is None else outs[-2]
            half_ref[...] = outs[0][:span, :]
            if before is not None:
                for r in range(3):
                    at = r * (old + width)
                    outs[-1][:, at : at + old] = refs[n_in - 1][span:, r * old : (r + 1) * old]
                    outs[-1][:, at + old : at + old + width] = outs[0][span:, r * width : (r + 1) * width]

    copies_most = 2 + 2 * len(runs_of(blocks)) + 4
    scratch = [
        pltpu.VMEM((BONDS, rows), jnp.int32),
        pltpu.VMEM((rows,), jnp.int32),
        pltpu.VMEM((9, BONDS, rows), jnp.float32),
        pltpu.VMEM((3, rows, modes), jnp.bfloat16),
        pltpu.VMEM((3, HALO, modes), jnp.bfloat16),
        pltpu.VMEM((3, HALO, modes), jnp.bfloat16),
        pltpu.VMEM((3 * SPAN, 6 * LANES), jnp.bfloat16),
        pltpu.SemaphoreType.DMA((copies_most,)),
    ]
    return call(kernel, "images", in_specs, out_specs, out_shape, operands, 0.8 + 1.2 * len(blocks), scratch)


def products_of(chunks, place, partners, mine, theirs, rows_from, rows, after=()):
    cols = partners.shape[2]
    count = len(chunks)

    def kernel(place_ref, partners_ref, *refs):
        keep_ref, send_ref = refs[-2:]

        def half(who):
            total = None
            for i, blocks in enumerate(chunks):
                image_ref = refs[who * count + i]
                at_rows = slice(rows_from[i], rows_from[i] + rows)
                width = len(blocks) * LANES
                for r in range(3):
                    for spot, block, length in runs_of(blocks):
                        at = r * width + spot * LANES
                        part = jnp.dot(
                            image_ref[at_rows, at : at + length * LANES],
                            partners_ref[r, block * LANES : (block + length) * LANES, :],
                            preferred_element_type=jnp.float32,
                        )
                        total = part if total is None else total + part
            return total

        first, second = half(0), half(1)
        kept = place_ref[0] == place_ref[1]
        keep_ref[...] = jnp.where(kept, first, second)
        send_ref[...] = jnp.where(kept, second, first).astype(jnp.bfloat16)

    return call(
        kernel,
        "products",
        [SMEM] + [VMEM] * (1 + 2 * count) + [ANY] * len(after),
        [VMEM, VMEM],
        [jax.ShapeDtypeStruct((rows, cols), jnp.float32), jax.ShapeDtypeStruct((rows, cols), jnp.bfloat16)],
        (place, partners, *mine, *theirs, *after),
        2.5,
    )


def all_products(chunks, half, partners, mine, theirs):
    modes, cols = mine[0].shape[0], partners.shape[2]
    place = jnp.stack([half, jnp.zeros((), jnp.int32)])
    low = products_of(chunks, place, partners, mine, theirs, [0] * len(chunks), modes)[0]
    high = products_of(chunks, place + jnp.array([0, 1], jnp.int32), partners, mine, theirs, [0] * len(chunks), modes)[0]
    return jnp.stack([low, high])


def settle(cells, bit, rows_dev):
    depth = lax.axis_size("atoms")
    place = lax.axis_index("atoms")
    while cells.shape[0] > 1:
        pairs = cells.reshape(cells.shape[0] // 2, 2, rows_dev, -1)
        own = (place >> bit) & 1
        keep = lax.dynamic_index_in_dim(pairs, own, 1, keepdims=False)
        send = lax.dynamic_index_in_dim(pairs, 1 - own, 1, keepdims=False)
        step = 1 << bit
        got = lax.ppermute(send.astype(jnp.bfloat16), "atoms", [(z, z ^ step) for z in range(depth)])
        cells = keep + got.astype(jnp.float32)
        bit += 1
    return cells[0], bit


def collected(terms, bit, shift):
    groups, depth = lax.axis_size("modes"), lax.axis_size("atoms")
    level = 0
    while (1 << level) < groups:
        moves = []
        for z in range(depth):
            for m in range(groups):
                goal = m ^ shift
                settled = all(((z >> (bit + u)) ^ (goal >> u)) & 1 == 0 for u in range(level))
                if settled and ((z >> (bit + level)) ^ (goal >> level)) & 1:
                    moves.append((z * groups + m, (z ^ (1 << (bit + level))) * groups + m))
        sent = sum(term.astype(jnp.float32) for term in terms).astype(jnp.bfloat16)
        terms = terms + [lax.ppermute(sent, ("atoms", "modes"), moves)]
        level += 1
    return terms


def finish(flag, early, late, my_start, my_length, my_freq, partner_freq, first_col, norm_scale):
    rows, cols = early[0].shape
    n_early, parts, n_late = len(early), len(late), len(late[0])
    operands = [flag, my_start, my_length, my_freq, partner_freq, *early, *[t for part in late for t in part]]

    def kernel(flag_ref, start_ref, length_ref, freq_ref, partner_ref, *refs):
        out_ref, sum_ref = refs[-2:]
        span = rows // parts

        def sums(some):
            total = some[0][...]
            for ref in some[1:]:
                total = total + ref[...].astype(jnp.float32)
            return total

        @pl.when(flag_ref[0] == 1)
        def _():
            out_ref[...] = sums(refs[:n_early])

        @pl.when(flag_ref[0] == 0)
        def _():
            for part in range(parts):
                at = n_early + part * n_late
                out_ref[part * span : (part + 1) * span, :] = sums(refs[at : at + n_late])

        columns = lax.broadcasted_iota(jnp.int32, (rows, cols), 1) + flag_ref[1]
        start = start_ref[...]
        inside = (columns >= start) & (columns < start + length_ref[...])
        elements = jnp.where(inside, out_ref[...] * norm_scale, 0.0)
        out_ref[...] = elements
        offset = freq_ref[...] - partner_ref[...]
        lorentz = lorentz_width / (math.pi * (offset * offset + lorentz_width * lorentz_width))
        weighted = jnp.where(inside, lorentz, 0.0) * elements * elements
        folded = weighted[:, :LANES]
        for at in range(LANES, cols, LANES):
            folded = folded + weighted[:, at : at + LANES]
        if rows < LANES:
            folded = jnp.concatenate([folded, jnp.zeros((LANES - rows, LANES), jnp.float32)], axis=0)
        sum_ref[...] = jnp.sum(folded.T, axis=0, keepdims=True)

    return call(
        kernel,
        "finish",
        [SMEM] + [VMEM] * (len(operands) - 1),
        [VMEM, VMEM],
        [jax.ShapeDtypeStruct((rows, cols), jnp.float32), jax.ShapeDtypeStruct((1, LANES), jnp.float32)],
        operands,
        2.0,
    )


def body(
    mode_panel,
    partners,
    bond_blocks,
    neighbors,
    bond_count,
    panel_freq,
    partner_freq,
    win_start,
    win_len,
):
    atom_rows, modes = mode_panel.shape[1:]
    atom_index = lax.axis_index("atoms")
    atom_count = lax.axis_size("atoms")
    groups = lax.axis_size("modes")
    group_index = lax.axis_index("modes")
    half_index = lax.axis_index("sub")
    column_index = lax.axis_index(("modes", "sub"))
    part_cols = partners.shape[2]
    panel_total = win_start.shape[0]
    rows_dev = panel_total // atom_count
    whole_halves = rows_dev == modes

    nbr = neighbors.T
    coef = bond_blocks.transpose(0, 2, 1)
    base = (atom_index * atom_rows).astype(jnp.int32)[None]

    last = atom_rows // LANES - 1
    middle = list(range(1, last))
    chunks = [middle, [last, 0]]
    shared = (base, mode_panel, nbr, coef, bond_count)
    first_images, head, tail, *first_half = images_of(middle, *shared, edges=True, halved=whole_halves)
    low_halo = lax.ppermute(tail, "atoms", [(z, z + 1) for z in range(atom_count - 1)])
    high_halo = lax.ppermute(head, "atoms", [(z + 1, z) for z in range(atom_count - 1)])
    edge_images, *rest_half = images_of(
        [last, 0],
        *shared,
        halos=(low_halo, high_halo),
        before=first_images if whole_halves else None,
        halved=whole_halves,
    )
    if whole_halves:
        pieces = [first_half[0], rest_half[0], rest_half[1]]
    else:
        pieces = [first_images, edge_images]

    swap = [(0, 1), (1, 0)]

    def from_group(cells, shift):
        return lax.ppermute(cells, "modes", [(m ^ shift, m) for m in range(groups)])

    def from_sibling(cells):
        return lax.ppermute(cells, "sub", swap)

    mine = [first_images, edge_images]
    theirs = [from_sibling(first_images), from_sibling(edge_images)]
    half = half_index.astype(jnp.int32)
    place = jnp.stack([half, (atom_index & 1).astype(jnp.int32)])
    goal = atom_index * groups // atom_count

    far_all = {shift: [from_group(cells, shift) for cells in pieces] for shift in range(1, groups)}
    if whole_halves:
        def level_zero(lists, some_mine, some_theirs, after=()):
            rows = some_mine[0].shape[0]
            keep, send = products_of(lists, place, partners, some_mine, some_theirs, [0] * len(lists), rows, after)
            got = lax.ppermute(send, "atoms", [(z, z ^ 1) for z in range(atom_count)])
            return [keep, got]

        early_zero = level_zero(chunks, mine, theirs, [far[0] for far in far_all.values()])
        early = collected(early_zero, 1, 0)
    else:
        cells, bit = settle(all_products(chunks, half, partners, mine, theirs).reshape(-1, rows_dev, part_cols), 0, rows_dev)
        early = collected([cells], bit, 0)

    late = None
    for shift in range(1, groups):
        far = far_all[shift]
        if whole_halves:
            first, early[0] = lax.optimization_barrier((far[1], early[0]))
            far = [far[0], first, far[2]]
            near = [from_sibling(far[0]), from_sibling(far[1])]
            found = level_zero(chunks, far[:2], near)
            second, found[1] = lax.optimization_barrier((far[2], found[1]))
            terms = [
                collected(found, 1, shift),
                collected(level_zero([middle + [last, 0]], [second], [from_sibling(second)]), 1, shift),
            ]
        else:
            cells, bit = settle(
                all_products(chunks, half, partners, far, [from_sibling(cells) for cells in far]).reshape(-1, rows_dev, part_cols), 0, rows_dev
            )
            terms = [collected([cells], bit, shift)]
        if late is None:
            late = terms
        else:
            here = (group_index ^ shift) == goal
            late = [[jnp.where(here, a, b) for a, b in zip(new, old)] for new, old in zip(terms, late)]

    def my_rows(values):
        return lax.dynamic_slice_in_dim(values, atom_index * rows_dev, rows_dev, 0)

    my_freq = my_rows(panel_freq)
    flag = jnp.stack([(group_index == goal).astype(jnp.int32), (column_index * part_cols).astype(jnp.int32)])
    elements, numerator = finish(
        flag,
        early,
        late,
        my_rows(win_start)[:, None],
        my_rows(win_len)[:, None],
        my_freq[:, None],
        partner_freq[None, :],
        column_index * part_cols,
        1.0 / math.sqrt(3 * atom_rows * atom_count),
    )
    holders = groups * 2
    sums = [numerator] + [
        lax.ppermute(numerator, ("modes", "sub"), [(i, i ^ code) for i in range(holders)])
        for code in range(1, holders)
    ]
    while len(sums) > 1:
        sums = [sums[i] + sums[i + 1] for i in range(0, len(sums), 2)]
    diffusivity = math.pi / 3.0 * sums[0][0, :rows_dev] / (my_freq * my_freq)
    return (elements, diffusivity)


def solution(mesh):
    return jax.shard_map(
        body,
        mesh=mesh,
        in_specs=(
            P(None, ("dom", "atoms"), ("modes", "sub")),
            P(None, ("dom", "atoms"), ("modes", "sub")),
            P(None, ("dom", "atoms"), None),
            P(("dom", "atoms"), None),
            P(("dom", "atoms")),
            P("dom"),
            P(("dom", "modes", "sub")),
            P("dom"),
            P("dom"),
        ),
        out_specs=(P(("dom", "atoms"), ("modes", "sub")), P(("dom", "atoms"))),
        check_vma=False,
    )
```

```python
import math

import jax
import jax.numpy as jnp
from jax import lax
from jax.experimental import pallas as pl
from jax.experimental.pallas import tpu as pltpu
from jax.sharding import PartitionSpec as P

HALO = 96
BONDS = 16
LANES = 128
SPAN = LANES + 2 * HALO
GROUP = 16
VMEM_BYTES = 14 * 1024 * 1024

lorentz_width = 0.05

EARLY_US = 6.0
LATE_US = 0.1

HBM = pl.BlockSpec(memory_space=pltpu.HBM)
ANY = pl.BlockSpec(memory_space=pl.ANY)
VMEM = pl.BlockSpec(memory_space=pltpu.VMEM)
SMEM = pl.BlockSpec(memory_space=pltpu.SMEM)


def call(kernel, name, in_specs, out_specs, out_shape, operands, busy_us, scratch=()):
    return pl.pallas_call(
        kernel,
        in_specs=in_specs,
        out_specs=out_specs,
        out_shape=out_shape,
        scratch_shapes=list(scratch),
        compiler_params=pltpu.CompilerParams(vmem_limit_bytes=VMEM_BYTES),
        cost_estimate=pl.CostEstimate(
            flops=int(busy_us * 1.1e9), bytes_accessed=int(busy_us * 1e5), transcendentals=0
        ),
        name=name,
    )(*operands)


def runs_of(blocks):
    runs = []
    for place, block in enumerate(blocks):
        if runs and runs[-1][1] + runs[-1][2] == block:
            runs[-1][2] += 1
        else:
            runs.append([place, block, 1])
    return runs


def build_block(first, base, nbr_ref, coef_ref, count_ref, dense_ref):
    lanes = pl.ds(first, LANES)
    target = nbr_ref[:, lanes] - (base + (first - HALO))
    slot_ids = lax.broadcasted_iota(jnp.int32, (BONDS, LANES), 0)
    live = slot_ids < count_ref[lanes].reshape(1, LANES)
    coefs = [jnp.where(live, coef_ref[e, :, lanes], 0.0) for e in range(9)]
    halves = [(target[h : h + 8], slot_ids[h : h + 8]) for h in (0, 8)]
    merged = [[jnp.zeros((8, LANES), jnp.float32) for _ in range(9)] for _ in range(2)]
    named = [jnp.broadcast_to(target[k : k + 1], (8, LANES)) for k in range(BONDS)]
    for k in range(BONDS):
        rows = [jnp.broadcast_to(coefs[e][k : k + 1], (8, LANES)) for e in range(9)]
        for h in range(k // 8, 2):
            same = (halves[h][0] == named[k]) & (halves[h][1] >= k)
            for e in range(9):
                merged[h][e] = merged[h][e] + jnp.where(same, rows[e], 0.0)
    row_ids = lax.broadcasted_iota(jnp.int32, (8, LANES), 0)

    def group_step(g, carry):
        cells = [[] for _ in range(9)]
        for tile in range(GROUP // 8):
            here = row_ids + (g * GROUP + tile * 8)
            slot = jnp.full((8, LANES), -1, jnp.int32)
            for k in range(BONDS):
                slot = jnp.where(named[k] == here, k, slot)
            place = slot & 7
            early, live_cell = slot < 8, slot >= 0
            for e in range(9):
                picks = [
                    jnp.take_along_axis(merged[h][e], place, axis=0, mode="promise_in_bounds")
                    for h in range(2)
                ]
                cells[e].append(jnp.where(live_cell, jnp.where(early, picks[0], picks[1]), 0.0))
        for r in range(3):
            for c in range(3):
                value = jnp.concatenate(cells[3 * r + c], axis=0)
                high = value.astype(jnp.bfloat16)
                low = (value - high.astype(jnp.float32)).astype(jnp.bfloat16)
                at = pl.ds(pl.multiple_of(c * SPAN + g * GROUP, GROUP), GROUP)
                dense_ref[at, 2 * r * LANES : (2 * r + 1) * LANES] = high
                dense_ref[at, (2 * r + 1) * LANES : (2 * r + 2) * LANES] = low
        return carry

    lax.fori_loop(0, SPAN // GROUP, group_step, 0)


def window(first, rows, c, panel_ref, low_ref, high_ref):
    begin, end = first - HALO, first - HALO + SPAN
    if begin < 0:
        return jnp.concatenate([low_ref[c, HALO + begin :], panel_ref[c, :end]], axis=0)
    if end > rows:
        return jnp.concatenate([panel_ref[c, begin:], high_ref[c, : end - rows]], axis=0)
    return panel_ref[c, begin:end]


def images_of(blocks, base, panel, nbr, coef, count, halos=(), before=None, joined=False, edges=False, halved=False):
    rows, modes = panel.shape[1:]
    operands = [base, *[pltpu.with_memory_space_constraint(x, pltpu.HBM) for x in (nbr, count, coef, panel)], *halos]
    in_specs = [SMEM] + [HBM] * 4 + [ANY] * len(halos)
    old = 0
    if before is not None:
        operands.append(before)
        in_specs.append(VMEM)
        old = before.shape[1] // 3
    ahead = old if joined else 0
    width = ahead + len(blocks) * LANES
    tail = halved and before is not None and not joined
    out_shape = [jax.ShapeDtypeStruct((modes, 3 * width), jnp.bfloat16)]
    out_specs = [VMEM]
    if edges:
        out_shape += [jax.ShapeDtypeStruct((3, HALO, modes), jnp.bfloat16)] * 2
        out_specs += [ANY] * 2
    if halved:
        out_shape.append(jax.ShapeDtypeStruct((modes // 2, 3 * width), jnp.bfloat16))
        out_specs.append(VMEM)
        if tail:
            out_shape.append(jax.ShapeDtypeStruct((modes // 2, 3 * (old + width)), jnp.bfloat16))
            out_specs.append(VMEM)
    n_in, n_out = len(operands), len(out_shape)

    def kernel(*refs):
        base_ref, nbr_hbm, count_hbm, coef_hbm, panel_hbm = refs[:5]
        outs = refs[n_in : n_in + n_out]
        nbr_ref, count_ref, coef_ref, panel_ref, low_ref, high_ref, dense_ref, sems = refs[n_in + n_out :]
        copies, panel_copies = [], []

        def start(source, target, kept):
            copy = pltpu.make_async_copy(source, target, sems.at[len(copies) + len(panel_copies)])
            copy.start()
            kept.append(copy)

        start(nbr_hbm, nbr_ref, copies)
        start(count_hbm, count_ref, copies)
        for _, block, length in runs_of(blocks):
            at = pl.ds(block * LANES, length * LANES)
            start(coef_hbm.at[:, :, at], coef_ref.at[:, :, at], copies)
        for _, block, length in runs_of(blocks):
            begin = max(block * LANES - HALO, 0)
            end = min((block + length) * LANES + HALO, rows)
            at = pl.ds(begin, end - begin)
            start(panel_hbm.at[:, at], panel_ref.at[:, at], panel_copies)
        if halos:
            start(refs[5], low_ref, panel_copies)
            start(refs[6], high_ref, panel_copies)
        if edges:
            start(panel_hbm.at[:, pl.ds(0, HALO)], outs[1], panel_copies)
            start(panel_hbm.at[:, pl.ds(rows - HALO, HALO)], outs[2], panel_copies)
        for copy in copies:
            copy.wait()
        for place, block in enumerate(blocks):
            first = block * LANES
            build_block(first, base_ref[0], nbr_ref, coef_ref, count_ref, dense_ref)
            if place == 0:
                for copy in panel_copies:
                    copy.wait()
            cells = jnp.concatenate(
                [window(first, rows, c, panel_ref, low_ref, high_ref) for c in range(3)], axis=0
            )
            both = lax.dot_general(
                cells, dense_ref[...], (((0,), (0,)), ((), ())), preferred_element_type=jnp.float32
            )
            for r in range(3):
                image = both[:, 2 * r * LANES : (2 * r + 1) * LANES]
                image = image + both[:, (2 * r + 1) * LANES : (2 * r + 2) * LANES]
                at = r * width + ahead + place * LANES
                outs[0][:, at : at + LANES] = image.astype(jnp.bfloat16)
        if joined:
            for r in range(3):
                outs[0][:, r * width : r * width + old] = refs[n_in - 1][:, r * old : (r + 1) * old]
        if halved:
            span = modes // 2
            half_ref = outs[-2] if tail else outs[-1]
            half_ref[...] = outs[0][:span, :]
            if tail:
                for r in range(3):
                    at = r * (old + width)
                    outs[-1][:, at : at + old] = refs[n_in - 1][span:, r * old : (r + 1) * old]
                    outs[-1][:, at + old : at + old + width] = outs[0][span:, r * width : (r + 1) * width]

    copies_most = 2 + 2 * len(runs_of(blocks)) + 4
    scratch = [
        pltpu.VMEM((BONDS, rows), jnp.int32),
        pltpu.VMEM((rows,), jnp.int32),
        pltpu.VMEM((9, BONDS, rows), jnp.float32),
        pltpu.VMEM((3, rows, modes), jnp.bfloat16),
        pltpu.VMEM((3, HALO, modes), jnp.bfloat16),
        pltpu.VMEM((3, HALO, modes), jnp.bfloat16),
        pltpu.VMEM((3 * SPAN, 6 * LANES), jnp.bfloat16),
        pltpu.SemaphoreType.DMA((copies_most,)),
    ]
    return call(kernel, "images", in_specs, out_specs, out_shape, operands, 0.8 + 1.2 * len(blocks), scratch)


def products_of(chunks, place, partners, mine, theirs, after=(), busy_us=2.0):
    rows, cols = mine[0].shape[0], partners.shape[2]
    count = len(chunks)
    depth = partners.shape[1]

    def kernel(place_ref, partners_ref, *refs):
        keep_ref, send_ref, left_ref = refs[-3:]
        kept = place_ref[0] == place_ref[1]
        for who in range(2):
            at_rows = pl.ds(pl.multiple_of(jnp.where(kept == (who == 0), 0, rows), rows), rows)
            for i, blocks in enumerate(chunks):
                image_ref = refs[who * count + i]
                width = len(blocks) * LANES
                for r in range(3):
                    for spot, block, length in runs_of(blocks):
                        at, to = r * width + spot * LANES, r * depth + block * LANES
                        left_ref[at_rows, to : to + length * LANES] = image_ref[:, at : at + length * LANES]
        total = jnp.dot(
            left_ref[...], partners_ref[...].reshape(3 * depth, cols), preferred_element_type=jnp.float32
        )
        keep_ref[...] = total[:rows]
        send_ref[...] = total[rows:].astype(jnp.bfloat16)

    return call(
        kernel,
        "products",
        [SMEM] + [VMEM] * (1 + 2 * count) + [ANY] * len(after),
        [VMEM, VMEM],
        [jax.ShapeDtypeStruct((rows, cols), jnp.float32), jax.ShapeDtypeStruct((rows, cols), jnp.bfloat16)],
        (place, partners, *mine, *theirs, *after),
        busy_us,
        [pltpu.VMEM((2 * rows, 3 * depth), jnp.bfloat16)],
    )


def all_products(chunks, half, partners, mine, theirs):
    place = jnp.stack([half, jnp.zeros((), jnp.int32)])
    low = products_of(chunks, place, partners, mine, theirs)[0]
    high = products_of(chunks, place + jnp.array([0, 1], jnp.int32), partners, mine, theirs)[0]
    return jnp.stack([low, high])


def settle(cells, bit, rows_dev):
    depth = lax.axis_size("atoms")
    place = lax.axis_index("atoms")
    while cells.shape[0] > 1:
        pairs = cells.reshape(cells.shape[0] // 2, 2, rows_dev, -1)
        own = (place >> bit) & 1
        keep = lax.dynamic_index_in_dim(pairs, own, 1, keepdims=False)
        send = lax.dynamic_index_in_dim(pairs, 1 - own, 1, keepdims=False)
        step = 1 << bit
        got = lax.ppermute(send.astype(jnp.bfloat16), "atoms", [(z, z ^ step) for z in range(depth)])
        cells = keep + got.astype(jnp.float32)
        bit += 1
    return cells[0], bit


def collected(terms, bit, shift):
    groups, depth = lax.axis_size("modes"), lax.axis_size("atoms")
    level = 0
    while (1 << level) < groups:
        moves = []
        for z in range(depth):
            for m in range(groups):
                goal = m ^ shift
                settled = all(((z >> (bit + u)) ^ (goal >> u)) & 1 == 0 for u in range(level))
                if settled and ((z >> (bit + level)) ^ (goal >> level)) & 1:
                    moves.append((z * groups + m, (z ^ (1 << (bit + level))) * groups + m))
        sent = sum(term.astype(jnp.float32) for term in terms).astype(jnp.bfloat16)
        terms = terms + [lax.ppermute(sent, ("atoms", "modes"), moves)]
        level += 1
    return terms


def finish(flag, early, late, my_start, my_length, my_freq, partner_freq, first_col, norm_scale):
    rows, cols = early[0].shape
    n_early, parts, n_late = len(early), len(late), len(late[0])
    operands = [flag, my_start, my_length, my_freq, partner_freq, *early, *[t for part in late for t in part]]

    def kernel(flag_ref, start_ref, length_ref, freq_ref, partner_ref, *refs):
        out_ref, sum_ref = refs[-2:]
        span = rows // parts

        def sums(some):
            total = some[0][...]
            for ref in some[1:]:
                total = total + ref[...].astype(jnp.float32)
            return total

        @pl.when(flag_ref[0] == 1)
        def _():
            out_ref[...] = sums(refs[:n_early])

        @pl.when(flag_ref[0] == 0)
        def _():
            for part in range(parts):
                at = n_early + part * n_late
                out_ref[part * span : (part + 1) * span, :] = sums(refs[at : at + n_late])

        columns = lax.broadcasted_iota(jnp.int32, (rows, cols), 1) + flag_ref[1]
        start = start_ref[...]
        inside = (columns >= start) & (columns < start + length_ref[...])
        elements = jnp.where(inside, out_ref[...] * norm_scale, 0.0)
        out_ref[...] = elements
        offset = freq_ref[...] - partner_ref[...]
        lorentz = lorentz_width / (math.pi * (offset * offset + lorentz_width * lorentz_width))
        weighted = jnp.where(inside, lorentz, 0.0) * elements * elements
        folded = weighted[:, :LANES]
        for at in range(LANES, cols, LANES):
            folded = folded + weighted[:, at : at + LANES]
        if rows < LANES:
            folded = jnp.concatenate([folded, jnp.zeros((LANES - rows, LANES), jnp.float32)], axis=0)
        sum_ref[...] = jnp.sum(folded.T, axis=0, keepdims=True)

    return call(
        kernel,
        "finish",
        [SMEM] + [VMEM] * (len(operands) - 1),
        [VMEM, VMEM],
        [jax.ShapeDtypeStruct((rows, cols), jnp.float32), jax.ShapeDtypeStruct((1, LANES), jnp.float32)],
        operands,
        2.0,
    )


def body(
    mode_panel,
    partners,
    bond_blocks,
    neighbors,
    bond_count,
    panel_freq,
    partner_freq,
    win_start,
    win_len,
):
    atom_rows, modes = mode_panel.shape[1:]
    atom_index = lax.axis_index("atoms")
    atom_count = lax.axis_size("atoms")
    groups = lax.axis_size("modes")
    group_index = lax.axis_index("modes")
    half_index = lax.axis_index("sub")
    column_index = lax.axis_index(("modes", "sub"))
    part_cols = partners.shape[2]
    panel_total = win_start.shape[0]
    rows_dev = panel_total // atom_count
    whole_halves = rows_dev == modes

    nbr = neighbors.T
    coef = bond_blocks.transpose(0, 2, 1)
    base = (atom_index * atom_rows).astype(jnp.int32)[None]

    last = atom_rows // LANES - 1
    middle = list(range(1, last))
    chunks = [middle, [last, 0]]
    shared = (base, mode_panel, nbr, coef, bond_count)
    cut = len(middle) // 2
    opening, head, tail = images_of(middle[:cut], *shared, edges=True)
    low_halo = lax.ppermute(tail, "atoms", [(z, z + 1) for z in range(atom_count - 1)])
    high_halo = lax.ppermute(head, "atoms", [(z + 1, z) for z in range(atom_count - 1)])
    first_images, *first_half = images_of(middle[cut:], *shared, before=opening, joined=True, halved=whole_halves)
    edge_images, *rest_half = images_of(
        [last, 0],
        *shared,
        halos=(low_halo, high_halo),
        before=first_images if whole_halves else None,
        halved=whole_halves,
    )
    if whole_halves:
        pieces = [first_half[0], rest_half[0], rest_half[1]]
    else:
        pieces = [first_images, edge_images]

    swap = [(0, 1), (1, 0)]

    def from_group(cells, shift):
        return lax.ppermute(cells, "modes", [(m ^ shift, m) for m in range(groups)])

    def from_sibling(cells):
        return lax.ppermute(cells, "sub", swap)

    mine = [first_images, edge_images]
    theirs = [from_sibling(first_images), from_sibling(edge_images)]
    half = half_index.astype(jnp.int32)
    place = jnp.stack([half, (atom_index & 1).astype(jnp.int32)])
    goal = atom_index * groups // atom_count

    far_all = {shift: [from_group(cells, shift) for cells in pieces] for shift in range(1, groups)}
    if whole_halves:
        def level_zero(lists, some_mine, some_theirs, after=()):
            keep, send = products_of(
                lists, place, partners, some_mine, some_theirs, after, EARLY_US if after else LATE_US
            )
            got = lax.ppermute(send, "atoms", [(z, z ^ 1) for z in range(atom_count)])
            return [keep, got]

        early_zero = level_zero(chunks, mine, theirs, [far[0] for far in far_all.values()])
        early = collected(early_zero, 1, 0)
    else:
        cells, bit = settle(all_products(chunks, half, partners, mine, theirs).reshape(-1, rows_dev, part_cols), 0, rows_dev)
        early = collected([cells], bit, 0)

    late = None
    for shift in range(1, groups):
        far = far_all[shift]
        if whole_halves:
            first, early[0] = lax.optimization_barrier((far[1], early[0]))
            far = [far[0], first, far[2]]
            near = [from_sibling(far[0]), from_sibling(far[1])]
            found = level_zero(chunks, far[:2], near)
            second, found[1] = lax.optimization_barrier((far[2], found[1]))
            terms = [
                collected(found, 1, shift),
                collected(level_zero([middle + [last, 0]], [second], [from_sibling(second)]), 1, shift),
            ]
        else:
            cells, bit = settle(
                all_products(chunks, half, partners, far, [from_sibling(cells) for cells in far]).reshape(-1, rows_dev, part_cols), 0, rows_dev
            )
            terms = [collected([cells], bit, shift)]
        if late is None:
            late = terms
        else:
            here = (group_index ^ shift) == goal
            late = [[jnp.where(here, a, b) for a, b in zip(new, old)] for new, old in zip(terms, late)]

    def my_rows(values):
        return lax.dynamic_slice_in_dim(values, atom_index * rows_dev, rows_dev, 0)

    my_freq = my_rows(panel_freq)
    flag = jnp.stack([(group_index == goal).astype(jnp.int32), (column_index * part_cols).astype(jnp.int32)])
    elements, numerator = finish(
        flag,
        early,
        late,
        my_rows(win_start)[:, None],
        my_rows(win_len)[:, None],
        my_freq[:, None],
        partner_freq[None, :],
        column_index * part_cols,
        1.0 / math.sqrt(3 * atom_rows * atom_count),
    )
    holders = groups * 2
    sums = [numerator] + [
        lax.ppermute(numerator, ("modes", "sub"), [(i, i ^ code) for i in range(holders)])
        for code in range(1, holders)
    ]
    while len(sums) > 1:
        sums = [sums[i] + sums[i + 1] for i in range(0, len(sums), 2)]
    diffusivity = math.pi / 3.0 * sums[0][0, :rows_dev] / (my_freq * my_freq)
    return (elements, diffusivity)


def solution(mesh):
    return jax.shard_map(
        body,
        mesh=mesh,
        in_specs=(
            P(None, ("dom", "atoms"), ("modes", "sub")),
            P(None, ("dom", "atoms"), ("modes", "sub")),
            P(None, ("dom", "atoms"), None),
            P(("dom", "atoms"), None),
            P(("dom", "atoms")),
            P("dom"),
            P(("dom", "modes", "sub")),
            P("dom"),
            P("dom"),
        ),
        out_specs=(P(("dom", "atoms"), ("modes", "sub")), P(("dom", "atoms"))),
        check_vma=False,
    )
```

```python
import math

import jax
import jax.numpy as jnp
from jax import lax
from jax.experimental import pallas as pl
from jax.experimental.pallas import tpu as pltpu
from jax.sharding import PartitionSpec as P

HALO = 96
BONDS = 16
LANES = 128
SPAN = LANES + 2 * HALO
GROUP = 16
VMEM_BYTES = 14 * 1024 * 1024

lorentz_width = 0.05

EARLY_US = 6.0
LATE_US = 0.1

HBM = pl.BlockSpec(memory_space=pltpu.HBM)
ANY = pl.BlockSpec(memory_space=pl.ANY)
VMEM = pl.BlockSpec(memory_space=pltpu.VMEM)
SMEM = pl.BlockSpec(memory_space=pltpu.SMEM)


def call(kernel, name, in_specs, out_specs, out_shape, operands, busy_us, scratch=()):
    return pl.pallas_call(
        kernel,
        in_specs=in_specs,
        out_specs=out_specs,
        out_shape=out_shape,
        scratch_shapes=list(scratch),
        compiler_params=pltpu.CompilerParams(vmem_limit_bytes=VMEM_BYTES),
        cost_estimate=pl.CostEstimate(
            flops=int(busy_us * 1.1e9), bytes_accessed=int(busy_us * 1e5), transcendentals=0
        ),
        name=name,
    )(*operands)


def runs_of(blocks):
    runs = []
    for place, block in enumerate(blocks):
        if runs and runs[-1][1] + runs[-1][2] == block:
            runs[-1][2] += 1
        else:
            runs.append([place, block, 1])
    return runs


def build_block(first, base, nbr_ref, coef_ref, count_ref, dense_ref):
    lanes = pl.ds(first, LANES)
    target = nbr_ref[:, lanes] - (base + (first - HALO))
    slot_ids = lax.broadcasted_iota(jnp.int32, (BONDS, LANES), 0)
    live = slot_ids < count_ref[lanes].reshape(1, LANES)
    coefs = [jnp.where(live, coef_ref[e, :, lanes], 0.0) for e in range(9)]
    halves = [(target[h : h + 8], slot_ids[h : h + 8]) for h in (0, 8)]
    merged = [[jnp.zeros((8, LANES), jnp.float32) for _ in range(9)] for _ in range(2)]
    named = [jnp.broadcast_to(target[k : k + 1], (8, LANES)) for k in range(BONDS)]
    for k in range(BONDS):
        rows = [jnp.broadcast_to(coefs[e][k : k + 1], (8, LANES)) for e in range(9)]
        for h in range(k // 8, 2):
            same = (halves[h][0] == named[k]) & (halves[h][1] >= k)
            for e in range(9):
                merged[h][e] = merged[h][e] + jnp.where(same, rows[e], 0.0)
    row_ids = lax.broadcasted_iota(jnp.int32, (8, LANES), 0)

    def group_step(g, carry):
        cells = [[] for _ in range(9)]
        for tile in range(GROUP // 8):
            here = row_ids + (g * GROUP + tile * 8)
            slot = jnp.full((8, LANES), -1, jnp.int32)
            for k in range(BONDS):
                slot = jnp.where(named[k] == here, k, slot)
            place = slot & 7
            early, live_cell = slot < 8, slot >= 0
            for e in range(9):
                picks = [
                    jnp.take_along_axis(merged[h][e], place, axis=0, mode="promise_in_bounds")
                    for h in range(2)
                ]
                cells[e].append(jnp.where(live_cell, jnp.where(early, picks[0], picks[1]), 0.0))
        for r in range(3):
            for c in range(3):
                value = jnp.concatenate(cells[3 * r + c], axis=0)
                high = value.astype(jnp.bfloat16)
                low = (value - high.astype(jnp.float32)).astype(jnp.bfloat16)
                at = pl.ds(pl.multiple_of(c * SPAN + g * GROUP, GROUP), GROUP)
                dense_ref[at, 2 * r * LANES : (2 * r + 1) * LANES] = high
                dense_ref[at, (2 * r + 1) * LANES : (2 * r + 2) * LANES] = low
        return carry

    lax.fori_loop(0, SPAN // GROUP, group_step, 0)


def images_of(blocks, base, panel, nbr, coef, count, halos=(), before=None, joined=False, edges=False, halved=False):
    rows, modes = panel.shape[1:]
    loads = before is None
    operands = [nbr, count, coef, panel]
    if loads:
        operands = [pltpu.with_memory_space_constraint(x, pltpu.HBM) for x in operands]
    operands = [base, *operands, *halos]
    in_specs = [SMEM] + [HBM if loads else VMEM] * 4 + [VMEM] * len(halos)
    old = 0
    if before is not None:
        operands.append(before)
        in_specs.append(VMEM)
        old = before.shape[1] // 3
    ahead = old if joined else 0
    width = ahead + len(blocks) * LANES
    tail = halved and before is not None and not joined
    out_shape = [jax.ShapeDtypeStruct((modes, 3 * width), jnp.bfloat16)]
    out_specs = [VMEM]
    if edges:
        out_shape += [jax.ShapeDtypeStruct((3, HALO, modes), jnp.bfloat16)] * 2
        out_specs += [ANY] * 2
    if halved:
        out_shape.append(jax.ShapeDtypeStruct((modes // 2, 3 * width), jnp.bfloat16))
        out_specs.append(VMEM)
        if tail:
            out_shape.append(jax.ShapeDtypeStruct((modes // 2, 3 * (old + width)), jnp.bfloat16))
            out_specs.append(VMEM)
    n_in, n_out = len(operands), len(out_shape)

    def pieces_of(block):
        begin, end = block * LANES - HALO, (block + 1) * LANES + HALO
        found = []
        if begin < 0:
            found.append((1, HALO + begin, 0, -begin))
        low, high = max(begin, 0), min(end, rows)
        found.append((0, low, low - begin, high - low))
        if end > rows:
            found.append((2, 0, rows - begin, end - rows))
        return found

    def kernel(*refs):
        base_ref, nbr_ref, count_ref, coef_ref, panel_ref = refs[:5]
        outs = refs[n_in : n_in + n_out]
        window_ref, dense_ref, *scratch_refs = refs[n_in + n_out :]
        window_copies = []
        if loads:
            sources = (nbr_ref, count_ref, coef_ref)
            nbr_ref, count_ref, coef_ref, sems = scratch_refs
            copies = []

            def start(source, target, kept):
                copy = pltpu.make_async_copy(source, target, sems.at[len(copies) + len(window_copies)])
                copy.start()
                kept.append(copy)

            start(sources[0], nbr_ref, copies)
            start(sources[1], count_ref, copies)
            for _, block, length in runs_of(blocks):
                at = pl.ds(block * LANES, length * LANES)
                start(sources[2].at[:, :, at], coef_ref.at[:, :, at], copies)
            for place, block in enumerate(blocks):
                for _, source, at, length in pieces_of(block):
                    start(
                        panel_ref.at[:, pl.ds(source, length)], window_ref.at[place, :, pl.ds(at, length)], window_copies
                    )
            if edges:
                start(panel_ref.at[:, pl.ds(0, HALO)], outs[1], window_copies)
                start(panel_ref.at[:, pl.ds(rows - HALO, HALO)], outs[2], window_copies)
            for copy in copies:
                copy.wait()
        else:
            for place, block in enumerate(blocks):
                for which, source, at, length in pieces_of(block):
                    source_ref = (panel_ref, *refs[5:])[which]
                    window_ref[place, :, at : at + length, :] = source_ref[:, source : source + length, :]

        def block_step(place, carry):
            first = (blocks[0] + place * (blocks[1] - blocks[0])) * LANES
            build_block(pl.multiple_of(first, LANES), base_ref[0], nbr_ref, coef_ref, count_ref, dense_ref)
            if loads:

                @pl.when(place == 0)
                def _():
                    for copy in window_copies:
                        copy.wait()

            both = lax.dot_general(
                window_ref[place].reshape(3 * SPAN, modes),
                dense_ref[...],
                (((0,), (0,)), ((), ())),
                preferred_element_type=jnp.float32,
            )
            for r in range(3):
                image = both[:, 2 * r * LANES : (2 * r + 1) * LANES]
                image = image + both[:, (2 * r + 1) * LANES : (2 * r + 2) * LANES]
                at = pl.multiple_of(r * width + ahead + place * LANES, LANES)
                outs[0][:, pl.ds(at, LANES)] = image.astype(jnp.bfloat16)
            return carry

        lax.fori_loop(0, len(blocks), block_step, 0)
        if joined:
            for r in range(3):
                outs[0][:, r * width : r * width + old] = refs[n_in - 1][:, r * old : (r + 1) * old]
        if halved:
            span = modes // 2
            half_ref = outs[-2] if tail else outs[-1]
            half_ref[...] = outs[0][:span, :]
            if tail:
                for r in range(3):
                    at = r * (old + width)
                    outs[-1][:, at : at + old] = refs[n_in - 1][span:, r * old : (r + 1) * old]
                    outs[-1][:, at + old : at + old + width] = outs[0][span:, r * width : (r + 1) * width]

    scratch = [
        pltpu.VMEM((len(blocks), 3, SPAN, modes), jnp.bfloat16),
        pltpu.VMEM((3 * SPAN, 6 * LANES), jnp.bfloat16),
    ]
    if loads:
        scratch += [
            pltpu.VMEM((BONDS, rows), jnp.int32),
            pltpu.VMEM((rows,), jnp.int32),
            pltpu.VMEM((9, BONDS, rows), jnp.float32),
            pltpu.SemaphoreType.DMA((4 + 3 * len(blocks) + 2,)),
        ]
    return call(kernel, "images", in_specs, out_specs, out_shape, operands, 0.8 + 1.2 * len(blocks), scratch)


def products_of(chunks, place, partners, mine, theirs, after=(), busy_us=2.0):
    rows, cols = mine[0].shape[0], partners.shape[2]
    count = len(chunks)
    depth = partners.shape[1]

    def kernel(place_ref, partners_ref, *refs):
        keep_ref, send_ref, left_ref, total_ref = refs[-4:]
        kept = place_ref[0] == place_ref[1]
        for who in range(2):
            at_rows = pl.ds(pl.multiple_of(jnp.where(kept == (who == 0), 0, rows), rows), rows)
            for i, blocks in enumerate(chunks):
                image_ref = refs[who * count + i]
                width = len(blocks) * LANES
                for r in range(3):
                    for spot, block, length in runs_of(blocks):
                        at, to = r * width + spot * LANES, block * LANES
                        left_ref[r, at_rows, to : to + length * LANES] = image_ref[:, at : at + length * LANES]

        def component(r, carry):
            total_ref[...] = total_ref[...] + jnp.dot(
                left_ref[r], partners_ref[r], preferred_element_type=jnp.float32
            )
            return carry

        total_ref[...] = jnp.zeros_like(total_ref)
        lax.fori_loop(0, 3, component, 0)
        keep_ref[...] = total_ref[:rows]
        send_ref[...] = total_ref[rows:].astype(jnp.bfloat16)

    return call(
        kernel,
        "products",
        [SMEM] + [VMEM] * (1 + 2 * count) + [ANY] * len(after),
        [VMEM, VMEM],
        [jax.ShapeDtypeStruct((rows, cols), jnp.float32), jax.ShapeDtypeStruct((rows, cols), jnp.bfloat16)],
        (place, partners, *mine, *theirs, *after),
        busy_us,
        [pltpu.VMEM((3, 2 * rows, depth), jnp.bfloat16), pltpu.VMEM((2 * rows, cols), jnp.float32)],
    )


def all_products(chunks, half, partners, mine, theirs):
    place = jnp.stack([half, jnp.zeros((), jnp.int32)])
    low = products_of(chunks, place, partners, mine, theirs)[0]
    high = products_of(chunks, place + jnp.array([0, 1], jnp.int32), partners, mine, theirs)[0]
    return jnp.stack([low, high])


def settle(cells, bit, rows_dev):
    depth = lax.axis_size("atoms")
    place = lax.axis_index("atoms")
    while cells.shape[0] > 1:
        pairs = cells.reshape(cells.shape[0] // 2, 2, rows_dev, -1)
        own = (place >> bit) & 1
        keep = lax.dynamic_index_in_dim(pairs, own, 1, keepdims=False)
        send = lax.dynamic_index_in_dim(pairs, 1 - own, 1, keepdims=False)
        step = 1 << bit
        got = lax.ppermute(send.astype(jnp.bfloat16), "atoms", [(z, z ^ step) for z in range(depth)])
        cells = keep + got.astype(jnp.float32)
        bit += 1
    return cells[0], bit


def collected(terms, bit, shift):
    groups, depth = lax.axis_size("modes"), lax.axis_size("atoms")
    level = 0
    while (1 << level) < groups:
        moves = []
        for z in range(depth):
            for m in range(groups):
                goal = m ^ shift
                settled = all(((z >> (bit + u)) ^ (goal >> u)) & 1 == 0 for u in range(level))
                if settled and ((z >> (bit + level)) ^ (goal >> level)) & 1:
                    moves.append((z * groups + m, (z ^ (1 << (bit + level))) * groups + m))
        sent = sum(term.astype(jnp.float32) for term in terms).astype(jnp.bfloat16)
        terms = terms + [lax.ppermute(sent, ("atoms", "modes"), moves)]
        level += 1
    return terms


def finish(flag, early, late, starts, lengths, freqs, partner_freq, norm_scale):
    rows, cols = early[0].shape
    n_early, parts, n_late = len(early), len(late), len(late[0])
    operands = [flag, starts, lengths, freqs, partner_freq, *early, *[t for part in late for t in part]]
    step = 16

    def kernel(flag_ref, starts_ref, lengths_ref, freqs_ref, partner_ref, *refs):
        out_ref, sum_ref, start_ref, end_ref, freq_ref, folded_ref = refs[-6:]
        span = rows // parts

        def sums(some):
            total = some[0][...]
            for ref in some[1:]:
                total = total + ref[...].astype(jnp.float32)
            return total

        @pl.when(flag_ref[0] == 1)
        def _():
            out_ref[...] = sums(refs[:n_early])

        @pl.when(flag_ref[0] == 0)
        def _():
            for part in range(parts):
                at = n_early + part * n_late
                out_ref[part * span : (part + 1) * span, :] = sums(refs[at : at + n_late])

        def turned(row):
            return jnp.broadcast_to(row, (LANES, rows)).T

        mine = pl.ds(flag_ref[2], 1)
        start_row = starts_ref[mine, :].astype(jnp.float32)
        start_ref[...] = turned(start_row)
        end_ref[...] = turned(start_row + lengths_ref[mine, :].astype(jnp.float32))
        freq_ref[...] = turned(freqs_ref[mine, :])
        lane_ids = lax.broadcasted_iota(jnp.int32, (step, LANES), 1)

        def row_step(i, carry):
            at_rows = pl.ds(pl.multiple_of(i * step, step), step)
            start, end, freq = start_ref[at_rows, :], end_ref[at_rows, :], freq_ref[at_rows, :]
            folded = jnp.zeros((step, LANES), jnp.float32)
            for at in range(0, cols, LANES):
                columns = (lane_ids + (flag_ref[1] + at)).astype(jnp.float32)
                inside = (columns >= start) & (columns < end)
                elements = jnp.where(inside, out_ref[at_rows, at : at + LANES] * norm_scale, 0.0)
                out_ref[at_rows, at : at + LANES] = elements
                offset = freq - partner_ref[:, at : at + LANES]
                lorentz = lorentz_width / (math.pi * (offset * offset + lorentz_width * lorentz_width))
                folded = folded + jnp.where(inside, lorentz, 0.0) * elements * elements
            folded_ref[at_rows, :] = folded
            return carry

        lax.fori_loop(0, rows // step, row_step, 0)
        sum_ref[...] = jnp.sum(folded_ref[...].T, axis=0, keepdims=True)

    return call(
        kernel,
        "finish",
        [SMEM] + [VMEM] * (len(operands) - 1),
        [VMEM, VMEM],
        [jax.ShapeDtypeStruct((rows, cols), jnp.float32), jax.ShapeDtypeStruct((1, rows), jnp.float32)],
        operands,
        2.0,
        [pltpu.VMEM((rows, LANES), jnp.float32)] * 4,
    )


def body(
    mode_panel,
    partners,
    bond_blocks,
    neighbors,
    bond_count,
    panel_freq,
    partner_freq,
    win_start,
    win_len,
):
    atom_rows, modes = mode_panel.shape[1:]
    atom_index = lax.axis_index("atoms")
    atom_count = lax.axis_size("atoms")
    groups = lax.axis_size("modes")
    group_index = lax.axis_index("modes")
    half_index = lax.axis_index("sub")
    column_index = lax.axis_index(("modes", "sub"))
    part_cols = partners.shape[2]
    panel_total = win_start.shape[0]
    rows_dev = panel_total // atom_count
    whole_halves = rows_dev == modes

    nbr = neighbors.T
    coef = bond_blocks.transpose(0, 2, 1)
    base = (atom_index * atom_rows).astype(jnp.int32)[None]

    last = atom_rows // LANES - 1
    middle = list(range(1, last))
    chunks = [middle, [last, 0]]
    shared = (base, mode_panel, nbr, coef, bond_count)
    cut = len(middle) // 2
    opening, head, tail = images_of(middle[:cut], *shared, edges=True)
    low_halo = lax.ppermute(tail, "atoms", [(z, z + 1) for z in range(atom_count - 1)])
    high_halo = lax.ppermute(head, "atoms", [(z + 1, z) for z in range(atom_count - 1)])
    first_images, *first_half = images_of(middle[cut:], *shared, before=opening, joined=True, halved=whole_halves)
    edge_images, *rest_half = images_of(
        [last, 0],
        *shared,
        halos=(low_halo, high_halo),
        before=first_images if whole_halves else None,
        halved=whole_halves,
    )
    if whole_halves:
        pieces = [first_half[0], rest_half[0], rest_half[1]]
    else:
        pieces = [first_images, edge_images]

    swap = [(0, 1), (1, 0)]

    def from_group(cells, shift):
        return lax.ppermute(cells, "modes", [(m ^ shift, m) for m in range(groups)])

    def from_sibling(cells):
        return lax.ppermute(cells, "sub", swap)

    mine = [first_images, edge_images]
    theirs = [from_sibling(first_images), from_sibling(edge_images)]
    half = half_index.astype(jnp.int32)
    place = jnp.stack([half, (atom_index & 1).astype(jnp.int32)])
    goal = atom_index * groups // atom_count

    far_all = {shift: [from_group(cells, shift) for cells in pieces] for shift in range(1, groups)}
    if whole_halves:
        def level_zero(lists, some_mine, some_theirs, after=()):
            keep, send = products_of(
                lists, place, partners, some_mine, some_theirs, after, EARLY_US if after else LATE_US
            )
            got = lax.ppermute(send, "atoms", [(z, z ^ 1) for z in range(atom_count)])
            return [keep, got]

        early_zero = level_zero(chunks, mine, theirs, [far[0] for far in far_all.values()])
        early = collected(early_zero, 1, 0)
    else:
        cells, bit = settle(all_products(chunks, half, partners, mine, theirs).reshape(-1, rows_dev, part_cols), 0, rows_dev)
        early = collected([cells], bit, 0)

    late = None
    for shift in range(1, groups):
        far = far_all[shift]
        if whole_halves:
            first, early[0] = lax.optimization_barrier((far[1], early[0]))
            far = [far[0], first, far[2]]
            near = [from_sibling(far[0]), from_sibling(far[1])]
            found = level_zero(chunks, far[:2], near)
            second, found[1] = lax.optimization_barrier((far[2], found[1]))
            terms = [
                collected(found, 1, shift),
                collected(level_zero([middle + [last, 0]], [second], [from_sibling(second)]), 1, shift),
            ]
        else:
            cells, bit = settle(
                all_products(chunks, half, partners, far, [from_sibling(cells) for cells in far]).reshape(-1, rows_dev, part_cols), 0, rows_dev
            )
            terms = [collected([cells], bit, shift)]
        if late is None:
            late = terms
        else:
            here = (group_index ^ shift) == goal
            late = [[jnp.where(here, a, b) for a, b in zip(new, old)] for new, old in zip(terms, late)]

    def my_rows(values):
        return lax.dynamic_slice_in_dim(values, atom_index * rows_dev, rows_dev, 0)

    my_freq = my_rows(panel_freq)
    flag = jnp.stack(
        [
            (group_index == goal).astype(jnp.int32),
            (column_index * part_cols).astype(jnp.int32),
            atom_index.astype(jnp.int32),
        ]
    )
    elements, numerator = finish(
        flag,
        early,
        late,
        win_start.reshape(atom_count, rows_dev),
        win_len.reshape(atom_count, rows_dev),
        panel_freq.reshape(atom_count, rows_dev),
        partner_freq[None, :],
        1.0 / math.sqrt(3 * atom_rows * atom_count),
    )
    holders = groups * 2
    sums = [numerator] + [
        lax.ppermute(numerator, ("modes", "sub"), [(i, i ^ code) for i in range(holders)])
        for code in range(1, holders)
    ]
    while len(sums) > 1:
        sums = [sums[i] + sums[i + 1] for i in range(0, len(sums), 2)]
    diffusivity = math.pi / 3.0 * sums[0][0] / (my_freq * my_freq)
    return (elements, diffusivity)


def solution(mesh):
    return jax.shard_map(
        body,
        mesh=mesh,
        in_specs=(
            P(None, ("dom", "atoms"), ("modes", "sub")),
            P(None, ("dom", "atoms"), ("modes", "sub")),
            P(None, ("dom", "atoms"), None),
            P(("dom", "atoms"), None),
            P(("dom", "atoms")),
            P("dom"),
            P(("dom", "modes", "sub")),
            P("dom"),
            P("dom"),
        ),
        out_specs=(P(("dom", "atoms"), ("modes", "sub")), P(("dom", "atoms"))),
        check_vma=False,
    )
```

```python
import math

import jax
import jax.numpy as jnp
from jax import lax
from jax.experimental import pallas as pl
from jax.experimental.pallas import tpu as pltpu
from jax.sharding import PartitionSpec as P

HALO = 96
BONDS = 16
LANES = 128
SPAN = LANES + 2 * HALO
GROUP = 16
VMEM_BYTES = 14 * 1024 * 1024

lorentz_width = 0.05

EARLY_US = 6.0
LATE_US = 0.1

HBM = pl.BlockSpec(memory_space=pltpu.HBM)
ANY = pl.BlockSpec(memory_space=pl.ANY)
VMEM = pl.BlockSpec(memory_space=pltpu.VMEM)
SMEM = pl.BlockSpec(memory_space=pltpu.SMEM)


def call(kernel, name, in_specs, out_specs, out_shape, operands, busy_us, scratch=()):
    return pl.pallas_call(
        kernel,
        in_specs=in_specs,
        out_specs=out_specs,
        out_shape=out_shape,
        scratch_shapes=list(scratch),
        compiler_params=pltpu.CompilerParams(vmem_limit_bytes=VMEM_BYTES),
        cost_estimate=pl.CostEstimate(
            flops=int(busy_us * 1.1e9), bytes_accessed=int(busy_us * 1e5), transcendentals=0
        ),
        name=name,
    )(*operands)


def runs_of(blocks):
    runs = []
    for place, block in enumerate(blocks):
        if runs and runs[-1][1] + runs[-1][2] == block:
            runs[-1][2] += 1
        else:
            runs.append([place, block, 1])
    return runs


def build_block(first, base, nbr_ref, coef_ref, count_ref, dense_ref):
    lanes = pl.ds(first, LANES)
    target = nbr_ref[:, lanes] - (base + (first - HALO))
    slot_ids = lax.broadcasted_iota(jnp.int32, (BONDS, LANES), 0)
    live = slot_ids < count_ref[lanes].reshape(1, LANES)
    coefs = [jnp.where(live, coef_ref[e, :, lanes], 0.0) for e in range(9)]
    halves = [(target[h : h + 8], slot_ids[h : h + 8]) for h in (0, 8)]
    merged = [[jnp.zeros((8, LANES), jnp.float32) for _ in range(9)] for _ in range(2)]
    named = [jnp.broadcast_to(target[k : k + 1], (8, LANES)) for k in range(BONDS)]
    for k in range(BONDS):
        rows = [jnp.broadcast_to(coefs[e][k : k + 1], (8, LANES)) for e in range(9)]
        for h in range(k // 8, 2):
            same = (halves[h][0] == named[k]) & (halves[h][1] >= k)
            for e in range(9):
                merged[h][e] = merged[h][e] + jnp.where(same, rows[e], 0.0)
    row_ids = lax.broadcasted_iota(jnp.int32, (8, LANES), 0)

    def group_step(g, carry):
        cells = [[] for _ in range(9)]
        for tile in range(GROUP // 8):
            here = row_ids + (g * GROUP + tile * 8)
            slot = jnp.full((8, LANES), -1, jnp.int32)
            for k in range(BONDS):
                slot = jnp.where(named[k] == here, k, slot)
            place = slot & 7
            early, live_cell = slot < 8, slot >= 0
            for e in range(9):
                picks = [
                    jnp.take_along_axis(merged[h][e], place, axis=0, mode="promise_in_bounds")
                    for h in range(2)
                ]
                cells[e].append(jnp.where(live_cell, jnp.where(early, picks[0], picks[1]), 0.0))
        for r in range(3):
            for c in range(3):
                value = jnp.concatenate(cells[3 * r + c], axis=0)
                high = value.astype(jnp.bfloat16)
                low = (value - high.astype(jnp.float32)).astype(jnp.bfloat16)
                at = pl.ds(pl.multiple_of(c * SPAN + g * GROUP, GROUP), GROUP)
                dense_ref[at, 2 * r * LANES : (2 * r + 1) * LANES] = high
                dense_ref[at, (2 * r + 1) * LANES : (2 * r + 2) * LANES] = low
        return carry

    lax.fori_loop(0, SPAN // GROUP, group_step, 0)


def images_of(blocks, spot, panel, nbr, coef, count, halos=(), before=None, edges=False):
    rows, modes = panel.shape[1:]
    loads = before is None
    operands = [nbr, count, coef, panel]
    if loads:
        operands = [pltpu.with_memory_space_constraint(x, pltpu.HBM) for x in operands]
    operands = [spot, *operands, *halos]
    in_specs = [SMEM] + [HBM if loads else VMEM] * 4 + [VMEM] * len(halos)
    if before is not None:
        operands.append(before)
        in_specs.append(ANY)
    width = len(blocks) * LANES
    out_shape = [jax.ShapeDtypeStruct((modes, 3 * width), jnp.bfloat16)]
    out_specs = [VMEM]
    if edges:
        out_shape += [jax.ShapeDtypeStruct((3, HALO, modes), jnp.bfloat16)] * 2
        out_specs += [ANY] * 2
    n_in, n_out = len(operands), len(out_shape)

    def pieces_of(block):
        begin, end = block * LANES - HALO, (block + 1) * LANES + HALO
        found = []
        if begin < 0:
            found.append((1, HALO + begin, 0, -begin))
        low, high = max(begin, 0), min(end, rows)
        found.append((0, low, low - begin, high - low))
        if end > rows:
            found.append((2, 0, rows - begin, end - rows))
        return found

    def kernel(*refs):
        spot_ref, nbr_ref, count_ref, coef_ref, panel_ref = refs[:5]
        odd = spot_ref[1]
        outs = refs[n_in : n_in + n_out]
        window_ref, dense_ref, *scratch_refs = refs[n_in + n_out :]
        window_copies = []
        if loads:
            sources = (nbr_ref, count_ref, coef_ref)
            nbr_ref, count_ref, coef_ref, sems = scratch_refs
            copies = []

            def start(source, target, kept):
                copy = pltpu.make_async_copy(source, target, sems.at[len(copies) + len(window_copies)])
                copy.start()
                kept.append(copy)

            start(sources[0], nbr_ref, copies)
            start(sources[1], count_ref, copies)
            for _, block, length in runs_of(blocks):
                at = pl.ds(block * LANES, length * LANES)
                start(sources[2].at[:, :, at], coef_ref.at[:, :, at], copies)
            for place, block in enumerate(blocks):
                for _, source, at, length in pieces_of(block):
                    start(
                        panel_ref.at[:, pl.ds(source, length)], window_ref.at[place, :, pl.ds(at, length)], window_copies
                    )
            if edges:
                for turn, out in enumerate(outs[1:3]):
                    at = pl.multiple_of(jnp.where(odd == turn, rows - HALO, 0), 32)
                    start(panel_ref.at[:, pl.ds(at, HALO)], out, window_copies)
            for copy in copies:
                copy.wait()
        else:
            for place, block in enumerate(blocks):
                for which, source, at, length in pieces_of(block):
                    there = slice(source, source + length)
                    if which == 0:
                        found = panel_ref[:, there, :]
                    else:
                        found = jnp.where((odd == 1) == (which == 1), refs[5][:, there, :], refs[6][:, there, :])
                    window_ref[place, :, at : at + length, :] = found

        def block_step(place, carry):
            first = (blocks[0] + place * (blocks[1] - blocks[0])) * LANES
            build_block(pl.multiple_of(first, LANES), spot_ref[0], nbr_ref, coef_ref, count_ref, dense_ref)
            if loads:

                @pl.when(place == 0)
                def _():
                    for copy in window_copies:
                        copy.wait()

            both = lax.dot_general(
                window_ref[place].reshape(3 * SPAN, modes),
                dense_ref[...],
                (((0,), (0,)), ((), ())),
                preferred_element_type=jnp.float32,
            )
            for r in range(3):
                image = both[:, 2 * r * LANES : (2 * r + 1) * LANES]
                image = image + both[:, (2 * r + 1) * LANES : (2 * r + 2) * LANES]
                at = pl.multiple_of(r * width + place * LANES, LANES)
                outs[0][:, pl.ds(at, LANES)] = image.astype(jnp.bfloat16)
            return carry

        lax.fori_loop(0, len(blocks), block_step, 0)

    scratch = [
        pltpu.VMEM((len(blocks), 3, SPAN, modes), jnp.bfloat16),
        pltpu.VMEM((3 * SPAN, 6 * LANES), jnp.bfloat16),
    ]
    if loads:
        scratch += [
            pltpu.VMEM((BONDS, rows), jnp.int32),
            pltpu.VMEM((rows,), jnp.int32),
            pltpu.VMEM((9, BONDS, rows), jnp.float32),
            pltpu.SemaphoreType.DMA((4 + 3 * len(blocks) + 2,)),
        ]
    return call(kernel, "images", in_specs, out_specs, out_shape, operands, 0.8 + 1.2 * len(blocks), scratch)


def products_of(chunks, place, partners, mine, theirs, after=(), busy_us=2.0):
    rows, cols = mine[0].shape[0], partners.shape[2]
    count = len(chunks)
    depth = partners.shape[1]

    def kernel(place_ref, partners_ref, *refs):
        keep_ref, send_ref, left_ref = refs[-3:]
        kept = place_ref[0] == place_ref[1]
        for who in range(2):
            at_rows = pl.ds(pl.multiple_of(jnp.where(kept == (who == 0), 0, rows), rows), rows)
            for i, blocks in enumerate(chunks):
                image_ref = refs[who * count + i]
                width = len(blocks) * LANES
                for r in range(3):
                    for spot, block, length in runs_of(blocks):
                        at, to = r * width + spot * LANES, r * depth + block * LANES
                        left_ref[at_rows, to : to + length * LANES] = image_ref[:, at : at + length * LANES]
        total = jnp.dot(
            left_ref[...], partners_ref[...].reshape(3 * depth, cols), preferred_element_type=jnp.float32
        )
        keep_ref[...] = total[:rows]
        send_ref[...] = total[rows:].astype(jnp.bfloat16)

    return call(
        kernel,
        "products",
        [SMEM] + [VMEM] * (1 + 2 * count) + [ANY] * len(after),
        [VMEM, VMEM],
        [jax.ShapeDtypeStruct((rows, cols), jnp.float32), jax.ShapeDtypeStruct((rows, cols), jnp.bfloat16)],
        (place, partners, *mine, *theirs, *after),
        busy_us,
        [pltpu.VMEM((2 * rows, 3 * depth), jnp.bfloat16)],
    )


def all_products(chunks, half, partners, mine, theirs):
    place = jnp.stack([half, jnp.zeros((), jnp.int32)])
    low = products_of(chunks, place, partners, mine, theirs)[0]
    high = products_of(chunks, place + jnp.array([0, 1], jnp.int32), partners, mine, theirs)[0]
    return jnp.stack([low, high])


def settle(cells, bit, rows_dev):
    depth = lax.axis_size("atoms")
    place = lax.axis_index("atoms")
    while cells.shape[0] > 1:
        pairs = cells.reshape(cells.shape[0] // 2, 2, rows_dev, -1)
        own = (place >> bit) & 1
        keep = lax.dynamic_index_in_dim(pairs, own, 1, keepdims=False)
        send = lax.dynamic_index_in_dim(pairs, 1 - own, 1, keepdims=False)
        step = 1 << bit
        got = lax.ppermute(send.astype(jnp.bfloat16), "atoms", [(z, z ^ step) for z in range(depth)])
        cells = keep + got.astype(jnp.float32)
        bit += 1
    return cells[0], bit


def collected(terms, bit, shift):
    groups, depth = lax.axis_size("modes"), lax.axis_size("atoms")
    level = 0
    while (1 << level) < groups:
        moves = []
        for z in range(depth):
            for m in range(groups):
                goal = m ^ shift
                settled = all(((z >> (bit + u)) ^ (goal >> u)) & 1 == 0 for u in range(level))
                if settled and ((z >> (bit + level)) ^ (goal >> level)) & 1:
                    moves.append((z * groups + m, (z ^ (1 << (bit + level))) * groups + m))
        sent = sum(term.astype(jnp.float32) for term in terms).astype(jnp.bfloat16)
        terms = terms + [lax.ppermute(sent, ("atoms", "modes"), moves)]
        level += 1
    return terms


def finish(flag, early, late, starts, lengths, freqs, partner_freq, norm_scale):
    rows, cols = early[0].shape
    n_early = len(early)
    operands = [flag, starts, lengths, freqs, partner_freq, *early, *late]
    step = 16

    def kernel(flag_ref, starts_ref, lengths_ref, freqs_ref, partner_ref, *refs):
        out_ref, sum_ref, start_ref, end_ref, freq_ref, folded_ref = refs[-6:]
        def sums(some):
            total = some[0][...]
            for ref in some[1:]:
                total = total + ref[...].astype(jnp.float32)
            return total

        @pl.when(flag_ref[0] == 1)
        def _():
            out_ref[...] = sums(refs[:n_early])

        @pl.when(flag_ref[0] == 0)
        def _():
            out_ref[...] = sums(refs[n_early:-6])

        def turned(row):
            return jnp.broadcast_to(row, (LANES, rows)).T

        mine = pl.ds(flag_ref[2], 1)
        start_row = starts_ref[mine, :].astype(jnp.float32)
        start_ref[...] = turned(start_row)
        end_ref[...] = turned(start_row + lengths_ref[mine, :].astype(jnp.float32))
        freq_ref[...] = turned(freqs_ref[mine, :])
        lane_ids = lax.broadcasted_iota(jnp.int32, (step, LANES), 1)

        def row_step(i, carry):
            at_rows = pl.ds(pl.multiple_of(i * step, step), step)
            start, end, freq = start_ref[at_rows, :], end_ref[at_rows, :], freq_ref[at_rows, :]
            folded = jnp.zeros((step, LANES), jnp.float32)
            for at in range(0, cols, LANES):
                columns = (lane_ids + (flag_ref[1] + at)).astype(jnp.float32)
                inside = (columns >= start) & (columns < end)
                elements = jnp.where(inside, out_ref[at_rows, at : at + LANES] * norm_scale, 0.0)
                out_ref[at_rows, at : at + LANES] = elements
                offset = freq - partner_ref[:, at : at + LANES]
                lorentz = lorentz_width / (math.pi * (offset * offset + lorentz_width * lorentz_width))
                folded = folded + jnp.where(inside, lorentz, 0.0) * elements * elements
            folded_ref[at_rows, :] = folded
            return carry

        lax.fori_loop(0, rows // step, row_step, 0)
        sum_ref[...] = jnp.sum(folded_ref[...].T, axis=0, keepdims=True)

    return call(
        kernel,
        "finish",
        [SMEM] + [VMEM] * (len(operands) - 1),
        [VMEM, VMEM],
        [jax.ShapeDtypeStruct((rows, cols), jnp.float32), jax.ShapeDtypeStruct((1, rows), jnp.float32)],
        operands,
        2.0,
        [pltpu.VMEM((rows, LANES), jnp.float32)] * 4,
    )


def body(
    mode_panel,
    partners,
    bond_blocks,
    neighbors,
    bond_count,
    panel_freq,
    partner_freq,
    win_start,
    win_len,
):
    atom_rows, modes = mode_panel.shape[1:]
    atom_index = lax.axis_index("atoms")
    atom_count = lax.axis_size("atoms")
    groups = lax.axis_size("modes")
    group_index = lax.axis_index("modes")
    half_index = lax.axis_index("sub")
    column_index = lax.axis_index(("modes", "sub"))
    part_cols = partners.shape[2]
    panel_total = win_start.shape[0]
    rows_dev = panel_total // atom_count

    nbr = neighbors.T
    coef = bond_blocks.transpose(0, 2, 1)
    spot = jnp.stack([(atom_index * atom_rows).astype(jnp.int32), (atom_index & 1).astype(jnp.int32)])

    last = atom_rows // LANES - 1
    middle = list(range(1, last))
    cut = len(middle) // 2
    chunks = [middle[:cut], middle[cut:], [last, 0]]
    shared = (spot, mode_panel, nbr, coef, bond_count)
    near, edge_one, edge_two = images_of(chunks[0], *shared, edges=True)
    pairs = [(z, z ^ 1) for z in range(atom_count)]
    others = [(z, ((z + 1) ^ 1) - 1) for z in range(1, atom_count - 1)]
    halos = (lax.ppermute(edge_one, "atoms", pairs), lax.ppermute(edge_two, "atoms", others))
    middle_images = images_of(chunks[1], *shared, before=near)[0]
    mine = [near, middle_images, images_of(chunks[2], *shared, halos=halos, before=middle_images)[0]]

    def from_group(cells, shift):
        return lax.ppermute(cells, "modes", [(m ^ shift, m) for m in range(groups)])

    def from_sibling(cells):
        return lax.ppermute(cells, "sub", [(0, 1), (1, 0)])

    theirs = [from_sibling(cells) for cells in mine]
    far_all = {shift: [from_group(cells, shift) for cells in mine] for shift in range(1, groups)}
    half = half_index.astype(jnp.int32)
    goal = atom_index * groups // atom_count

    if rows_dev == modes and groups == 2:
        place = jnp.stack([half, (atom_index & 1).astype(jnp.int32)])

        def next_door(some_mine, some_theirs, after=()):
            keep, send = products_of(
                chunks, place, partners, some_mine, some_theirs, after, EARLY_US if after else LATE_US
            )
            return keep, lax.ppermute(send, "atoms", pairs)

        far = far_all[1]
        early = next_door(mine, theirs, far[:1])
        second, kept = lax.optimization_barrier((far[1], early[0]))
        third, kept = lax.optimization_barrier((far[2], kept))
        early = (kept, early[1])
        far = [far[0], second, third]
        late = next_door(far, [from_sibling(cells) for cells in far])
        sent = jnp.where(
            group_index == goal,
            late[0] + late[1].astype(jnp.float32),
            early[0] + early[1].astype(jnp.float32),
        ).astype(jnp.bfloat16)
        swapped = lax.ppermute(sent, "atoms", [(z, z ^ 2) for z in range(atom_count)])
        early, late = [*early, swapped], [*late, swapped]
    else:

        def settled(some_mine, some_theirs, shift):
            cells = all_products(chunks, half, partners, some_mine, some_theirs)
            cells, bit = settle(cells.reshape(-1, rows_dev, part_cols), 0, rows_dev)
            return collected([cells], bit, shift)

        early, late = settled(mine, theirs, 0), None
        for shift, far in far_all.items():
            terms = settled(far, [from_sibling(cells) for cells in far], shift)
            if late is None:
                late = terms
            else:
                here = (group_index ^ shift) == goal
                late = [jnp.where(here, new, old) for new, old in zip(terms, late)]

    my_freq = lax.dynamic_slice_in_dim(panel_freq, atom_index * rows_dev, rows_dev, 0)
    flag = jnp.stack(
        [
            (group_index == goal).astype(jnp.int32),
            (column_index * part_cols).astype(jnp.int32),
            atom_index.astype(jnp.int32),
        ]
    )
    elements, numerator = finish(
        flag,
        early,
        late,
        win_start.reshape(atom_count, rows_dev),
        win_len.reshape(atom_count, rows_dev),
        panel_freq.reshape(atom_count, rows_dev),
        partner_freq[None, :],
        1.0 / math.sqrt(3 * atom_rows * atom_count),
    )
    holders = groups * 2
    sums = [numerator] + [
        lax.ppermute(numerator, ("modes", "sub"), [(i, i ^ code) for i in range(holders)])
        for code in range(1, holders)
    ]
    while len(sums) > 1:
        sums = [sums[i] + sums[i + 1] for i in range(0, len(sums), 2)]
    diffusivity = math.pi / 3.0 * sums[0][0] / (my_freq * my_freq)
    return (elements, diffusivity)


def solution(mesh):
    return jax.shard_map(
        body,
        mesh=mesh,
        in_specs=(
            P(None, ("dom", "atoms"), ("modes", "sub")),
            P(None, ("dom", "atoms"), ("modes", "sub")),
            P(None, ("dom", "atoms"), None),
            P(("dom", "atoms"), None),
            P(("dom", "atoms")),
            P("dom"),
            P(("dom", "modes", "sub")),
            P("dom"),
            P("dom"),
        ),
        out_specs=(P(("dom", "atoms"), ("modes", "sub")), P(("dom", "atoms"))),
        check_vma=False,
    )
```

```python
import math

import jax
import jax.numpy as jnp
from jax import lax
from jax.experimental import pallas as pl
from jax.experimental.pallas import tpu as pltpu
from jax.sharding import PartitionSpec as P

HALO = 96
BONDS = 16
LANES = 128
SPAN = LANES + 2 * HALO
GROUP = 32
VMEM_BYTES = 14 * 1024 * 1024

lorentz_width = 0.05

EARLY_US = 6.0
LATE_US = 0.1

HBM = pl.BlockSpec(memory_space=pltpu.HBM)
ANY = pl.BlockSpec(memory_space=pl.ANY)
VMEM = pl.BlockSpec(memory_space=pltpu.VMEM)
SMEM = pl.BlockSpec(memory_space=pltpu.SMEM)


def call(kernel, name, in_specs, out_specs, out_shape, operands, busy_us, scratch=()):
    return pl.pallas_call(
        kernel,
        in_specs=in_specs,
        out_specs=out_specs,
        out_shape=out_shape,
        scratch_shapes=list(scratch),
        compiler_params=pltpu.CompilerParams(vmem_limit_bytes=VMEM_BYTES),
        cost_estimate=pl.CostEstimate(
            flops=int(busy_us * 1.1e9), bytes_accessed=int(busy_us * 1e5), transcendentals=0
        ),
        name=name,
    )(*operands)


def runs_of(blocks):
    runs = []
    for place, block in enumerate(blocks):
        if runs and runs[-1][1] + runs[-1][2] == block:
            runs[-1][2] += 1
        else:
            runs.append([place, block, 1])
    return runs


def build_block(first, base, nbr_ref, coef_ref, count_ref, dense_ref):
    lanes = pl.ds(first, LANES)
    target = nbr_ref[:, lanes] - (base + (first - HALO))
    slot_ids = lax.broadcasted_iota(jnp.int32, (BONDS, LANES), 0)
    live = slot_ids < count_ref[lanes].reshape(1, LANES)
    coefs = [jnp.where(live, coef_ref[e, :, lanes], 0.0) for e in range(9)]
    halves = [(target[h : h + 8], slot_ids[h : h + 8]) for h in (0, 8)]
    merged = [[jnp.zeros((8, LANES), jnp.float32) for _ in range(9)] for _ in range(2)]
    named = [jnp.broadcast_to(target[k : k + 1], (8, LANES)) for k in range(BONDS)]
    for k in range(BONDS):
        rows = [jnp.broadcast_to(coefs[e][k : k + 1], (8, LANES)) for e in range(9)]
        for h in range(k // 8, 2):
            same = (halves[h][0] == named[k]) & (halves[h][1] >= k)
            for e in range(9):
                merged[h][e] = merged[h][e] + jnp.where(same, rows[e], 0.0)
    row_ids = lax.broadcasted_iota(jnp.int32, (8, LANES), 0)

    def group_step(g, carry):
        cells = [[] for _ in range(9)]
        for tile in range(GROUP // 8):
            here = row_ids + (g * GROUP + tile * 8)
            slot = jnp.full((8, LANES), -1, jnp.int32)
            for k in range(BONDS):
                slot = jnp.where(named[k] == here, k, slot)
            place = slot & 7
            early, live_cell = slot < 8, slot >= 0
            for e in range(9):
                picks = [
                    jnp.take_along_axis(merged[h][e], place, axis=0, mode="promise_in_bounds")
                    for h in range(2)
                ]
                cells[e].append(jnp.where(live_cell, jnp.where(early, picks[0], picks[1]), 0.0))
        for r in range(3):
            for c in range(3):
                value = jnp.concatenate(cells[3 * r + c], axis=0)
                high = value.astype(jnp.bfloat16)
                low = (value - high.astype(jnp.float32)).astype(jnp.bfloat16)
                at = pl.ds(pl.multiple_of(c * SPAN + g * GROUP, GROUP), GROUP)
                dense_ref[at, 2 * r * LANES : (2 * r + 1) * LANES] = high
                dense_ref[at, (2 * r + 1) * LANES : (2 * r + 2) * LANES] = low
        return carry

    lax.fori_loop(0, SPAN // GROUP, group_step, 0)


def images_of(blocks, spot, panel, nbr, coef, count, halos=(), before=(), edges=False):
    rows, modes = panel.shape[1:]
    loads = len(before) == 0
    operands = [nbr, count, coef, panel]
    if loads:
        operands = [pltpu.with_memory_space_constraint(x, pltpu.HBM) for x in operands]
    operands = [spot, *operands, *halos, *before]
    in_specs = [SMEM] + [HBM if loads else VMEM] * 4 + [VMEM] * len(halos) + [ANY] * len(before)
    width = len(blocks) * LANES
    out_shape = [pltpu.VMEM((modes, 3 * width), jnp.bfloat16)]
    out_specs = [VMEM]
    if edges:
        out_shape += [jax.ShapeDtypeStruct((3, HALO, modes), jnp.bfloat16)] * 2
        out_specs += [ANY] * 2
    n_in, n_out = len(operands), len(out_shape)

    def pieces_of(block):
        begin, end = block * LANES - HALO, (block + 1) * LANES + HALO
        found = []
        if begin < 0:
            found.append((1, HALO + begin, 0, -begin))
        low, high = max(begin, 0), min(end, rows)
        found.append((0, low, low - begin, high - low))
        if end > rows:
            found.append((2, 0, rows - begin, end - rows))
        return found

    def kernel(*refs):
        spot_ref, nbr_ref, count_ref, coef_ref, panel_ref = refs[:5]
        odd = spot_ref[1]
        outs = refs[n_in : n_in + n_out]
        window_ref, dense_ref, *scratch_refs = refs[n_in + n_out :]
        window_copies = []
        if loads:
            sources = (nbr_ref, count_ref, coef_ref)
            nbr_ref, count_ref, coef_ref, sems = scratch_refs
            copies = []

            def start(source, target, kept):
                copy = pltpu.make_async_copy(source, target, sems.at[len(copies) + len(window_copies)])
                copy.start()
                kept.append(copy)

            start(sources[0], nbr_ref, copies)
            start(sources[1], count_ref, copies)
            for _, block, length in runs_of(blocks):
                at = pl.ds(block * LANES, length * LANES)
                start(sources[2].at[:, :, at], coef_ref.at[:, :, at], copies)
            for place, block in enumerate(blocks):
                for _, source, at, length in pieces_of(block):
                    start(
                        panel_ref.at[:, pl.ds(source, length)], window_ref.at[place, :, pl.ds(at, length)], window_copies
                    )
            if edges:
                for turn, out in enumerate(outs[1:3]):
                    at = pl.multiple_of(jnp.where(odd == turn, rows - HALO, 0), 32)
                    start(panel_ref.at[:, pl.ds(at, HALO)], out, window_copies)
            for copy in copies:
                copy.wait()
        else:
            for place, block in enumerate(blocks):
                for which, source, at, length in pieces_of(block):
                    there = slice(source, source + length)
                    if which == 0:
                        found = panel_ref[:, there, :]
                    else:
                        found = jnp.where((odd == 1) == (which == 1), refs[5][:, there, :], refs[6][:, there, :])
                    window_ref[place, :, at : at + length, :] = found

        for place, block in enumerate(blocks):
            build_block(block * LANES, spot_ref[0], nbr_ref, coef_ref, count_ref, dense_ref)
            if loads and place == 0:
                for copy in window_copies:
                    copy.wait()
            both = lax.dot_general(
                window_ref[place].reshape(3 * SPAN, modes),
                dense_ref[...],
                (((0,), (0,)), ((), ())),
                preferred_element_type=jnp.float32,
            )
            for r in range(3):
                image = both[:, 2 * r * LANES : (2 * r + 1) * LANES]
                image = image + both[:, (2 * r + 1) * LANES : (2 * r + 2) * LANES]
                at = r * width + place * LANES
                outs[0][:, at : at + LANES] = image.astype(jnp.bfloat16)

    scratch = [
        pltpu.VMEM((len(blocks), 3, SPAN, modes), jnp.bfloat16),
        pltpu.VMEM((3 * SPAN, 6 * LANES), jnp.bfloat16),
    ]
    if loads:
        scratch += [
            pltpu.VMEM((BONDS, rows), jnp.int32),
            pltpu.VMEM((rows,), jnp.int32),
            pltpu.VMEM((9, BONDS, rows), jnp.float32),
            pltpu.SemaphoreType.DMA((4 + 3 * len(blocks) + 2,)),
        ]
    return call(kernel, "images", in_specs, out_specs, out_shape, operands, 0.8 + 1.2 * len(blocks), scratch)


def products_of(chunks, place, partners, mine, theirs, after=(), busy_us=2.0):
    rows, cols = mine[0].shape[0], partners.shape[2]
    count = len(chunks)
    depth = partners.shape[1]

    def kernel(place_ref, partners_ref, *refs):
        keep_ref, send_ref, left_ref = refs[-3:]
        kept = place_ref[0] == place_ref[1]
        for who in range(2):
            at_rows = pl.ds(pl.multiple_of(jnp.where(kept == (who == 0), 0, rows), rows), rows)
            for i, blocks in enumerate(chunks):
                image_ref = refs[who * count + i]
                width = len(blocks) * LANES
                for r in range(3):
                    for spot, block, length in runs_of(blocks):
                        at, to = r * width + spot * LANES, r * depth + block * LANES
                        left_ref[at_rows, to : to + length * LANES] = image_ref[:, at : at + length * LANES]
        total = jnp.dot(
            left_ref[...], partners_ref[...].reshape(3 * depth, cols), preferred_element_type=jnp.float32
        )
        keep_ref[...] = total[:rows]
        send_ref[...] = total[rows:].astype(jnp.bfloat16)

    return call(
        kernel,
        "products",
        [SMEM] + [VMEM] * (1 + 2 * count) + [ANY] * len(after),
        [VMEM, VMEM],
        [pltpu.VMEM((rows, cols), jnp.float32), pltpu.VMEM((rows, cols), jnp.bfloat16)],
        (place, partners, *mine, *theirs, *after),
        busy_us,
        [pltpu.VMEM((2 * rows, 3 * depth), jnp.bfloat16)],
    )


def all_products(chunks, half, partners, mine, theirs):
    place = jnp.stack([half, jnp.zeros((), jnp.int32)])
    low = products_of(chunks, place, partners, mine, theirs)[0]
    high = products_of(chunks, place + jnp.array([0, 1], jnp.int32), partners, mine, theirs)[0]
    return jnp.stack([low, high])


def settle(cells, bit, rows_dev):
    depth = lax.axis_size("atoms")
    place = lax.axis_index("atoms")
    while cells.shape[0] > 1:
        pairs = cells.reshape(cells.shape[0] // 2, 2, rows_dev, -1)
        own = (place >> bit) & 1
        keep = lax.dynamic_index_in_dim(pairs, own, 1, keepdims=False)
        send = lax.dynamic_index_in_dim(pairs, 1 - own, 1, keepdims=False)
        step = 1 << bit
        got = lax.ppermute(send.astype(jnp.bfloat16), "atoms", [(z, z ^ step) for z in range(depth)])
        cells = keep + got.astype(jnp.float32)
        bit += 1
    return cells[0], bit


def collected(terms, bit, shift):
    groups, depth = lax.axis_size("modes"), lax.axis_size("atoms")
    level = 0
    while (1 << level) < groups:
        moves = []
        for z in range(depth):
            for m in range(groups):
                goal = m ^ shift
                settled = all(((z >> (bit + u)) ^ (goal >> u)) & 1 == 0 for u in range(level))
                if settled and ((z >> (bit + level)) ^ (goal >> level)) & 1:
                    moves.append((z * groups + m, (z ^ (1 << (bit + level))) * groups + m))
        sent = sum(term.astype(jnp.float32) for term in terms).astype(jnp.bfloat16)
        terms = terms + [lax.ppermute(sent, ("atoms", "modes"), moves)]
        level += 1
    return terms


def finish(flag, early, late, starts, lengths, freqs, partner_freq, norm_scale):
    rows, cols = early[0].shape
    n_early = len(early)
    operands = [flag, starts, lengths, freqs, partner_freq, *early, *late]
    step = 16

    def kernel(flag_ref, starts_ref, lengths_ref, freqs_ref, partner_ref, *refs):
        out_ref, sum_ref, start_ref, end_ref, freq_ref, folded_ref = refs[-6:]
        def sums(some):
            total = some[0][...]
            for ref in some[1:]:
                total = total + ref[...].astype(jnp.float32)
            return total

        @pl.when(flag_ref[0] == 1)
        def _():
            out_ref[...] = sums(refs[:n_early])

        @pl.when(flag_ref[0] == 0)
        def _():
            out_ref[...] = sums(refs[n_early:-6])

        def turned(row):
            return jnp.broadcast_to(row, (LANES, rows)).T

        mine = pl.ds(flag_ref[2], 1)
        start_row = starts_ref[mine, :].astype(jnp.float32)
        start_ref[...] = turned(start_row)
        end_ref[...] = turned(start_row + lengths_ref[mine, :].astype(jnp.float32))
        freq_ref[...] = turned(freqs_ref[mine, :])
        lane_ids = lax.broadcasted_iota(jnp.int32, (step, LANES), 1)

        def row_step(i, carry):
            at_rows = pl.ds(pl.multiple_of(i * step, step), step)
            start, end, freq = start_ref[at_rows, :], end_ref[at_rows, :], freq_ref[at_rows, :]
            folded = jnp.zeros((step, LANES), jnp.float32)
            for at in range(0, cols, LANES):
                columns = (lane_ids + (flag_ref[1] + at)).astype(jnp.float32)
                inside = (columns >= start) & (columns < end)
                elements = jnp.where(inside, out_ref[at_rows, at : at + LANES] * norm_scale, 0.0)
                out_ref[at_rows, at : at + LANES] = elements
                offset = freq - partner_ref[:, at : at + LANES]
                lorentz = lorentz_width / (math.pi * (offset * offset + lorentz_width * lorentz_width))
                folded = folded + jnp.where(inside, lorentz, 0.0) * elements * elements
            folded_ref[at_rows, :] = folded
            return carry

        lax.fori_loop(0, rows // step, row_step, 0)
        sum_ref[...] = jnp.sum(folded_ref[...].T, axis=0, keepdims=True)

    return call(
        kernel,
        "finish",
        [SMEM] + [VMEM] * (len(operands) - 1),
        [VMEM, VMEM],
        [jax.ShapeDtypeStruct((rows, cols), jnp.float32), jax.ShapeDtypeStruct((1, rows), jnp.float32)],
        operands,
        2.0,
        [pltpu.VMEM((rows, LANES), jnp.float32)] * 4,
    )


def body(
    mode_panel,
    partners,
    bond_blocks,
    neighbors,
    bond_count,
    panel_freq,
    partner_freq,
    win_start,
    win_len,
):
    atom_rows, modes = mode_panel.shape[1:]
    atom_index = lax.axis_index("atoms")
    atom_count = lax.axis_size("atoms")
    groups = lax.axis_size("modes")
    group_index = lax.axis_index("modes")
    half_index = lax.axis_index("sub")
    column_index = lax.axis_index(("modes", "sub"))
    part_cols = partners.shape[2]
    panel_total = win_start.shape[0]
    rows_dev = panel_total // atom_count

    nbr = neighbors.T
    coef = bond_blocks.transpose(0, 2, 1)
    spot = jnp.stack([(atom_index * atom_rows).astype(jnp.int32), (atom_index & 1).astype(jnp.int32)])

    last = atom_rows // LANES - 1
    middle = list(range(1, last))
    cut = len(middle) // 2
    chunks = [middle[:cut], middle[cut:], [last, 0]]
    shared = (spot, mode_panel, nbr, coef, bond_count)
    near, edge_one, edge_two = images_of(chunks[0], *shared, edges=True)
    pairs = [(z, z ^ 1) for z in range(atom_count)]
    others = [(z, ((z + 1) ^ 1) - 1) for z in range(1, atom_count - 1)]
    halos = (lax.ppermute(edge_one, "atoms", pairs), lax.ppermute(edge_two, "atoms", others))

    def from_group(cells, shift):
        return lax.ppermute(cells, "modes", [(m ^ shift, m) for m in range(groups)])

    def from_sibling(cells):
        return lax.ppermute(cells, "sub", [(0, 1), (1, 0)])

    far_all = {shift: [from_group(near, shift)] for shift in range(1, groups)}
    middle_images = images_of(chunks[1], *shared, before=[near])[0]
    before = [middle_images, *[far[0] for far in far_all.values()]]
    mine = [near, middle_images, images_of(chunks[2], *shared, halos=halos, before=before)[0]]
    for shift, far in far_all.items():
        far += [from_group(cells, shift) for cells in mine[1:]]
    theirs = [from_sibling(cells) for cells in mine]
    half = half_index.astype(jnp.int32)
    goal = atom_index * groups // atom_count

    if rows_dev == modes and groups == 2:
        place = jnp.stack([half, (atom_index & 1).astype(jnp.int32)])

        def next_door(some_mine, some_theirs, after=()):
            keep, send = products_of(
                chunks, place, partners, some_mine, some_theirs, after, EARLY_US if after else LATE_US
            )
            return keep, lax.ppermute(send, "atoms", pairs)

        far = far_all[1]
        early = next_door(mine, theirs, far[:2])
        third, kept = lax.optimization_barrier((far[2], early[0]))
        early = (kept, early[1])
        far = [far[0], far[1], third]
        late = next_door(far, [from_sibling(cells) for cells in far])
        sent = jnp.where(
            group_index == goal,
            late[0] + late[1].astype(jnp.float32),
            early[0] + early[1].astype(jnp.float32),
        ).astype(jnp.bfloat16)
        swapped = lax.ppermute(sent, "atoms", [(z, z ^ 2) for z in range(atom_count)])
        early, late = [*early, swapped], [*late, swapped]
    else:

        def settled(some_mine, some_theirs, shift):
            cells = all_products(chunks, half, partners, some_mine, some_theirs)
            cells, bit = settle(cells.reshape(-1, rows_dev, part_cols), 0, rows_dev)
            return collected([cells], bit, shift)

        early, late = settled(mine, theirs, 0), None
        for shift, far in far_all.items():
            terms = settled(far, [from_sibling(cells) for cells in far], shift)
            if late is None:
                late = terms
            else:
                here = (group_index ^ shift) == goal
                late = [jnp.where(here, new, old) for new, old in zip(terms, late)]

    my_freq = lax.dynamic_slice_in_dim(panel_freq, atom_index * rows_dev, rows_dev, 0)
    flag = jnp.stack(
        [
            (group_index == goal).astype(jnp.int32),
            (column_index * part_cols).astype(jnp.int32),
            atom_index.astype(jnp.int32),
        ]
    )
    elements, numerator = finish(
        flag,
        early,
        late,
        win_start.reshape(atom_count, rows_dev),
        win_len.reshape(atom_count, rows_dev),
        panel_freq.reshape(atom_count, rows_dev),
        partner_freq[None, :],
        1.0 / math.sqrt(3 * atom_rows * atom_count),
    )
    holders = groups * 2
    sums = [numerator] + [
        lax.ppermute(numerator, ("modes", "sub"), [(i, i ^ code) for i in range(holders)])
        for code in range(1, holders)
    ]
    while len(sums) > 1:
        sums = [sums[i] + sums[i + 1] for i in range(0, len(sums), 2)]
    diffusivity = math.pi / 3.0 * sums[0][0] / (my_freq * my_freq)
    return (elements, diffusivity)


def solution(mesh):
    return jax.shard_map(
        body,
        mesh=mesh,
        in_specs=(
            P(None, ("dom", "atoms"), ("modes", "sub")),
            P(None, ("dom", "atoms"), ("modes", "sub")),
            P(None, ("dom", "atoms"), None),
            P(("dom", "atoms"), None),
            P(("dom", "atoms")),
            P("dom"),
            P(("dom", "modes", "sub")),
            P("dom"),
            P("dom"),
        ),
        out_specs=(P(("dom", "atoms"), ("modes", "sub")), P(("dom", "atoms"))),
        check_vma=False,
    )
```

```python
import math

import jax
import jax.numpy as jnp
from jax import lax
from jax.experimental import pallas as pl
from jax.experimental.pallas import tpu as pltpu
from jax.sharding import PartitionSpec as P

HALO = 96
BONDS = 16
LANES = 128
SPAN = LANES + 2 * HALO
GROUP = 16
VMEM_BYTES = 14 * 1024 * 1024

lorentz_width = 0.05

EARLY_US = 6.0
LATE_US = 0.1

HBM = pl.BlockSpec(memory_space=pltpu.HBM)
ANY = pl.BlockSpec(memory_space=pl.ANY)
VMEM = pl.BlockSpec(memory_space=pltpu.VMEM)
SMEM = pl.BlockSpec(memory_space=pltpu.SMEM)


def call(kernel, name, in_specs, out_specs, out_shape, operands, busy_us, scratch=()):
    operands = [
        pltpu.with_memory_space_constraint(x, spec.memory_space) if spec is VMEM or spec is HBM else x
        for spec, x in zip(in_specs, operands)
    ]
    return pl.pallas_call(
        kernel,
        in_specs=in_specs,
        out_specs=out_specs,
        out_shape=out_shape,
        scratch_shapes=list(scratch),
        compiler_params=pltpu.CompilerParams(vmem_limit_bytes=VMEM_BYTES),
        cost_estimate=pl.CostEstimate(
            flops=int(busy_us * 1.1e9), bytes_accessed=int(busy_us * 1e5), transcendentals=0
        ),
        name=name,
    )(*operands)


def runs_of(blocks):
    runs = []
    for place, block in enumerate(blocks):
        if runs and runs[-1][1] + runs[-1][2] == block:
            runs[-1][2] += 1
        else:
            runs.append([place, block, 1])
    return runs


def build_block(first, base, nbr_ref, coef_ref, count_ref, dense_ref):
    lanes = pl.ds(first, LANES)
    target = nbr_ref[:, lanes] - (base + (first - HALO))
    slot_ids = lax.broadcasted_iota(jnp.int32, (BONDS, LANES), 0)
    live = slot_ids < count_ref[lanes].reshape(1, LANES)
    coefs = [jnp.where(live, coef_ref[e, :, lanes], 0.0) for e in range(9)]
    halves = [(target[h : h + 8], slot_ids[h : h + 8]) for h in (0, 8)]
    merged = [[jnp.zeros((8, LANES), jnp.float32) for _ in range(9)] for _ in range(2)]
    named = [jnp.broadcast_to(target[k : k + 1], (8, LANES)) for k in range(BONDS)]
    for k in range(BONDS):
        rows = [jnp.broadcast_to(coefs[e][k : k + 1], (8, LANES)) for e in range(9)]
        for h in range(k // 8, 2):
            same = (halves[h][0] == named[k]) & (halves[h][1] >= k)
            for e in range(9):
                merged[h][e] = merged[h][e] + jnp.where(same, rows[e], 0.0)
    row_ids = lax.broadcasted_iota(jnp.int32, (8, LANES), 0)

    def group_step(g, carry):
        cells = [[] for _ in range(9)]
        for tile in range(GROUP // 8):
            here = row_ids + (g * GROUP + tile * 8)
            slot = jnp.full((8, LANES), -1, jnp.int32)
            for k in range(BONDS):
                slot = jnp.where(named[k] == here, k, slot)
            place = slot & 7
            early, live_cell = slot < 8, slot >= 0
            for e in range(9):
                picks = [
                    jnp.take_along_axis(merged[h][e], place, axis=0, mode="promise_in_bounds")
                    for h in range(2)
                ]
                cells[e].append(jnp.where(live_cell, jnp.where(early, picks[0], picks[1]), 0.0))
        for r in range(3):
            for c in range(3):
                value = jnp.concatenate(cells[3 * r + c], axis=0)
                high = value.astype(jnp.bfloat16)
                low = (value - high.astype(jnp.float32)).astype(jnp.bfloat16)
                at = pl.ds(pl.multiple_of(c * SPAN + g * GROUP, GROUP), GROUP)
                dense_ref[at, 2 * r * LANES : (2 * r + 1) * LANES] = high
                dense_ref[at, (2 * r + 1) * LANES : (2 * r + 2) * LANES] = low
        return carry

    lax.fori_loop(0, SPAN // GROUP, group_step, 0)


def images_of(blocks, spot, panel, nbr, coef, count, halos=(), before=(), edges=False):
    rows, modes = panel.shape[1:]
    loads = len(before) == 0
    operands = [spot, nbr, count, coef, panel, *halos, *before]
    in_specs = [SMEM] + [HBM if loads else VMEM] * 4 + [VMEM] * len(halos) + [ANY] * len(before)
    width = len(blocks) * LANES
    out_shape = [pltpu.VMEM((modes, 3 * width), jnp.bfloat16)]
    out_specs = [VMEM]
    if edges:
        out_shape += [jax.ShapeDtypeStruct((3, HALO, modes), jnp.bfloat16)] * 2
        out_specs += [ANY] * 2
    n_in, n_out = len(operands), len(out_shape)

    def pieces_of(block):
        begin, end = block * LANES - HALO, (block + 1) * LANES + HALO
        found = []
        if begin < 0:
            found.append((1, HALO + begin, 0, -begin))
        low, high = max(begin, 0), min(end, rows)
        found.append((0, low, low - begin, high - low))
        if end > rows:
            found.append((2, 0, rows - begin, end - rows))
        return found

    def kernel(*refs):
        spot_ref, nbr_ref, count_ref, coef_ref, panel_ref = refs[:5]
        odd = spot_ref[1]
        outs = refs[n_in : n_in + n_out]
        window_ref, dense_ref, *scratch_refs = refs[n_in + n_out :]
        window_copies = []
        if loads:
            sources = (nbr_ref, count_ref, coef_ref)
            nbr_ref, count_ref, coef_ref, sems = scratch_refs
            copies = []

            def start(source, target, kept):
                copy = pltpu.make_async_copy(source, target, sems.at[len(copies) + len(window_copies)])
                copy.start()
                kept.append(copy)

            start(sources[0], nbr_ref, copies)
            start(sources[1], count_ref, copies)
            for _, block, length in runs_of(blocks):
                at = pl.ds(block * LANES, length * LANES)
                start(sources[2].at[:, :, at], coef_ref.at[:, :, at], copies)
            for place, block in enumerate(blocks):
                for _, source, at, length in pieces_of(block):
                    start(
                        panel_ref.at[:, pl.ds(source, length)], window_ref.at[place, :, pl.ds(at, length)], window_copies
                    )
            if edges:
                for turn, out in enumerate(outs[1:3]):
                    at = pl.multiple_of(jnp.where(odd == turn, rows - HALO, 0), 32)
                    start(panel_ref.at[:, pl.ds(at, HALO)], out, window_copies)
            for copy in copies:
                copy.wait()
        else:
            for place, block in enumerate(blocks):
                for which, source, at, length in pieces_of(block):
                    there = slice(source, source + length)
                    if which == 0:
                        found = panel_ref[:, there, :]
                    else:
                        found = jnp.where((odd == 1) == (which == 1), refs[5][:, there, :], refs[6][:, there, :])
                    window_ref[place, :, at : at + length, :] = found

        for place, block in enumerate(blocks):
            build_block(block * LANES, spot_ref[0], nbr_ref, coef_ref, count_ref, dense_ref)
            if loads and place == 0:
                for copy in window_copies:
                    copy.wait()
            both = lax.dot_general(
                window_ref[place].reshape(3 * SPAN, modes),
                dense_ref[...],
                (((0,), (0,)), ((), ())),
                preferred_element_type=jnp.float32,
            )
            for r in range(3):
                image = both[:, 2 * r * LANES : (2 * r + 1) * LANES]
                image = image + both[:, (2 * r + 1) * LANES : (2 * r + 2) * LANES]
                at = r * width + place * LANES
                outs[0][:, at : at + LANES] = image.astype(jnp.bfloat16)

    scratch = [
        pltpu.VMEM((len(blocks), 3, SPAN, modes), jnp.bfloat16),
        pltpu.VMEM((3 * SPAN, 6 * LANES), jnp.bfloat16),
    ]
    if loads:
        scratch += [
            pltpu.VMEM((BONDS, rows), jnp.int32),
            pltpu.VMEM((rows,), jnp.int32),
            pltpu.VMEM((9, BONDS, rows), jnp.float32),
            pltpu.SemaphoreType.DMA((4 + 3 * len(blocks) + 2,)),
        ]
    return call(kernel, "images", in_specs, out_specs, out_shape, operands, 0.8 + 1.2 * len(blocks), scratch)


def products_of(chunks, place, partners, mine, theirs, after=(), busy_us=2.0):
    rows, cols = mine[0].shape[0], partners.shape[2]
    count = len(chunks)
    depth = partners.shape[1]

    def kernel(place_ref, partners_ref, *refs):
        keep_ref, send_ref, left_ref = refs[-3:]
        kept = place_ref[0] == place_ref[1]
        for who in range(2):
            at_rows = pl.ds(pl.multiple_of(jnp.where(kept == (who == 0), 0, rows), rows), rows)
            for i, blocks in enumerate(chunks):
                image_ref = refs[who * count + i]
                width = len(blocks) * LANES
                for r in range(3):
                    for spot, block, length in runs_of(blocks):
                        at, to = r * width + spot * LANES, r * depth + block * LANES
                        left_ref[at_rows, to : to + length * LANES] = image_ref[:, at : at + length * LANES]
        total = jnp.dot(
            left_ref[...], partners_ref[...].reshape(3 * depth, cols), preferred_element_type=jnp.float32
        )
        keep_ref[...] = total[:rows]
        send_ref[...] = total[rows:].astype(jnp.bfloat16)

    return call(
        kernel,
        "products",
        [SMEM] + [VMEM] * (1 + 2 * count) + [ANY] * len(after),
        [VMEM, VMEM],
        [pltpu.VMEM((rows, cols), jnp.float32), pltpu.VMEM((rows, cols), jnp.bfloat16)],
        (place, partners, *mine, *theirs, *after),
        busy_us,
        [pltpu.VMEM((2 * rows, 3 * depth), jnp.bfloat16)],
    )


def all_products(chunks, half, partners, mine, theirs):
    place = jnp.stack([half, jnp.zeros((), jnp.int32)])
    low = products_of(chunks, place, partners, mine, theirs)[0]
    high = products_of(chunks, place + jnp.array([0, 1], jnp.int32), partners, mine, theirs)[0]
    return jnp.stack([low, high])


def settle(cells, bit, rows_dev):
    depth = lax.axis_size("atoms")
    place = lax.axis_index("atoms")
    while cells.shape[0] > 1:
        pairs = cells.reshape(cells.shape[0] // 2, 2, rows_dev, -1)
        own = (place >> bit) & 1
        keep = lax.dynamic_index_in_dim(pairs, own, 1, keepdims=False)
        send = lax.dynamic_index_in_dim(pairs, 1 - own, 1, keepdims=False)
        step = 1 << bit
        got = lax.ppermute(send.astype(jnp.bfloat16), "atoms", [(z, z ^ step) for z in range(depth)])
        cells = keep + got.astype(jnp.float32)
        bit += 1
    return cells[0], bit


def collected(terms, bit, shift):
    groups, depth = lax.axis_size("modes"), lax.axis_size("atoms")
    level = 0
    while (1 << level) < groups:
        moves = []
        for z in range(depth):
            for m in range(groups):
                goal = m ^ shift
                settled = all(((z >> (bit + u)) ^ (goal >> u)) & 1 == 0 for u in range(level))
                if settled and ((z >> (bit + level)) ^ (goal >> level)) & 1:
                    moves.append((z * groups + m, (z ^ (1 << (bit + level))) * groups + m))
        sent = sum(term.astype(jnp.float32) for term in terms).astype(jnp.bfloat16)
        terms = terms + [lax.ppermute(sent, ("atoms", "modes"), moves)]
        level += 1
    return terms


def finish(flag, early, late, starts, lengths, freqs, partner_freq, norm_scale):
    rows, cols = early[0].shape
    n_early = len(early)
    operands = [flag, starts, lengths, freqs, partner_freq, *early, *late]
    step = 16

    def kernel(flag_ref, starts_ref, lengths_ref, freqs_ref, partner_ref, *refs):
        out_ref, sum_ref, start_ref, end_ref, freq_ref, folded_ref = refs[-6:]
        def sums(some):
            total = some[0][...]
            for ref in some[1:]:
                total = total + ref[...].astype(jnp.float32)
            return total

        @pl.when(flag_ref[0] == 1)
        def _():
            out_ref[...] = sums(refs[:n_early])

        @pl.when(flag_ref[0] == 0)
        def _():
            out_ref[...] = sums(refs[n_early:-6])

        def turned(row):
            return jnp.broadcast_to(row, (LANES, rows)).T

        mine = pl.ds(flag_ref[2], 1)
        start_row = starts_ref[mine, :].astype(jnp.float32)
        start_ref[...] = turned(start_row)
        end_ref[...] = turned(start_row + lengths_ref[mine, :].astype(jnp.float32))
        freq_ref[...] = turned(freqs_ref[mine, :])
        lane_ids = lax.broadcasted_iota(jnp.int32, (step, LANES), 1)

        def row_step(i, carry):
            at_rows = pl.ds(pl.multiple_of(i * step, step), step)
            start, end, freq = start_ref[at_rows, :], end_ref[at_rows, :], freq_ref[at_rows, :]
            folded = jnp.zeros((step, LANES), jnp.float32)
            for at in range(0, cols, LANES):
                columns = (lane_ids + (flag_ref[1] + at)).astype(jnp.float32)
                inside = (columns >= start) & (columns < end)
                elements = jnp.where(inside, out_ref[at_rows, at : at + LANES] * norm_scale, 0.0)
                out_ref[at_rows, at : at + LANES] = elements
                offset = freq - partner_ref[:, at : at + LANES]
                lorentz = lorentz_width / (math.pi * (offset * offset + lorentz_width * lorentz_width))
                folded = folded + jnp.where(inside, lorentz, 0.0) * elements * elements
            folded_ref[at_rows, :] = folded
            return carry

        lax.fori_loop(0, rows // step, row_step, 0)
        sum_ref[...] = jnp.sum(folded_ref[...].T, axis=0, keepdims=True)

    return call(
        kernel,
        "finish",
        [SMEM] + [VMEM] * (len(operands) - 1),
        [VMEM, VMEM],
        [jax.ShapeDtypeStruct((rows, cols), jnp.float32), jax.ShapeDtypeStruct((1, rows), jnp.float32)],
        operands,
        2.0,
        [pltpu.VMEM((rows, LANES), jnp.float32)] * 4,
    )


def body(
    mode_panel,
    partners,
    bond_blocks,
    neighbors,
    bond_count,
    panel_freq,
    partner_freq,
    win_start,
    win_len,
):
    atom_rows, modes = mode_panel.shape[1:]
    atom_index = lax.axis_index("atoms")
    atom_count = lax.axis_size("atoms")
    groups = lax.axis_size("modes")
    group_index = lax.axis_index("modes")
    half_index = lax.axis_index("sub")
    column_index = lax.axis_index(("modes", "sub"))
    part_cols = partners.shape[2]
    panel_total = win_start.shape[0]
    rows_dev = panel_total // atom_count

    nbr = neighbors.T
    coef = bond_blocks.transpose(0, 2, 1)
    spot = jnp.stack([(atom_index * atom_rows).astype(jnp.int32), (atom_index & 1).astype(jnp.int32)])

    last = atom_rows // LANES - 1
    middle = list(range(1, last))
    cut = len(middle) // 2
    chunks = [middle[:cut], middle[cut:], [last, 0]]
    shared = (spot, mode_panel, nbr, coef, bond_count)
    near, edge_one, edge_two = images_of(chunks[0], *shared, edges=True)
    pairs = [(z, z ^ 1) for z in range(atom_count)]
    others = [(z, ((z + 1) ^ 1) - 1) for z in range(1, atom_count - 1)]
    halos = (lax.ppermute(edge_one, "atoms", pairs), lax.ppermute(edge_two, "atoms", others))

    def from_group(cells, shift):
        return lax.ppermute(cells, "modes", [(m ^ shift, m) for m in range(groups)])

    def from_sibling(cells):
        return lax.ppermute(cells, "sub", [(0, 1), (1, 0)])

    far_all = {shift: [from_group(near, shift)] for shift in range(1, groups)}
    middle_images = images_of(chunks[1], *shared, before=[near])[0]
    before = [middle_images, *[far[0] for far in far_all.values()]]
    mine = [near, middle_images, images_of(chunks[2], *shared, halos=halos, before=before)[0]]
    for shift, far in far_all.items():
        far += [from_group(cells, shift) for cells in mine[1:]]
    theirs = [from_sibling(cells) for cells in mine]
    half = half_index.astype(jnp.int32)
    goal = atom_index * groups // atom_count

    if rows_dev == modes and groups == 2:
        place = jnp.stack([half, (atom_index & 1).astype(jnp.int32)])

        def next_door(some_mine, some_theirs, after=()):
            keep, send = products_of(
                chunks, place, partners, some_mine, some_theirs, after, EARLY_US if after else LATE_US
            )
            return keep, lax.ppermute(send, "atoms", pairs)

        far = far_all[1]
        early = next_door(mine, theirs, far[:2])
        third, kept = lax.optimization_barrier((far[2], early[0]))
        early = (kept, early[1])
        far = [far[0], far[1], third]
        late = next_door(far, [from_sibling(cells) for cells in far])
        sent = jnp.where(
            group_index == goal,
            late[0] + late[1].astype(jnp.float32),
            early[0] + early[1].astype(jnp.float32),
        ).astype(jnp.bfloat16)
        swapped = lax.ppermute(sent, "atoms", [(z, z ^ 2) for z in range(atom_count)])
        early, late = [*early, swapped], [*late, swapped]
    else:

        def settled(some_mine, some_theirs, shift):
            cells = all_products(chunks, half, partners, some_mine, some_theirs)
            cells, bit = settle(cells.reshape(-1, rows_dev, part_cols), 0, rows_dev)
            return collected([cells], bit, shift)

        early, late = settled(mine, theirs, 0), None
        for shift, far in far_all.items():
            terms = settled(far, [from_sibling(cells) for cells in far], shift)
            if late is None:
                late = terms
            else:
                here = (group_index ^ shift) == goal
                late = [jnp.where(here, new, old) for new, old in zip(terms, late)]

    my_freq = lax.dynamic_slice_in_dim(panel_freq, atom_index * rows_dev, rows_dev, 0)
    flag = jnp.stack(
        [
            (group_index == goal).astype(jnp.int32),
            (column_index * part_cols).astype(jnp.int32),
            atom_index.astype(jnp.int32),
        ]
    )
    elements, numerator = finish(
        flag,
        early,
        late,
        win_start.reshape(atom_count, rows_dev),
        win_len.reshape(atom_count, rows_dev),
        panel_freq.reshape(atom_count, rows_dev),
        partner_freq[None, :],
        1.0 / math.sqrt(3 * atom_rows * atom_count),
    )
    holders = groups * 2
    sums = [numerator] + [
        lax.ppermute(numerator, ("modes", "sub"), [(i, i ^ code) for i in range(holders)])
        for code in range(1, holders)
    ]
    while len(sums) > 1:
        sums = [sums[i] + sums[i + 1] for i in range(0, len(sums), 2)]
    diffusivity = math.pi / 3.0 * sums[0][0] / (my_freq * my_freq)
    return (elements, diffusivity)


def solution(mesh):
    return jax.shard_map(
        body,
        mesh=mesh,
        in_specs=(
            P(None, ("dom", "atoms"), ("modes", "sub")),
            P(None, ("dom", "atoms"), ("modes", "sub")),
            P(None, ("dom", "atoms"), None),
            P(("dom", "atoms"), None),
            P(("dom", "atoms")),
            P("dom"),
            P(("dom", "modes", "sub")),
            P("dom"),
            P("dom"),
        ),
        out_specs=(P(("dom", "atoms"), ("modes", "sub")), P(("dom", "atoms"))),
        check_vma=False,
    )
```

```python
import math

import jax
import jax.numpy as jnp
from jax import lax
from jax.experimental import pallas as pl
from jax.experimental.pallas import tpu as pltpu
from jax.sharding import PartitionSpec as P

HALO = 96
BONDS = 16
LANES = 128
SPAN = LANES + 2 * HALO
GROUP = 16
VMEM_BYTES = 14 * 1024 * 1024

lorentz_width = 0.05

EARLY_US = 6.0
LATE_US = 0.1

HBM = pl.BlockSpec(memory_space=pltpu.HBM)
ANY = pl.BlockSpec(memory_space=pl.ANY)
VMEM = pl.BlockSpec(memory_space=pltpu.VMEM)
SMEM = pl.BlockSpec(memory_space=pltpu.SMEM)


def call(kernel, name, in_specs, out_specs, out_shape, operands, busy_us, scratch=()):
    operands = [
        pltpu.with_memory_space_constraint(x, spec.memory_space) if spec is VMEM or spec is HBM else x
        for spec, x in zip(in_specs, operands)
    ]
    return pl.pallas_call(
        kernel,
        in_specs=in_specs,
        out_specs=out_specs,
        out_shape=out_shape,
        scratch_shapes=list(scratch),
        compiler_params=pltpu.CompilerParams(vmem_limit_bytes=VMEM_BYTES),
        cost_estimate=pl.CostEstimate(
            flops=int(busy_us * 1.1e9), bytes_accessed=int(busy_us * 1e5), transcendentals=0
        ),
        name=name,
    )(*operands)


def runs_of(blocks):
    runs = []
    for place, block in enumerate(blocks):
        if runs and runs[-1][1] + runs[-1][2] == block:
            runs[-1][2] += 1
        else:
            runs.append([place, block, 1])
    return runs


def build_block(first, base, nbr_ref, coef_ref, count_ref, dense_ref):
    lanes = pl.ds(first, LANES)
    target = nbr_ref[:, lanes] - (base + (first - HALO))
    slot_ids = lax.broadcasted_iota(jnp.int32, (BONDS, LANES), 0)
    live = slot_ids < count_ref[lanes].reshape(1, LANES)
    coefs = [jnp.where(live, coef_ref[e, :, lanes], 0.0) for e in range(9)]
    halves = [(target[h : h + 8], slot_ids[h : h + 8]) for h in (0, 8)]
    merged = [[jnp.zeros((8, LANES), jnp.float32) for _ in range(9)] for _ in range(2)]
    named = [jnp.broadcast_to(target[k : k + 1], (8, LANES)) for k in range(BONDS)]
    for k in range(BONDS):
        rows = [jnp.broadcast_to(coefs[e][k : k + 1], (8, LANES)) for e in range(9)]
        for h in range(k // 8, 2):
            same = (halves[h][0] == named[k]) & (halves[h][1] >= k)
            for e in range(9):
                merged[h][e] = merged[h][e] + jnp.where(same, rows[e], 0.0)
    row_ids = lax.broadcasted_iota(jnp.int32, (8, LANES), 0)

    def group_step(g, carry):
        cells = [[] for _ in range(9)]
        for tile in range(GROUP // 8):
            here = row_ids + (g * GROUP + tile * 8)
            slot = jnp.full((8, LANES), -1, jnp.int32)
            for k in range(BONDS):
                slot = jnp.where(named[k] == here, k, slot)
            place = slot & 7
            early, live_cell = slot < 8, slot >= 0
            for e in range(9):
                picks = [
                    jnp.take_along_axis(merged[h][e], place, axis=0, mode="promise_in_bounds")
                    for h in range(2)
                ]
                cells[e].append(jnp.where(live_cell, jnp.where(early, picks[0], picks[1]), 0.0))
        for r in range(3):
            for c in range(3):
                value = jnp.concatenate(cells[3 * r + c], axis=0)
                high = value.astype(jnp.bfloat16)
                low = (value - high.astype(jnp.float32)).astype(jnp.bfloat16)
                at = pl.ds(pl.multiple_of(c * SPAN + g * GROUP, GROUP), GROUP)
                dense_ref[at, 2 * r * LANES : (2 * r + 1) * LANES] = high
                dense_ref[at, (2 * r + 1) * LANES : (2 * r + 2) * LANES] = low
        return carry

    lax.fori_loop(0, SPAN // GROUP, group_step, 0)


def images_of(blocks, spot, panel, nbr, coef, count, halos=(), before=(), edges=False):
    rows, modes = panel.shape[1:]
    loads = len(before) == 0
    operands = [spot, nbr, count, coef, panel, *halos, *before]
    in_specs = [SMEM] + [HBM if loads else VMEM] * 4 + [VMEM] * len(halos) + [ANY] * len(before)
    width = len(blocks) * LANES
    out_shape = [pltpu.VMEM((modes, 3 * width), jnp.bfloat16)]
    out_specs = [VMEM]
    if edges:
        out_shape += [jax.ShapeDtypeStruct((3, HALO, modes), jnp.bfloat16)] * 2
        out_specs += [ANY] * 2
    n_in, n_out = len(operands), len(out_shape)

    def pieces_of(block):
        begin, end = block * LANES - HALO, (block + 1) * LANES + HALO
        found = []
        if begin < 0:
            found.append((1, HALO + begin, 0, -begin))
        low, high = max(begin, 0), min(end, rows)
        found.append((0, low, low - begin, high - low))
        if end > rows:
            found.append((2, 0, rows - begin, end - rows))
        return found

    def kernel(*refs):
        spot_ref, nbr_ref, count_ref, coef_ref, panel_ref = refs[:5]
        odd = spot_ref[1]
        outs = refs[n_in : n_in + n_out]
        window_ref, dense_ref, *scratch_refs = refs[n_in + n_out :]
        window_copies = []
        if loads:
            sources = (nbr_ref, count_ref, coef_ref)
            nbr_ref, count_ref, coef_ref, sems = scratch_refs
            copies = []

            def start(source, target, kept):
                copy = pltpu.make_async_copy(source, target, sems.at[len(copies) + len(window_copies)])
                copy.start()
                kept.append(copy)

            start(sources[0], nbr_ref, copies)
            start(sources[1], count_ref, copies)
            for _, block, length in runs_of(blocks):
                at = pl.ds(block * LANES, length * LANES)
                start(sources[2].at[:, :, at], coef_ref.at[:, :, at], copies)
            for place, block in enumerate(blocks):
                for _, source, at, length in pieces_of(block):
                    start(
                        panel_ref.at[:, pl.ds(source, length)], window_ref.at[place, :, pl.ds(at, length)], window_copies
                    )
            if edges:
                for turn, out in enumerate(outs[1:3]):
                    at = pl.multiple_of(jnp.where(odd == turn, rows - HALO, 0), 32)
                    start(panel_ref.at[:, pl.ds(at, HALO)], out, window_copies)
            for copy in copies:
                copy.wait()
        else:
            for place, block in enumerate(blocks):
                for which, source, at, length in pieces_of(block):
                    there = slice(source, source + length)
                    if which == 0:
                        found = panel_ref[:, there, :]
                    else:
                        found = jnp.where((odd == 1) == (which == 1), refs[5][:, there, :], refs[6][:, there, :])
                    window_ref[place, :, at : at + length, :] = found

        for place, block in enumerate(blocks):
            build_block(block * LANES, spot_ref[0], nbr_ref, coef_ref, count_ref, dense_ref)
            if loads and place == 0:
                for copy in window_copies:
                    copy.wait()
            both = lax.dot_general(
                window_ref[place].reshape(3 * SPAN, modes),
                dense_ref[...],
                (((0,), (0,)), ((), ())),
                preferred_element_type=jnp.float32,
            )
            for r in range(3):
                image = both[:, 2 * r * LANES : (2 * r + 1) * LANES]
                image = image + both[:, (2 * r + 1) * LANES : (2 * r + 2) * LANES]
                at = r * width + place * LANES
                outs[0][:, at : at + LANES] = image.astype(jnp.bfloat16)

    scratch = [
        pltpu.VMEM((len(blocks), 3, SPAN, modes), jnp.bfloat16),
        pltpu.VMEM((3 * SPAN, 6 * LANES), jnp.bfloat16),
    ]
    if loads:
        scratch += [
            pltpu.VMEM((BONDS, rows), jnp.int32),
            pltpu.VMEM((rows,), jnp.int32),
            pltpu.VMEM((9, BONDS, rows), jnp.float32),
            pltpu.SemaphoreType.DMA((4 + 3 * len(blocks) + 2,)),
        ]
    return call(kernel, "images", in_specs, out_specs, out_shape, operands, 0.8 + 1.2 * len(blocks), scratch)


def products_of(chunks, place, partners, mine, theirs, after=(), busy_us=2.0):
    rows, cols = mine[0].shape[0], partners.shape[2]
    count = len(chunks)
    depth = partners.shape[1]

    def kernel(place_ref, partners_hbm, *refs):
        keep_ref, send_ref, left_ref, partners_ref, sems = refs[-5:]
        copies = [
            pltpu.make_async_copy(partners_hbm.at[r], partners_ref.at[r], sems.at[r]) for r in range(3)
        ]
        for copy in copies:
            copy.start()
        kept = place_ref[0] == place_ref[1]
        for who in range(2):
            at_rows = pl.ds(pl.multiple_of(jnp.where(kept == (who == 0), 0, rows), rows), rows)
            for i, blocks in enumerate(chunks):
                image_ref = refs[who * count + i]
                width = len(blocks) * LANES
                for r in range(3):
                    for spot, block, length in runs_of(blocks):
                        at, to = r * width + spot * LANES, r * depth + block * LANES
                        left_ref[at_rows, to : to + length * LANES] = image_ref[:, at : at + length * LANES]
        total = None
        for r, copy in enumerate(copies):
            copy.wait()
            part = jnp.dot(
                left_ref[:, r * depth : (r + 1) * depth], partners_ref[r], preferred_element_type=jnp.float32
            )
            total = part if total is None else total + part
        keep_ref[...] = total[:rows]
        send_ref[...] = total[rows:].astype(jnp.bfloat16)

    return call(
        kernel,
        "products",
        [SMEM, HBM] + [VMEM] * (2 * count) + [ANY] * len(after),
        [VMEM, VMEM],
        [pltpu.VMEM((rows, cols), jnp.float32), pltpu.VMEM((rows, cols), jnp.bfloat16)],
        (place, partners, *mine, *theirs, *after),
        busy_us,
        [
            pltpu.VMEM((2 * rows, 3 * depth), jnp.bfloat16),
            pltpu.VMEM((3, depth, cols), jnp.bfloat16),
            pltpu.SemaphoreType.DMA((3,)),
        ],
    )


def all_products(chunks, half, partners, mine, theirs):
    place = jnp.stack([half, jnp.zeros((), jnp.int32)])
    low = products_of(chunks, place, partners, mine, theirs)[0]
    high = products_of(chunks, place + jnp.array([0, 1], jnp.int32), partners, mine, theirs)[0]
    return jnp.stack([low, high])


def settle(cells, bit, rows_dev):
    depth = lax.axis_size("atoms")
    place = lax.axis_index("atoms")
    while cells.shape[0] > 1:
        pairs = cells.reshape(cells.shape[0] // 2, 2, rows_dev, -1)
        own = (place >> bit) & 1
        keep = lax.dynamic_index_in_dim(pairs, own, 1, keepdims=False)
        send = lax.dynamic_index_in_dim(pairs, 1 - own, 1, keepdims=False)
        step = 1 << bit
        got = lax.ppermute(send.astype(jnp.bfloat16), "atoms", [(z, z ^ step) for z in range(depth)])
        cells = keep + got.astype(jnp.float32)
        bit += 1
    return cells[0], bit


def collected(terms, bit, shift):
    groups, depth = lax.axis_size("modes"), lax.axis_size("atoms")
    level = 0
    while (1 << level) < groups:
        moves = []
        for z in range(depth):
            for m in range(groups):
                goal = m ^ shift
                settled = all(((z >> (bit + u)) ^ (goal >> u)) & 1 == 0 for u in range(level))
                if settled and ((z >> (bit + level)) ^ (goal >> level)) & 1:
                    moves.append((z * groups + m, (z ^ (1 << (bit + level))) * groups + m))
        sent = sum(term.astype(jnp.float32) for term in terms).astype(jnp.bfloat16)
        terms = terms + [lax.ppermute(sent, ("atoms", "modes"), moves)]
        level += 1
    return terms


def finish(flag, early, late, starts, lengths, freqs, partner_freq, norm_scale):
    rows, cols = early[0].shape
    n_early = len(early)
    operands = [flag, starts, lengths, freqs, partner_freq, *early, *late]
    step = 16

    def kernel(flag_ref, starts_ref, lengths_ref, freqs_ref, partner_ref, *refs):
        out_ref, sum_ref, start_ref, end_ref, freq_ref, folded_ref = refs[-6:]
        def sums(some):
            total = some[0][...]
            for ref in some[1:]:
                total = total + ref[...].astype(jnp.float32)
            return total

        @pl.when(flag_ref[0] == 1)
        def _():
            out_ref[...] = sums(refs[:n_early])

        @pl.when(flag_ref[0] == 0)
        def _():
            out_ref[...] = sums(refs[n_early:-6])

        def turned(row):
            return jnp.broadcast_to(row, (LANES, rows)).T

        mine = pl.ds(flag_ref[2], 1)
        start_row = starts_ref[mine, :].astype(jnp.float32)
        start_ref[...] = turned(start_row)
        end_ref[...] = turned(start_row + lengths_ref[mine, :].astype(jnp.float32))
        freq_ref[...] = turned(freqs_ref[mine, :])
        lane_ids = lax.broadcasted_iota(jnp.int32, (step, LANES), 1)

        def row_step(i, carry):
            at_rows = pl.ds(pl.multiple_of(i * step, step), step)
            start, end, freq = start_ref[at_rows, :], end_ref[at_rows, :], freq_ref[at_rows, :]
            folded = jnp.zeros((step, LANES), jnp.float32)
            for at in range(0, cols, LANES):
                columns = (lane_ids + (flag_ref[1] + at)).astype(jnp.float32)
                inside = (columns >= start) & (columns < end)
                elements = jnp.where(inside, out_ref[at_rows, at : at + LANES] * norm_scale, 0.0)
                out_ref[at_rows, at : at + LANES] = elements
                offset = freq - partner_ref[:, at : at + LANES]
                lorentz = lorentz_width / (math.pi * (offset * offset + lorentz_width * lorentz_width))
                folded = folded + jnp.where(inside, lorentz, 0.0) * elements * elements
            folded_ref[at_rows, :] = folded
            return carry

        lax.fori_loop(0, rows // step, row_step, 0)
        sum_ref[...] = jnp.sum(folded_ref[...].T, axis=0, keepdims=True)

    return call(
        kernel,
        "finish",
        [SMEM] + [VMEM] * (len(operands) - 1),
        [VMEM, VMEM],
        [jax.ShapeDtypeStruct((rows, cols), jnp.float32), jax.ShapeDtypeStruct((1, rows), jnp.float32)],
        operands,
        2.0,
        [pltpu.VMEM((rows, LANES), jnp.float32)] * 4,
    )


def body(
    mode_panel,
    partners,
    bond_blocks,
    neighbors,
    bond_count,
    panel_freq,
    partner_freq,
    win_start,
    win_len,
):
    atom_rows, modes = mode_panel.shape[1:]
    atom_index = lax.axis_index("atoms")
    atom_count = lax.axis_size("atoms")
    groups = lax.axis_size("modes")
    group_index = lax.axis_index("modes")
    half_index = lax.axis_index("sub")
    column_index = lax.axis_index(("modes", "sub"))
    part_cols = partners.shape[2]
    panel_total = win_start.shape[0]
    rows_dev = panel_total // atom_count

    nbr = neighbors.T
    coef = bond_blocks.transpose(0, 2, 1)
    spot = jnp.stack([(atom_index * atom_rows).astype(jnp.int32), (atom_index & 1).astype(jnp.int32)])

    last = atom_rows // LANES - 1
    middle = list(range(1, last))
    cut = len(middle) // 2
    chunks = [middle[:cut], middle[cut:], [last, 0]]
    shared = (spot, mode_panel, nbr, coef, bond_count)
    near, edge_one, edge_two = images_of(chunks[0], *shared, edges=True)
    pairs = [(z, z ^ 1) for z in range(atom_count)]
    others = [(z, ((z + 1) ^ 1) - 1) for z in range(1, atom_count - 1)]
    halos = (lax.ppermute(edge_one, "atoms", pairs), lax.ppermute(edge_two, "atoms", others))

    def from_group(cells, shift):
        return lax.ppermute(cells, "modes", [(m ^ shift, m) for m in range(groups)])

    def from_sibling(cells):
        return lax.ppermute(cells, "sub", [(0, 1), (1, 0)])

    far_all = {shift: [from_group(near, shift)] for shift in range(1, groups)}
    middle_images = images_of(chunks[1], *shared, before=[near])[0]
    before = [middle_images, *[far[0] for far in far_all.values()]]
    mine = [near, middle_images, images_of(chunks[2], *shared, halos=halos, before=before)[0]]
    for shift, far in far_all.items():
        far += [from_group(cells, shift) for cells in mine[1:]]
    theirs = [from_sibling(cells) for cells in mine]
    half = half_index.astype(jnp.int32)
    goal = atom_index * groups // atom_count

    if rows_dev == modes and groups == 2:
        place = jnp.stack([half, (atom_index & 1).astype(jnp.int32)])

        def next_door(some_mine, some_theirs, after=()):
            keep, send = products_of(
                chunks, place, partners, some_mine, some_theirs, after, EARLY_US if after else LATE_US
            )
            return keep, lax.ppermute(send, "atoms", pairs)

        far = far_all[1]
        early = next_door(mine, theirs, far[:2])
        third, kept = lax.optimization_barrier((far[2], early[0]))
        early = (kept, early[1])
        far = [far[0], far[1], third]
        late = next_door(far, [from_sibling(cells) for cells in far])
        sent = jnp.where(
            group_index == goal,
            late[0] + late[1].astype(jnp.float32),
            early[0] + early[1].astype(jnp.float32),
        ).astype(jnp.bfloat16)
        swapped = lax.ppermute(sent, "atoms", [(z, z ^ 2) for z in range(atom_count)])
        early, late = [*early, swapped], [*late, swapped]
    else:

        def settled(some_mine, some_theirs, shift):
            cells = all_products(chunks, half, partners, some_mine, some_theirs)
            cells, bit = settle(cells.reshape(-1, rows_dev, part_cols), 0, rows_dev)
            return collected([cells], bit, shift)

        early, late = settled(mine, theirs, 0), None
        for shift, far in far_all.items():
            terms = settled(far, [from_sibling(cells) for cells in far], shift)
            if late is None:
                late = terms
            else:
                here = (group_index ^ shift) == goal
                late = [jnp.where(here, new, old) for new, old in zip(terms, late)]

    my_freq = lax.dynamic_slice_in_dim(panel_freq, atom_index * rows_dev, rows_dev, 0)
    flag = jnp.stack(
        [
            (group_index == goal).astype(jnp.int32),
            (column_index * part_cols).astype(jnp.int32),
            atom_index.astype(jnp.int32),
        ]
    )
    elements, numerator = finish(
        flag,
        early,
        late,
        win_start.reshape(atom_count, rows_dev),
        win_len.reshape(atom_count, rows_dev),
        panel_freq.reshape(atom_count, rows_dev),
        partner_freq[None, :],
        1.0 / math.sqrt(3 * atom_rows * atom_count),
    )
    holders = groups * 2
    sums = [numerator] + [
        lax.ppermute(numerator, ("modes", "sub"), [(i, i ^ code) for i in range(holders)])
        for code in range(1, holders)
    ]
    while len(sums) > 1:
        sums = [sums[i] + sums[i + 1] for i in range(0, len(sums), 2)]
    diffusivity = math.pi / 3.0 * sums[0][0] / (my_freq * my_freq)
    return (elements, diffusivity)


def solution(mesh):
    return jax.shard_map(
        body,
        mesh=mesh,
        in_specs=(
            P(None, ("dom", "atoms"), ("modes", "sub")),
            P(None, ("dom", "atoms"), ("modes", "sub")),
            P(None, ("dom", "atoms"), None),
            P(("dom", "atoms"), None),
            P(("dom", "atoms")),
            P("dom"),
            P(("dom", "modes", "sub")),
            P("dom"),
            P("dom"),
        ),
        out_specs=(P(("dom", "atoms"), ("modes", "sub")), P(("dom", "atoms"))),
        check_vma=False,
    )
```

```python
import math

import jax
import jax.numpy as jnp
from jax import lax
from jax.experimental import pallas as pl
from jax.experimental.pallas import tpu as pltpu
from jax.sharding import PartitionSpec as P

HALO = 96
BONDS = 16
LANES = 128
SPAN = LANES + 2 * HALO
GROUP = 16
VMEM_BYTES = 14 * 1024 * 1024

lorentz_width = 0.05

EARLY_US = 6.0
LATE_US = 0.1

HBM = pl.BlockSpec(memory_space=pltpu.HBM)
ANY = pl.BlockSpec(memory_space=pl.ANY)
VMEM = pl.BlockSpec(memory_space=pltpu.VMEM)
SMEM = pl.BlockSpec(memory_space=pltpu.SMEM)


def call(kernel, name, in_specs, out_specs, out_shape, operands, busy_us, scratch=()):
    operands = [
        pltpu.with_memory_space_constraint(x, spec.memory_space) if spec is VMEM or spec is HBM else x
        for spec, x in zip(in_specs, operands)
    ]
    return pl.pallas_call(
        kernel,
        in_specs=in_specs,
        out_specs=out_specs,
        out_shape=out_shape,
        scratch_shapes=list(scratch),
        compiler_params=pltpu.CompilerParams(vmem_limit_bytes=VMEM_BYTES),
        cost_estimate=pl.CostEstimate(
            flops=int(busy_us * 1.1e9), bytes_accessed=int(busy_us * 1e5), transcendentals=0
        ),
        name=name,
    )(*operands)


def runs_of(blocks):
    runs = []
    for place, block in enumerate(blocks):
        if runs and runs[-1][1] + runs[-1][2] == block:
            runs[-1][2] += 1
        else:
            runs.append([place, block, 1])
    return runs


def build_block(first, base, nbr_ref, coef_ref, count_ref, dense_ref):
    lanes = pl.ds(first, LANES)
    target = nbr_ref[:, lanes] - (base + (first - HALO))
    slot_ids = lax.broadcasted_iota(jnp.int32, (BONDS, LANES), 0)
    live = slot_ids < count_ref[lanes].reshape(1, LANES)
    coefs = [jnp.where(live, coef_ref[e, :, lanes], 0.0) for e in range(9)]
    halves = [(target[h : h + 8], slot_ids[h : h + 8]) for h in (0, 8)]
    merged = [[jnp.zeros((8, LANES), jnp.float32) for _ in range(9)] for _ in range(2)]
    named = [jnp.broadcast_to(target[k : k + 1], (8, LANES)) for k in range(BONDS)]
    for k in range(BONDS):
        rows = [jnp.broadcast_to(coefs[e][k : k + 1], (8, LANES)) for e in range(9)]
        for h in range(k // 8, 2):
            same = (halves[h][0] == named[k]) & (halves[h][1] >= k)
            for e in range(9):
                merged[h][e] = merged[h][e] + jnp.where(same, rows[e], 0.0)
    row_ids = lax.broadcasted_iota(jnp.int32, (8, LANES), 0)

    def group_step(g, carry):
        cells = [[] for _ in range(9)]
        for tile in range(GROUP // 8):
            here = row_ids + (g * GROUP + tile * 8)
            slot = jnp.full((8, LANES), -1, jnp.int32)
            for k in range(BONDS):
                slot = jnp.where(named[k] == here, k, slot)
            place = slot & 7
            early, live_cell = slot < 8, slot >= 0
            for e in range(9):
                picks = [
                    jnp.take_along_axis(merged[h][e], place, axis=0, mode="promise_in_bounds")
                    for h in range(2)
                ]
                cells[e].append(jnp.where(live_cell, jnp.where(early, picks[0], picks[1]), 0.0))
        for r in range(3):
            for c in range(3):
                value = jnp.concatenate(cells[3 * r + c], axis=0)
                high = value.astype(jnp.bfloat16)
                low = (value - high.astype(jnp.float32)).astype(jnp.bfloat16)
                at = pl.ds(pl.multiple_of(c * SPAN + g * GROUP, GROUP), GROUP)
                dense_ref[at, 2 * r * LANES : (2 * r + 1) * LANES] = high
                dense_ref[at, (2 * r + 1) * LANES : (2 * r + 2) * LANES] = low
        return carry

    lax.fori_loop(0, SPAN // GROUP, group_step, 0)


def edges_of(spot, panel):
    rows, modes = panel.shape[1:]

    def kernel(spot_ref, panel_hbm, one_ref, two_ref, sems):
        copies = []
        for turn, out in enumerate((one_ref, two_ref)):
            at = pl.multiple_of(jnp.where(spot_ref[1] == turn, rows - HALO, 0), 32)
            copies.append(pltpu.make_async_copy(panel_hbm.at[:, pl.ds(at, HALO)], out, sems.at[turn]))
        for copy in copies:
            copy.start()
        for copy in copies:
            copy.wait()

    return call(
        kernel,
        "edges",
        [SMEM, HBM],
        [VMEM] * 2,
        [pltpu.VMEM((3, HALO, modes), jnp.bfloat16)] * 2,
        (spot, panel),
        1.0,
        [pltpu.SemaphoreType.DMA((2,))],
    )


def images_of(blocks, spot, panel, nbr, coef, count, halos=(), before=()):
    rows, modes = panel.shape[1:]
    loads = len(before) == 0
    operands = [spot, nbr, count, coef, panel, *halos, *before]
    in_specs = [SMEM] + [HBM if loads else VMEM] * 4 + [VMEM] * len(halos) + [ANY] * len(before)
    width = len(blocks) * LANES
    out_shape = [pltpu.VMEM((modes, 3 * width), jnp.bfloat16)]
    out_specs = [VMEM]
    n_in, n_out = len(operands), len(out_shape)

    def pieces_of(block):
        begin, end = block * LANES - HALO, (block + 1) * LANES + HALO
        found = []
        if begin < 0:
            found.append((1, HALO + begin, 0, -begin))
        low, high = max(begin, 0), min(end, rows)
        found.append((0, low, low - begin, high - low))
        if end > rows:
            found.append((2, 0, rows - begin, end - rows))
        return found

    def kernel(*refs):
        spot_ref, nbr_ref, count_ref, coef_ref, panel_ref = refs[:5]
        odd = spot_ref[1]
        outs = refs[n_in : n_in + n_out]
        window_ref, dense_ref, *scratch_refs = refs[n_in + n_out :]
        window_copies = []
        if loads:
            sources = (nbr_ref, count_ref, coef_ref)
            nbr_ref, count_ref, coef_ref, sems = scratch_refs
            copies = []

            def start(source, target, kept):
                copy = pltpu.make_async_copy(source, target, sems.at[len(copies) + len(window_copies)])
                copy.start()
                kept.append(copy)

            start(sources[0], nbr_ref, copies)
            start(sources[1], count_ref, copies)
            for _, block, length in runs_of(blocks):
                at = pl.ds(block * LANES, length * LANES)
                start(sources[2].at[:, :, at], coef_ref.at[:, :, at], copies)
            for place, block in enumerate(blocks):
                for _, source, at, length in pieces_of(block):
                    start(
                        panel_ref.at[:, pl.ds(source, length)], window_ref.at[place, :, pl.ds(at, length)], window_copies
                    )
            for copy in copies:
                copy.wait()
        else:
            for place, block in enumerate(blocks):
                for which, source, at, length in pieces_of(block):
                    there = slice(source, source + length)
                    if which == 0:
                        found = panel_ref[:, there, :]
                    else:
                        found = jnp.where((odd == 1) == (which == 1), refs[5][:, there, :], refs[6][:, there, :])
                    window_ref[place, :, at : at + length, :] = found

        for place, block in enumerate(blocks):
            build_block(block * LANES, spot_ref[0], nbr_ref, coef_ref, count_ref, dense_ref)
            if loads and place == 0:
                for copy in window_copies:
                    copy.wait()
            both = lax.dot_general(
                window_ref[place].reshape(3 * SPAN, modes),
                dense_ref[...],
                (((0,), (0,)), ((), ())),
                preferred_element_type=jnp.float32,
            )
            for r in range(3):
                image = both[:, 2 * r * LANES : (2 * r + 1) * LANES]
                image = image + both[:, (2 * r + 1) * LANES : (2 * r + 2) * LANES]
                at = r * width + place * LANES
                outs[0][:, at : at + LANES] = image.astype(jnp.bfloat16)

    scratch = [
        pltpu.VMEM((len(blocks), 3, SPAN, modes), jnp.bfloat16),
        pltpu.VMEM((3 * SPAN, 6 * LANES), jnp.bfloat16),
    ]
    if loads:
        scratch += [
            pltpu.VMEM((BONDS, rows), jnp.int32),
            pltpu.VMEM((rows,), jnp.int32),
            pltpu.VMEM((9, BONDS, rows), jnp.float32),
            pltpu.SemaphoreType.DMA((4 + 3 * len(blocks),)),
        ]
    return call(kernel, "images", in_specs, out_specs, out_shape, operands, 0.8 + 1.2 * len(blocks), scratch)


def products_of(chunks, place, partners, mine, theirs, after=(), busy_us=2.0):
    rows, cols = mine[0].shape[0], partners.shape[2]
    count = len(chunks)
    depth = partners.shape[1]

    def kernel(place_ref, partners_hbm, *refs):
        keep_ref, send_ref, left_ref, partners_ref, sems = refs[-5:]
        copies = [
            pltpu.make_async_copy(partners_hbm.at[r], partners_ref.at[r], sems.at[r]) for r in range(3)
        ]
        for copy in copies:
            copy.start()
        kept = place_ref[0] == place_ref[1]
        for who in range(2):
            at_rows = pl.ds(pl.multiple_of(jnp.where(kept == (who == 0), 0, rows), rows), rows)
            for i, blocks in enumerate(chunks):
                image_ref = refs[who * count + i]
                width = len(blocks) * LANES
                for r in range(3):
                    for spot, block, length in runs_of(blocks):
                        at, to = r * width + spot * LANES, r * depth + block * LANES
                        left_ref[at_rows, to : to + length * LANES] = image_ref[:, at : at + length * LANES]
        total = None
        for r, copy in enumerate(copies):
            copy.wait()
            part = jnp.dot(
                left_ref[:, r * depth : (r + 1) * depth], partners_ref[r], preferred_element_type=jnp.float32
            )
            total = part if total is None else total + part
        keep_ref[...] = total[:rows]
        send_ref[...] = total[rows:].astype(jnp.bfloat16)

    return call(
        kernel,
        "products",
        [SMEM, HBM] + [VMEM] * (2 * count) + [ANY] * len(after),
        [VMEM, VMEM],
        [pltpu.VMEM((rows, cols), jnp.float32), pltpu.VMEM((rows, cols), jnp.bfloat16)],
        (place, partners, *mine, *theirs, *after),
        busy_us,
        [
            pltpu.VMEM((2 * rows, 3 * depth), jnp.bfloat16),
            pltpu.VMEM((3, depth, cols), jnp.bfloat16),
            pltpu.SemaphoreType.DMA((3,)),
        ],
    )


def all_products(chunks, half, partners, mine, theirs):
    place = jnp.stack([half, jnp.zeros((), jnp.int32)])
    low = products_of(chunks, place, partners, mine, theirs)[0]
    high = products_of(chunks, place + jnp.array([0, 1], jnp.int32), partners, mine, theirs)[0]
    return jnp.stack([low, high])


def settle(cells, bit, rows_dev):
    depth = lax.axis_size("atoms")
    place = lax.axis_index("atoms")
    while cells.shape[0] > 1:
        pairs = cells.reshape(cells.shape[0] // 2, 2, rows_dev, -1)
        own = (place >> bit) & 1
        keep = lax.dynamic_index_in_dim(pairs, own, 1, keepdims=False)
        send = lax.dynamic_index_in_dim(pairs, 1 - own, 1, keepdims=False)
        step = 1 << bit
        got = lax.ppermute(send.astype(jnp.bfloat16), "atoms", [(z, z ^ step) for z in range(depth)])
        cells = keep + got.astype(jnp.float32)
        bit += 1
    return cells[0], bit


def collected(terms, bit, shift):
    groups, depth = lax.axis_size("modes"), lax.axis_size("atoms")
    level = 0
    while (1 << level) < groups:
        moves = []
        for z in range(depth):
            for m in range(groups):
                goal = m ^ shift
                settled = all(((z >> (bit + u)) ^ (goal >> u)) & 1 == 0 for u in range(level))
                if settled and ((z >> (bit + level)) ^ (goal >> level)) & 1:
                    moves.append((z * groups + m, (z ^ (1 << (bit + level))) * groups + m))
        sent = sum(term.astype(jnp.float32) for term in terms).astype(jnp.bfloat16)
        terms = terms + [lax.ppermute(sent, ("atoms", "modes"), moves)]
        level += 1
    return terms


def finish(flag, early, late, starts, lengths, freqs, partner_freq, norm_scale):
    rows, cols = early[0].shape
    n_early = len(early)
    operands = [flag, starts, lengths, freqs, partner_freq, *early, *late]
    step = 16

    def kernel(flag_ref, starts_ref, lengths_ref, freqs_ref, partner_ref, *refs):
        out_ref, sum_ref, start_ref, end_ref, freq_ref, folded_ref = refs[-6:]
        def sums(some):
            total = some[0][...]
            for ref in some[1:]:
                total = total + ref[...].astype(jnp.float32)
            return total

        @pl.when(flag_ref[0] == 1)
        def _():
            out_ref[...] = sums(refs[:n_early])

        @pl.when(flag_ref[0] == 0)
        def _():
            out_ref[...] = sums(refs[n_early:-6])

        def turned(row):
            return jnp.broadcast_to(row, (LANES, rows)).T

        mine = pl.ds(flag_ref[2], 1)
        start_row = starts_ref[mine, :].astype(jnp.float32)
        start_ref[...] = turned(start_row)
        end_ref[...] = turned(start_row + lengths_ref[mine, :].astype(jnp.float32))
        freq_ref[...] = turned(freqs_ref[mine, :])
        lane_ids = lax.broadcasted_iota(jnp.int32, (step, LANES), 1)

        def row_step(i, carry):
            at_rows = pl.ds(pl.multiple_of(i * step, step), step)
            start, end, freq = start_ref[at_rows, :], end_ref[at_rows, :], freq_ref[at_rows, :]
            folded = jnp.zeros((step, LANES), jnp.float32)
            for at in range(0, cols, LANES):
                columns = (lane_ids + (flag_ref[1] + at)).astype(jnp.float32)
                inside = (columns >= start) & (columns < end)
                elements = jnp.where(inside, out_ref[at_rows, at : at + LANES] * norm_scale, 0.0)
                out_ref[at_rows, at : at + LANES] = elements
                offset = freq - partner_ref[:, at : at + LANES]
                lorentz = lorentz_width / (math.pi * (offset * offset + lorentz_width * lorentz_width))
                folded = folded + jnp.where(inside, lorentz, 0.0) * elements * elements
            folded_ref[at_rows, :] = folded
            return carry

        lax.fori_loop(0, rows // step, row_step, 0)
        sum_ref[...] = jnp.sum(folded_ref[...].T, axis=0, keepdims=True)

    return call(
        kernel,
        "finish",
        [SMEM] + [VMEM] * (len(operands) - 1),
        [VMEM, VMEM],
        [jax.ShapeDtypeStruct((rows, cols), jnp.float32), jax.ShapeDtypeStruct((1, rows), jnp.float32)],
        operands,
        2.0,
        [pltpu.VMEM((rows, LANES), jnp.float32)] * 4,
    )


def body(
    mode_panel,
    partners,
    bond_blocks,
    neighbors,
    bond_count,
    panel_freq,
    partner_freq,
    win_start,
    win_len,
):
    atom_rows, modes = mode_panel.shape[1:]
    atom_index = lax.axis_index("atoms")
    atom_count = lax.axis_size("atoms")
    groups = lax.axis_size("modes")
    group_index = lax.axis_index("modes")
    half_index = lax.axis_index("sub")
    column_index = lax.axis_index(("modes", "sub"))
    part_cols = partners.shape[2]
    panel_total = win_start.shape[0]
    rows_dev = panel_total // atom_count

    nbr = neighbors.T
    coef = bond_blocks.transpose(0, 2, 1)
    spot = jnp.stack([(atom_index * atom_rows).astype(jnp.int32), (atom_index & 1).astype(jnp.int32)])

    last = atom_rows // LANES - 1
    middle = list(range(1, last))
    cut = len(middle) // 2
    chunks = [middle[:cut], middle[cut:], [last, 0]]
    shared = (spot, mode_panel, nbr, coef, bond_count)
    edge_one, edge_two = edges_of(spot, mode_panel)
    pairs = [(z, z ^ 1) for z in range(atom_count)]
    others = [(z, ((z + 1) ^ 1) - 1) for z in range(1, atom_count - 1)]
    halos = (lax.ppermute(edge_one, "atoms", pairs), lax.ppermute(edge_two, "atoms", others))
    near = images_of(chunks[0], *shared)[0]

    def from_group(cells, shift):
        return lax.ppermute(cells, "modes", [(m ^ shift, m) for m in range(groups)])

    def from_sibling(cells):
        return lax.ppermute(cells, "sub", [(0, 1), (1, 0)])

    far_all = {shift: [from_group(near, shift)] for shift in range(1, groups)}
    middle_images = images_of(chunks[1], *shared, before=[near, *halos])[0]
    before = [middle_images, *[far[0] for far in far_all.values()]]
    mine = [near, middle_images, images_of(chunks[2], *shared, halos=halos, before=before)[0]]
    for shift, far in far_all.items():
        far += [from_group(cells, shift) for cells in mine[1:]]
    theirs = [from_sibling(cells) for cells in mine]
    half = half_index.astype(jnp.int32)
    goal = atom_index * groups // atom_count

    if rows_dev == modes and groups == 2:
        place = jnp.stack([half, (atom_index & 1).astype(jnp.int32)])

        def next_door(some_mine, some_theirs, after=()):
            keep, send = products_of(
                chunks, place, partners, some_mine, some_theirs, after, EARLY_US if after else LATE_US
            )
            return keep, lax.ppermute(send, "atoms", pairs)

        far = far_all[1]
        early = next_door(mine, theirs, far[:2])
        third, kept = lax.optimization_barrier((far[2], early[0]))
        early = (kept, early[1])
        far = [far[0], far[1], third]
        late = next_door(far, [from_sibling(cells) for cells in far])
        sent = jnp.where(
            group_index == goal,
            late[0] + late[1].astype(jnp.float32),
            early[0] + early[1].astype(jnp.float32),
        ).astype(jnp.bfloat16)
        swapped = lax.ppermute(sent, "atoms", [(z, z ^ 2) for z in range(atom_count)])
        early, late = [*early, swapped], [*late, swapped]
    else:

        def settled(some_mine, some_theirs, shift):
            cells = all_products(chunks, half, partners, some_mine, some_theirs)
            cells, bit = settle(cells.reshape(-1, rows_dev, part_cols), 0, rows_dev)
            return collected([cells], bit, shift)

        early, late = settled(mine, theirs, 0), None
        for shift, far in far_all.items():
            terms = settled(far, [from_sibling(cells) for cells in far], shift)
            if late is None:
                late = terms
            else:
                here = (group_index ^ shift) == goal
                late = [jnp.where(here, new, old) for new, old in zip(terms, late)]

    my_freq = lax.dynamic_slice_in_dim(panel_freq, atom_index * rows_dev, rows_dev, 0)
    flag = jnp.stack(
        [
            (group_index == goal).astype(jnp.int32),
            (column_index * part_cols).astype(jnp.int32),
            atom_index.astype(jnp.int32),
        ]
    )
    elements, numerator = finish(
        flag,
        early,
        late,
        win_start.reshape(atom_count, rows_dev),
        win_len.reshape(atom_count, rows_dev),
        panel_freq.reshape(atom_count, rows_dev),
        partner_freq[None, :],
        1.0 / math.sqrt(3 * atom_rows * atom_count),
    )
    holders = groups * 2
    sums = [numerator] + [
        lax.ppermute(numerator, ("modes", "sub"), [(i, i ^ code) for i in range(holders)])
        for code in range(1, holders)
    ]
    while len(sums) > 1:
        sums = [sums[i] + sums[i + 1] for i in range(0, len(sums), 2)]
    diffusivity = math.pi / 3.0 * sums[0][0] / (my_freq * my_freq)
    return (elements, diffusivity)


def solution(mesh):
    return jax.shard_map(
        body,
        mesh=mesh,
        in_specs=(
            P(None, ("dom", "atoms"), ("modes", "sub")),
            P(None, ("dom", "atoms"), ("modes", "sub")),
            P(None, ("dom", "atoms"), None),
            P(("dom", "atoms"), None),
            P(("dom", "atoms")),
            P("dom"),
            P(("dom", "modes", "sub")),
            P("dom"),
            P("dom"),
        ),
        out_specs=(P(("dom", "atoms"), ("modes", "sub")), P(("dom", "atoms"))),
        check_vma=False,
    )
```

```python
import math

import jax
import jax.numpy as jnp
from jax import lax
from jax.experimental import pallas as pl
from jax.experimental.pallas import tpu as pltpu
from jax.sharding import PartitionSpec as P

HALO = 96
BONDS = 16
LANES = 128
SPAN = LANES + 2 * HALO
GROUP = 16
VMEM_BYTES = 14 * 1024 * 1024

lorentz_width = 0.05

EARLY_US = 6.0
LATE_US = 0.1

HBM = pl.BlockSpec(memory_space=pltpu.HBM)
ANY = pl.BlockSpec(memory_space=pl.ANY)
VMEM = pl.BlockSpec(memory_space=pltpu.VMEM)
SMEM = pl.BlockSpec(memory_space=pltpu.SMEM)


def call(kernel, name, in_specs, out_specs, out_shape, operands, busy_us, scratch=()):
    operands = [
        pltpu.with_memory_space_constraint(x, spec.memory_space) if spec is VMEM or spec is HBM else x
        for spec, x in zip(in_specs, operands)
    ]
    return pl.pallas_call(
        kernel,
        in_specs=in_specs,
        out_specs=out_specs,
        out_shape=out_shape,
        scratch_shapes=list(scratch),
        compiler_params=pltpu.CompilerParams(vmem_limit_bytes=VMEM_BYTES),
        cost_estimate=pl.CostEstimate(
            flops=int(busy_us * 1.1e9), bytes_accessed=int(busy_us * 1e5), transcendentals=0
        ),
        name=name,
    )(*operands)


def runs_of(blocks):
    runs = []
    for place, block in enumerate(blocks):
        if runs and runs[-1][1] + runs[-1][2] == block:
            runs[-1][2] += 1
        else:
            runs.append([place, block, 1])
    return runs


def build_block(first, base, nbr_ref, coef_ref, count_ref, dense_ref):
    lanes = pl.ds(first, LANES)
    target = nbr_ref[:, lanes] - (base + (first - HALO))
    slot_ids = lax.broadcasted_iota(jnp.int32, (BONDS, LANES), 0)
    live = slot_ids < count_ref[lanes].reshape(1, LANES)
    coefs = [jnp.where(live, coef_ref[e, :, lanes], 0.0) for e in range(9)]
    halves = [(target[h : h + 8], slot_ids[h : h + 8]) for h in (0, 8)]
    merged = [[jnp.zeros((8, LANES), jnp.float32) for _ in range(9)] for _ in range(2)]
    named = [jnp.broadcast_to(target[k : k + 1], (8, LANES)) for k in range(BONDS)]
    for k in range(BONDS):
        rows = [jnp.broadcast_to(coefs[e][k : k + 1], (8, LANES)) for e in range(9)]
        for h in range(k // 8, 2):
            same = (halves[h][0] == named[k]) & (halves[h][1] >= k)
            for e in range(9):
                merged[h][e] = merged[h][e] + jnp.where(same, rows[e], 0.0)
    row_ids = lax.broadcasted_iota(jnp.int32, (8, LANES), 0)

    def group_step(g, carry):
        cells = [[] for _ in range(9)]
        for tile in range(GROUP // 8):
            here = row_ids + (g * GROUP + tile * 8)
            slot = jnp.full((8, LANES), -1, jnp.int32)
            for k in range(BONDS):
                slot = jnp.where(named[k] == here, k, slot)
            place = slot & 7
            early, live_cell = slot < 8, slot >= 0
            for e in range(9):
                picks = [
                    jnp.take_along_axis(merged[h][e], place, axis=0, mode="promise_in_bounds")
                    for h in range(2)
                ]
                cells[e].append(jnp.where(live_cell, jnp.where(early, picks[0], picks[1]), 0.0))
        for r in range(3):
            for c in range(3):
                value = jnp.concatenate(cells[3 * r + c], axis=0)
                high = value.astype(jnp.bfloat16)
                low = (value - high.astype(jnp.float32)).astype(jnp.bfloat16)
                at = pl.ds(pl.multiple_of(c * SPAN + g * GROUP, GROUP), GROUP)
                dense_ref[at, 2 * r * LANES : (2 * r + 1) * LANES] = high
                dense_ref[at, (2 * r + 1) * LANES : (2 * r + 2) * LANES] = low
        return carry

    lax.fori_loop(0, SPAN // GROUP, group_step, 0)


def images_of(blocks, spot, panel, nbr, coef, count, halos=(), before=(), edges=False):
    rows, modes = panel.shape[1:]
    loads = len(before) == 0
    operands = [spot, nbr, count, coef, panel, *halos, *before]
    in_specs = [SMEM] + [HBM if loads else VMEM] * 4 + [VMEM] * len(halos) + [ANY] * len(before)
    width = len(blocks) * LANES
    out_shape = [pltpu.VMEM((modes, 3 * width), jnp.bfloat16)]
    out_specs = [VMEM]
    if edges:
        out_shape += [jax.ShapeDtypeStruct((3, HALO, modes), jnp.bfloat16)] * 2
        out_specs += [ANY] * 2
    n_in, n_out = len(operands), len(out_shape)

    def pieces_of(block):
        begin, end = block * LANES - HALO, (block + 1) * LANES + HALO
        found = []
        if begin < 0:
            found.append((1, HALO + begin, 0, -begin))
        low, high = max(begin, 0), min(end, rows)
        found.append((0, low, low - begin, high - low))
        if end > rows:
            found.append((2, 0, rows - begin, end - rows))
        return found

    def kernel(*refs):
        spot_ref, nbr_ref, count_ref, coef_ref, panel_ref = refs[:5]
        odd = spot_ref[1]
        outs = refs[n_in : n_in + n_out]
        window_ref, dense_ref, *scratch_refs = refs[n_in + n_out :]
        window_copies = []
        if loads:
            sources = (nbr_ref, count_ref, coef_ref)
            nbr_ref, count_ref, coef_ref, sems = scratch_refs
            copies = []

            def start(source, target, kept):
                copy = pltpu.make_async_copy(source, target, sems.at[len(copies) + len(window_copies)])
                copy.start()
                kept.append(copy)

            start(sources[0], nbr_ref, copies)
            start(sources[1], count_ref, copies)
            for _, block, length in runs_of(blocks):
                at = pl.ds(block * LANES, length * LANES)
                start(sources[2].at[:, :, at], coef_ref.at[:, :, at], copies)
            for place, block in enumerate(blocks):
                for _, source, at, length in pieces_of(block):
                    start(
                        panel_ref.at[:, pl.ds(source, length)], window_ref.at[place, :, pl.ds(at, length)], window_copies
                    )
            if edges:
                for turn, out in enumerate(outs[1:3]):
                    at = pl.multiple_of(jnp.where(odd == turn, rows - HALO, 0), 32)
                    start(panel_ref.at[:, pl.ds(at, HALO)], out, window_copies)
            for copy in copies:
                copy.wait()
        else:
            for place, block in enumerate(blocks):
                for which, source, at, length in pieces_of(block):
                    there = slice(source, source + length)
                    if which == 0:
                        found = panel_ref[:, there, :]
                    else:
                        found = jnp.where((odd == 1) == (which == 1), refs[5][:, there, :], refs[6][:, there, :])
                    window_ref[place, :, at : at + length, :] = found

        for place, block in enumerate(blocks):
            build_block(block * LANES, spot_ref[0], nbr_ref, coef_ref, count_ref, dense_ref)
            if loads and place == 0:
                for copy in window_copies:
                    copy.wait()
            both = lax.dot_general(
                window_ref[place].reshape(3 * SPAN, modes),
                dense_ref[...],
                (((0,), (0,)), ((), ())),
                preferred_element_type=jnp.float32,
            )
            for r in range(3):
                image = both[:, 2 * r * LANES : (2 * r + 1) * LANES]
                image = image + both[:, (2 * r + 1) * LANES : (2 * r + 2) * LANES]
                at = r * width + place * LANES
                outs[0][:, at : at + LANES] = image.astype(jnp.bfloat16)

    scratch = [
        pltpu.VMEM((len(blocks), 3, SPAN, modes), jnp.bfloat16),
        pltpu.VMEM((3 * SPAN, 6 * LANES), jnp.bfloat16),
    ]
    if loads:
        scratch += [
            pltpu.VMEM((BONDS, rows), jnp.int32),
            pltpu.VMEM((rows,), jnp.int32),
            pltpu.VMEM((9, BONDS, rows), jnp.float32),
            pltpu.SemaphoreType.DMA((4 + 3 * len(blocks) + 2,)),
        ]
    return call(kernel, "images", in_specs, out_specs, out_shape, operands, 0.8 + 1.2 * len(blocks), scratch)


def products_of(chunks, place, partners, mine, theirs, after=(), busy_us=2.0, parts=1):
    rows, cols = mine[0].shape[0], partners.shape[2]
    count = len(chunks)
    depth = partners.shape[1]

    def kernel(place_ref, partners_hbm, *refs):
        keep_ref, *send_refs = refs[-4 - parts : -3]
        left_ref, partners_ref, sems = refs[-3:]
        copies = [
            pltpu.make_async_copy(partners_hbm.at[r], partners_ref.at[r], sems.at[r]) for r in range(3)
        ]
        for copy in copies:
            copy.start()
        kept = place_ref[0] == place_ref[1]
        for who in range(2):
            at_rows = pl.ds(pl.multiple_of(jnp.where(kept == (who == 0), 0, rows), rows), rows)
            for i, blocks in enumerate(chunks):
                image_ref = refs[who * count + i]
                width = len(blocks) * LANES
                for r in range(3):
                    for spot, block, length in runs_of(blocks):
                        at, to = r * width + spot * LANES, r * depth + block * LANES
                        left_ref[at_rows, to : to + length * LANES] = image_ref[:, at : at + length * LANES]
        total = None
        for r, copy in enumerate(copies):
            copy.wait()
            part = jnp.dot(
                left_ref[:, r * depth : (r + 1) * depth], partners_ref[r], preferred_element_type=jnp.float32
            )
            total = part if total is None else total + part
        keep_ref[...] = total[:rows]
        for part, send_ref in enumerate(send_refs):
            at = rows + part * (rows // parts)
            send_ref[...] = total[at : at + rows // parts].astype(jnp.bfloat16)

    return call(
        kernel,
        "products",
        [SMEM, HBM] + [VMEM] * (2 * count) + [ANY] * len(after),
        [VMEM] * (1 + parts),
        [pltpu.VMEM((rows, cols), jnp.float32)] + [pltpu.VMEM((rows // parts, cols), jnp.bfloat16)] * parts,
        (place, partners, *mine, *theirs, *after),
        busy_us,
        [
            pltpu.VMEM((2 * rows, 3 * depth), jnp.bfloat16),
            pltpu.VMEM((3, depth, cols), jnp.bfloat16),
            pltpu.SemaphoreType.DMA((3,)),
        ],
    )


def all_products(chunks, half, partners, mine, theirs):
    place = jnp.stack([half, jnp.zeros((), jnp.int32)])
    low = products_of(chunks, place, partners, mine, theirs)[0]
    high = products_of(chunks, place + jnp.array([0, 1], jnp.int32), partners, mine, theirs)[0]
    return jnp.stack([low, high])


def settle(cells, bit, rows_dev):
    depth = lax.axis_size("atoms")
    place = lax.axis_index("atoms")
    while cells.shape[0] > 1:
        pairs = cells.reshape(cells.shape[0] // 2, 2, rows_dev, -1)
        own = (place >> bit) & 1
        keep = lax.dynamic_index_in_dim(pairs, own, 1, keepdims=False)
        send = lax.dynamic_index_in_dim(pairs, 1 - own, 1, keepdims=False)
        step = 1 << bit
        got = lax.ppermute(send.astype(jnp.bfloat16), "atoms", [(z, z ^ step) for z in range(depth)])
        cells = keep + got.astype(jnp.float32)
        bit += 1
    return cells[0], bit


def collected(terms, bit, shift):
    groups, depth = lax.axis_size("modes"), lax.axis_size("atoms")
    level = 0
    while (1 << level) < groups:
        moves = []
        for z in range(depth):
            for m in range(groups):
                goal = m ^ shift
                settled = all(((z >> (bit + u)) ^ (goal >> u)) & 1 == 0 for u in range(level))
                if settled and ((z >> (bit + level)) ^ (goal >> level)) & 1:
                    moves.append((z * groups + m, (z ^ (1 << (bit + level))) * groups + m))
        sent = sum(term.astype(jnp.float32) for term in terms).astype(jnp.bfloat16)
        terms = terms + [lax.ppermute(sent, ("atoms", "modes"), moves)]
        level += 1
    return terms


def finish(flag, early, late, starts, lengths, freqs, partner_freq, norm_scale):
    rows, cols = early[0][0].shape
    terms = early + late
    operands = [flag, starts, lengths, freqs, partner_freq, *[piece for term in terms for piece in term]]
    step = 16

    def kernel(flag_ref, starts_ref, lengths_ref, freqs_ref, partner_ref, *refs):
        out_ref, sum_ref, start_ref, end_ref, freq_ref, folded_ref = refs[-6:]
        pieces = iter(refs[:-6])
        grouped = [[next(pieces) for _ in term] for term in terms]

        def add_up(some):
            out_ref[...] = some[0][0][...]
            for term in some[1:]:
                span = rows // len(term)
                for i, ref in enumerate(term):
                    at = slice(i * span, (i + 1) * span)
                    out_ref[at, :] = out_ref[at, :] + ref[...].astype(jnp.float32)

        @pl.when(flag_ref[0] == 1)
        def _():
            add_up(grouped[: len(early)])

        @pl.when(flag_ref[0] == 0)
        def _():
            add_up(grouped[len(early) :])

        def turned(row):
            return jnp.broadcast_to(row, (LANES, rows)).T

        mine = pl.ds(flag_ref[2], 1)
        start_row = starts_ref[mine, :].astype(jnp.float32)
        start_ref[...] = turned(start_row)
        end_ref[...] = turned(start_row + lengths_ref[mine, :].astype(jnp.float32))
        freq_ref[...] = turned(freqs_ref[mine, :])
        lane_ids = lax.broadcasted_iota(jnp.int32, (step, LANES), 1)

        def row_step(i, carry):
            at_rows = pl.ds(pl.multiple_of(i * step, step), step)
            start, end, freq = start_ref[at_rows, :], end_ref[at_rows, :], freq_ref[at_rows, :]
            folded = jnp.zeros((step, LANES), jnp.float32)
            for at in range(0, cols, LANES):
                columns = (lane_ids + (flag_ref[1] + at)).astype(jnp.float32)
                inside = (columns >= start) & (columns < end)
                elements = jnp.where(inside, out_ref[at_rows, at : at + LANES] * norm_scale, 0.0)
                out_ref[at_rows, at : at + LANES] = elements
                offset = freq - partner_ref[:, at : at + LANES]
                lorentz = lorentz_width / (math.pi * (offset * offset + lorentz_width * lorentz_width))
                folded = folded + jnp.where(inside, lorentz, 0.0) * elements * elements
            folded_ref[at_rows, :] = folded
            return carry

        lax.fori_loop(0, rows // step, row_step, 0)
        sum_ref[...] = jnp.sum(folded_ref[...].T, axis=0, keepdims=True)

    return call(
        kernel,
        "finish",
        [SMEM] + [VMEM] * (len(operands) - 1),
        [VMEM, VMEM],
        [jax.ShapeDtypeStruct((rows, cols), jnp.float32), jax.ShapeDtypeStruct((1, rows), jnp.float32)],
        operands,
        2.0,
        [pltpu.VMEM((rows, LANES), jnp.float32)] * 4,
    )


def body(
    mode_panel,
    partners,
    bond_blocks,
    neighbors,
    bond_count,
    panel_freq,
    partner_freq,
    win_start,
    win_len,
):
    atom_rows, modes = mode_panel.shape[1:]
    atom_index = lax.axis_index("atoms")
    atom_count = lax.axis_size("atoms")
    groups = lax.axis_size("modes")
    group_index = lax.axis_index("modes")
    half_index = lax.axis_index("sub")
    column_index = lax.axis_index(("modes", "sub"))
    part_cols = partners.shape[2]
    panel_total = win_start.shape[0]
    rows_dev = panel_total // atom_count

    nbr = neighbors.T
    coef = bond_blocks.transpose(0, 2, 1)
    spot = jnp.stack([(atom_index * atom_rows).astype(jnp.int32), (atom_index & 1).astype(jnp.int32)])

    last = atom_rows // LANES - 1
    middle = list(range(1, last))
    cut = len(middle) // 2
    chunks = [middle[:cut], middle[cut:], [last, 0]]
    shared = (spot, mode_panel, nbr, coef, bond_count)
    near, edge_one, edge_two = images_of(chunks[0], *shared, edges=True)
    pairs = [(z, z ^ 1) for z in range(atom_count)]
    others = [(z, ((z + 1) ^ 1) - 1) for z in range(1, atom_count - 1)]
    halos = (lax.ppermute(edge_one, "atoms", pairs), lax.ppermute(edge_two, "atoms", others))

    def from_group(cells, shift):
        return lax.ppermute(cells, "modes", [(m ^ shift, m) for m in range(groups)])

    def from_sibling(cells):
        return lax.ppermute(cells, "sub", [(0, 1), (1, 0)])

    far_all = {shift: [from_group(near, shift)] for shift in range(1, groups)}
    middle_images = images_of(chunks[1], *shared, before=[near])[0]
    before = [middle_images, *[far[0] for far in far_all.values()]]
    mine = [near, middle_images, images_of(chunks[2], *shared, halos=halos, before=before)[0]]
    for shift, far in far_all.items():
        far += [from_group(cells, shift) for cells in mine[1:]]
    theirs = [from_sibling(cells) for cells in mine]
    half = half_index.astype(jnp.int32)
    goal = atom_index * groups // atom_count

    if rows_dev == modes and groups == 2:
        place = jnp.stack([half, (atom_index & 1).astype(jnp.int32)])

        def next_door(some_mine, some_theirs, after=(), parts=1):
            keep, *sends = products_of(
                chunks, place, partners, some_mine, some_theirs, after, EARLY_US if after else LATE_US, parts
            )
            return keep, [lax.ppermute(send, "atoms", pairs) for send in sends]

        far = far_all[1]
        early = next_door(mine, theirs, far[:2])
        third, kept = lax.optimization_barrier((far[2], early[0]))
        early = (kept, early[1])
        far = [far[0], far[1], third]
        parts = 2
        span = modes // parts
        late = next_door(far, [from_sibling(cells) for cells in far], parts=parts)
        swapped = []
        for part, got in enumerate(late[1]):
            at = slice(part * span, (part + 1) * span)
            if part:
                got, _ = lax.optimization_barrier((got, sent))
            sent = jnp.where(
                group_index == goal,
                late[0][at] + got.astype(jnp.float32),
                early[0][at] + early[1][0][at].astype(jnp.float32),
            ).astype(jnp.bfloat16)
            swapped.append(lax.ppermute(sent, "atoms", [(z, z ^ 2) for z in range(atom_count)]))
        early, late = [[early[0]], early[1], swapped], [[late[0]], late[1], swapped]
    else:

        def settled(some_mine, some_theirs, shift):
            cells = all_products(chunks, half, partners, some_mine, some_theirs)
            cells, bit = settle(cells.reshape(-1, rows_dev, part_cols), 0, rows_dev)
            return collected([cells], bit, shift)

        early, late = settled(mine, theirs, 0), None
        for shift, far in far_all.items():
            terms = settled(far, [from_sibling(cells) for cells in far], shift)
            if late is None:
                late = terms
            else:
                here = (group_index ^ shift) == goal
                late = [jnp.where(here, new, old) for new, old in zip(terms, late)]
        early, late = [[term] for term in early], [[term] for term in late]

    my_freq = lax.dynamic_slice_in_dim(panel_freq, atom_index * rows_dev, rows_dev, 0)
    flag = jnp.stack(
        [
            (group_index == goal).astype(jnp.int32),
            (column_index * part_cols).astype(jnp.int32),
            atom_index.astype(jnp.int32),
        ]
    )
    elements, numerator = finish(
        flag,
        early,
        late,
        win_start.reshape(atom_count, rows_dev),
        win_len.reshape(atom_count, rows_dev),
        panel_freq.reshape(atom_count, rows_dev),
        partner_freq[None, :],
        1.0 / math.sqrt(3 * atom_rows * atom_count),
    )
    numerator = numerator + lax.ppermute(numerator, "sub", [(0, 1), (1, 0)])
    step = 1
    while step < groups:
        numerator = numerator + lax.ppermute(numerator, "modes", [(m, m ^ step) for m in range(groups)])
        step *= 2
    diffusivity = math.pi / 3.0 * numerator[0] / (my_freq * my_freq)
    return (elements, diffusivity)


def solution(mesh):
    return jax.shard_map(
        body,
        mesh=mesh,
        in_specs=(
            P(None, ("dom", "atoms"), ("modes", "sub")),
            P(None, ("dom", "atoms"), ("modes", "sub")),
            P(None, ("dom", "atoms"), None),
            P(("dom", "atoms"), None),
            P(("dom", "atoms")),
            P("dom"),
            P(("dom", "modes", "sub")),
            P("dom"),
            P("dom"),
        ),
        out_specs=(P(("dom", "atoms"), ("modes", "sub")), P(("dom", "atoms"))),
        check_vma=False,
    )
```

```python
import math

import jax
import jax.numpy as jnp
from jax import lax
from jax.experimental import pallas as pl
from jax.experimental.pallas import tpu as pltpu
from jax.sharding import PartitionSpec as P

HALO = 96
BONDS = 16
LANES = 128
SPAN = LANES + 2 * HALO
GROUP = 16
VMEM_BYTES = 14 * 1024 * 1024

lorentz_width = 0.05

EARLY_US = 6.0
LATE_US = 0.1

HBM = pl.BlockSpec(memory_space=pltpu.HBM)
ANY = pl.BlockSpec(memory_space=pl.ANY)
VMEM = pl.BlockSpec(memory_space=pltpu.VMEM)
SMEM = pl.BlockSpec(memory_space=pltpu.SMEM)


def call(kernel, name, in_specs, out_specs, out_shape, operands, busy_us, scratch=()):
    operands = [
        pltpu.with_memory_space_constraint(x, spec.memory_space) if spec is VMEM or spec is HBM else x
        for spec, x in zip(in_specs, operands)
    ]
    return pl.pallas_call(
        kernel,
        in_specs=in_specs,
        out_specs=out_specs,
        out_shape=out_shape,
        scratch_shapes=list(scratch),
        compiler_params=pltpu.CompilerParams(vmem_limit_bytes=VMEM_BYTES),
        cost_estimate=pl.CostEstimate(
            flops=int(busy_us * 1.1e9), bytes_accessed=int(busy_us * 1e5), transcendentals=0
        ),
        name=name,
    )(*operands)


def runs_of(blocks):
    runs = []
    for place, block in enumerate(blocks):
        if runs and runs[-1][1] + runs[-1][2] == block:
            runs[-1][2] += 1
        else:
            runs.append([place, block, 1])
    return runs


def build_block(first, base, nbr_ref, coef_ref, count_ref, dense_ref):
    lanes = pl.ds(first, LANES)
    target = nbr_ref[:, lanes] - (base + (first - HALO))
    slot_ids = lax.broadcasted_iota(jnp.int32, (BONDS, LANES), 0)
    live = slot_ids < count_ref[lanes].reshape(1, LANES)
    coefs = [jnp.where(live, coef_ref[e, :, lanes], 0.0) for e in range(9)]
    halves = [(target[h : h + 8], slot_ids[h : h + 8]) for h in (0, 8)]
    merged = [[jnp.zeros((8, LANES), jnp.float32) for _ in range(9)] for _ in range(2)]
    named = [jnp.broadcast_to(target[k : k + 1], (8, LANES)) for k in range(BONDS)]
    for k in range(BONDS):
        rows = [jnp.broadcast_to(coefs[e][k : k + 1], (8, LANES)) for e in range(9)]
        for h in range(k // 8, 2):
            same = (halves[h][0] == named[k]) & (halves[h][1] >= k)
            for e in range(9):
                merged[h][e] = merged[h][e] + jnp.where(same, rows[e], 0.0)
    row_ids = lax.broadcasted_iota(jnp.int32, (8, LANES), 0)

    def group_step(g, carry):
        cells = [[] for _ in range(9)]
        for tile in range(GROUP // 8):
            here = row_ids + (g * GROUP + tile * 8)
            slot = jnp.full((8, LANES), -1, jnp.int32)
            for k in range(BONDS):
                slot = jnp.where(named[k] == here, k, slot)
            place = slot & 7
            early, live_cell = slot < 8, slot >= 0
            for e in range(9):
                picks = [
                    jnp.take_along_axis(merged[h][e], place, axis=0, mode="promise_in_bounds")
                    for h in range(2)
                ]
                cells[e].append(jnp.where(live_cell, jnp.where(early, picks[0], picks[1]), 0.0))
        for r in range(3):
            for c in range(3):
                value = jnp.concatenate(cells[3 * r + c], axis=0)
                high = value.astype(jnp.bfloat16)
                low = (value - high.astype(jnp.float32)).astype(jnp.bfloat16)
                at = pl.ds(pl.multiple_of(c * SPAN + g * GROUP, GROUP), GROUP)
                dense_ref[at, 2 * r * LANES : (2 * r + 1) * LANES] = high
                dense_ref[at, (2 * r + 1) * LANES : (2 * r + 2) * LANES] = low
        return carry

    lax.fori_loop(0, SPAN // GROUP, group_step, 0)


def images_of(blocks, spot, panel, nbr, coef, count, halos=(), before=(), edges=False):
    rows, modes = panel.shape[1:]
    loads = len(before) == 0
    operands = [spot, nbr, count, coef, panel, *halos, *before]
    in_specs = [SMEM] + [HBM if loads else VMEM] * 4 + [VMEM] * len(halos) + [ANY] * len(before)
    width = len(blocks) * LANES
    out_shape = [pltpu.VMEM((modes, 3 * width), jnp.bfloat16)]
    out_specs = [VMEM]
    if edges:
        out_shape += [jax.ShapeDtypeStruct((3, HALO, modes), jnp.bfloat16)] * 2
        out_specs += [ANY] * 2
    n_in, n_out = len(operands), len(out_shape)

    def pieces_of(block):
        begin, end = block * LANES - HALO, (block + 1) * LANES + HALO
        found = []
        if begin < 0:
            found.append((1, HALO + begin, 0, -begin))
        low, high = max(begin, 0), min(end, rows)
        found.append((0, low, low - begin, high - low))
        if end > rows:
            found.append((2, 0, rows - begin, end - rows))
        return found

    def kernel(*refs):
        spot_ref, nbr_ref, count_ref, coef_ref, panel_ref = refs[:5]
        odd = spot_ref[1]
        outs = refs[n_in : n_in + n_out]
        window_ref, dense_ref, *scratch_refs = refs[n_in + n_out :]
        window_copies = []
        if loads:
            sources = (nbr_ref, count_ref, coef_ref)
            nbr_ref, count_ref, coef_ref, sems = scratch_refs
            copies = []

            def start(source, target, kept):
                copy = pltpu.make_async_copy(source, target, sems.at[len(copies) + len(window_copies)])
                copy.start()
                kept.append(copy)

            start(sources[0], nbr_ref, copies)
            start(sources[1], count_ref, copies)
            for _, block, length in runs_of(blocks):
                at = pl.ds(block * LANES, length * LANES)
                start(sources[2].at[:, :, at], coef_ref.at[:, :, at], copies)
            for place, block in enumerate(blocks):
                for _, source, at, length in pieces_of(block):
                    start(
                        panel_ref.at[:, pl.ds(source, length)], window_ref.at[place, :, pl.ds(at, length)], window_copies
                    )
            if edges:
                for turn, out in enumerate(outs[1:3]):
                    at = pl.multiple_of(jnp.where(odd == turn, rows - HALO, 0), 32)
                    start(panel_ref.at[:, pl.ds(at, HALO)], out, window_copies)
            for copy in copies:
                copy.wait()
        else:
            for place, block in enumerate(blocks):
                for which, source, at, length in pieces_of(block):
                    there = slice(source, source + length)
                    if which == 0:
                        found = panel_ref[:, there, :]
                    else:
                        found = jnp.where((odd == 1) == (which == 1), refs[5][:, there, :], refs[6][:, there, :])
                    window_ref[place, :, at : at + length, :] = found

        for place, block in enumerate(blocks):
            build_block(block * LANES, spot_ref[0], nbr_ref, coef_ref, count_ref, dense_ref)
            if loads and place == 0:
                for copy in window_copies:
                    copy.wait()
            both = lax.dot_general(
                window_ref[place].reshape(3 * SPAN, modes),
                dense_ref[...],
                (((0,), (0,)), ((), ())),
                preferred_element_type=jnp.float32,
            )
            for r in range(3):
                image = both[:, 2 * r * LANES : (2 * r + 1) * LANES]
                image = image + both[:, (2 * r + 1) * LANES : (2 * r + 2) * LANES]
                at = r * width + place * LANES
                outs[0][:, at : at + LANES] = image.astype(jnp.bfloat16)

    scratch = [
        pltpu.VMEM((len(blocks), 3, SPAN, modes), jnp.bfloat16),
        pltpu.VMEM((3 * SPAN, 6 * LANES), jnp.bfloat16),
    ]
    if loads:
        scratch += [
            pltpu.VMEM((BONDS, rows), jnp.int32),
            pltpu.VMEM((rows,), jnp.int32),
            pltpu.VMEM((9, BONDS, rows), jnp.float32),
            pltpu.SemaphoreType.DMA((4 + 3 * len(blocks) + 2,)),
        ]
    return call(kernel, "images", in_specs, out_specs, out_shape, operands, 0.8 + 1.2 * len(blocks), scratch)


def products_of(chunks, place, partners, mine, theirs, after=(), busy_us=2.0, parts=1):
    rows, cols = mine[0].shape[0], partners.shape[2]
    count = len(chunks)
    depth = partners.shape[1]

    def kernel(place_ref, partners_hbm, *refs):
        keep_ref, *send_refs = refs[-4 - parts : -3]
        left_ref, partners_ref, sems = refs[-3:]
        copies = [
            pltpu.make_async_copy(partners_hbm.at[r], partners_ref.at[r], sems.at[r]) for r in range(3)
        ]
        for copy in copies:
            copy.start()
        kept = place_ref[0] == place_ref[1]
        for who in range(2):
            at_rows = pl.ds(pl.multiple_of(jnp.where(kept == (who == 0), 0, rows), rows), rows)
            for i, blocks in enumerate(chunks):
                image_ref = refs[who * count + i]
                width = len(blocks) * LANES
                for r in range(3):
                    for spot, block, length in runs_of(blocks):
                        at, to = r * width + spot * LANES, r * depth + block * LANES
                        left_ref[at_rows, to : to + length * LANES] = image_ref[:, at : at + length * LANES]
        total = None
        for r, copy in enumerate(copies):
            copy.wait()
            part = jnp.dot(
                left_ref[:, r * depth : (r + 1) * depth], partners_ref[r], preferred_element_type=jnp.float32
            )
            total = part if total is None else total + part
        keep_ref[...] = total[:rows]
        for part, send_ref in enumerate(send_refs):
            at = rows + part * (rows // parts)
            send_ref[...] = total[at : at + rows // parts].astype(jnp.bfloat16)

    return call(
        kernel,
        "products",
        [SMEM, HBM] + [VMEM] * (2 * count) + [ANY] * len(after),
        [VMEM] * (1 + parts),
        [pltpu.VMEM((rows, cols), jnp.float32)] + [pltpu.VMEM((rows // parts, cols), jnp.bfloat16)] * parts,
        (place, partners, *mine, *theirs, *after),
        busy_us,
        [
            pltpu.VMEM((2 * rows, 3 * depth), jnp.bfloat16),
            pltpu.VMEM((3, depth, cols), jnp.bfloat16),
            pltpu.SemaphoreType.DMA((3,)),
        ],
    )


def all_products(chunks, half, partners, mine, theirs):
    place = jnp.stack([half, jnp.zeros((), jnp.int32)])
    low = products_of(chunks, place, partners, mine, theirs)[0]
    high = products_of(chunks, place + jnp.array([0, 1], jnp.int32), partners, mine, theirs)[0]
    return jnp.stack([low, high])


def settle(cells, bit, rows_dev):
    depth = lax.axis_size("atoms")
    place = lax.axis_index("atoms")
    while cells.shape[0] > 1:
        pairs = cells.reshape(cells.shape[0] // 2, 2, rows_dev, -1)
        own = (place >> bit) & 1
        keep = lax.dynamic_index_in_dim(pairs, own, 1, keepdims=False)
        send = lax.dynamic_index_in_dim(pairs, 1 - own, 1, keepdims=False)
        step = 1 << bit
        got = lax.ppermute(send.astype(jnp.bfloat16), "atoms", [(z, z ^ step) for z in range(depth)])
        cells = keep + got.astype(jnp.float32)
        bit += 1
    return cells[0], bit


def collected(terms, bit, shift):
    groups, depth = lax.axis_size("modes"), lax.axis_size("atoms")
    level = 0
    while (1 << level) < groups:
        moves = []
        for z in range(depth):
            for m in range(groups):
                goal = m ^ shift
                settled = all(((z >> (bit + u)) ^ (goal >> u)) & 1 == 0 for u in range(level))
                if settled and ((z >> (bit + level)) ^ (goal >> level)) & 1:
                    moves.append((z * groups + m, (z ^ (1 << (bit + level))) * groups + m))
        sent = sum(term.astype(jnp.float32) for term in terms).astype(jnp.bfloat16)
        terms = terms + [lax.ppermute(sent, ("atoms", "modes"), moves)]
        level += 1
    return terms


def finish(flag, early, late, starts, lengths, freqs, partner_freq, norm_scale):
    rows, cols = early[0][0].shape
    terms = early + late
    operands = [flag, starts, lengths, freqs, partner_freq, *[piece for term in terms for piece in term]]
    step = 16

    def kernel(flag_ref, starts_ref, lengths_ref, freqs_ref, partner_ref, *refs):
        out_ref, sum_ref, start_ref, end_ref, freq_ref, folded_ref = refs[-6:]
        pieces = iter(refs[:-6])
        grouped = [[next(pieces) for _ in term] for term in terms]

        def add_up(some):
            out_ref[...] = some[0][0][...]
            for term in some[1:]:
                span = rows // len(term)
                for i, ref in enumerate(term):
                    at = slice(i * span, (i + 1) * span)
                    out_ref[at, :] = out_ref[at, :] + ref[...].astype(jnp.float32)

        @pl.when(flag_ref[0] == 1)
        def _():
            add_up(grouped[: len(early)])

        @pl.when(flag_ref[0] == 0)
        def _():
            add_up(grouped[len(early) :])

        def turned(row):
            return jnp.broadcast_to(row, (LANES, rows)).T

        mine = pl.ds(flag_ref[2], 1)
        start_row = starts_ref[mine, :].astype(jnp.float32)
        start_ref[...] = turned(start_row)
        end_ref[...] = turned(start_row + lengths_ref[mine, :].astype(jnp.float32))
        freq_ref[...] = turned(freqs_ref[mine, :])
        lane_ids = lax.broadcasted_iota(jnp.int32, (step, LANES), 1)

        def row_step(i, carry):
            at_rows = pl.ds(pl.multiple_of(i * step, step), step)
            start, end, freq = start_ref[at_rows, :], end_ref[at_rows, :], freq_ref[at_rows, :]
            folded = jnp.zeros((step, LANES), jnp.float32)
            for at in range(0, cols, LANES):
                columns = (lane_ids + (flag_ref[1] + at)).astype(jnp.float32)
                inside = (columns >= start) & (columns < end)
                elements = jnp.where(inside, out_ref[at_rows, at : at + LANES] * norm_scale, 0.0)
                out_ref[at_rows, at : at + LANES] = elements
                offset = freq - partner_ref[:, at : at + LANES]
                lorentz = lorentz_width / (math.pi * (offset * offset + lorentz_width * lorentz_width))
                folded = folded + jnp.where(inside, lorentz, 0.0) * elements * elements
            folded_ref[at_rows, :] = folded
            return carry

        lax.fori_loop(0, rows // step, row_step, 0)
        sum_ref[...] = jnp.sum(folded_ref[...].T, axis=0, keepdims=True)

    return call(
        kernel,
        "finish",
        [SMEM] + [VMEM] * (len(operands) - 1),
        [VMEM, VMEM],
        [jax.ShapeDtypeStruct((rows, cols), jnp.float32), jax.ShapeDtypeStruct((1, rows), jnp.float32)],
        operands,
        2.0,
        [pltpu.VMEM((rows, LANES), jnp.float32)] * 4,
    )


def body(
    mode_panel,
    partners,
    bond_blocks,
    neighbors,
    bond_count,
    panel_freq,
    partner_freq,
    win_start,
    win_len,
):
    atom_rows, modes = mode_panel.shape[1:]
    atom_index = lax.axis_index("atoms")
    atom_count = lax.axis_size("atoms")
    groups = lax.axis_size("modes")
    group_index = lax.axis_index("modes")
    half_index = lax.axis_index("sub")
    column_index = lax.axis_index(("modes", "sub"))
    part_cols = partners.shape[2]
    panel_total = win_start.shape[0]
    rows_dev = panel_total // atom_count

    nbr = neighbors.T
    coef = bond_blocks.transpose(0, 2, 1)
    spot = jnp.stack([(atom_index * atom_rows).astype(jnp.int32), (atom_index & 1).astype(jnp.int32)])

    last = atom_rows // LANES - 1
    middle = list(range(1, last))
    cut = len(middle) // 2
    chunks = [middle[:cut], middle[cut:], [last, 0]]
    shared = (spot, mode_panel, nbr, coef, bond_count)
    near, edge_one, edge_two = images_of(chunks[0], *shared, edges=True)
    pairs = [(z, z ^ 1) for z in range(atom_count)]
    others = [(z, (z + 1 if z & 1 else z - 1) % atom_count) for z in range(atom_count)]
    halos = (lax.ppermute(edge_one, "atoms", pairs), lax.ppermute(edge_two, "atoms", others))

    def from_group(cells, shift):
        return lax.ppermute(cells, "modes", [(m ^ shift, m) for m in range(groups)])

    def from_sibling(cells):
        return lax.ppermute(cells, "sub", [(0, 1), (1, 0)])

    far_all = {shift: [from_group(near, shift)] for shift in range(1, groups)}
    middle_images = images_of(chunks[1], *shared, before=[near])[0]
    before = [middle_images, *[far[0] for far in far_all.values()]]
    mine = [near, middle_images, images_of(chunks[2], *shared, halos=halos, before=before)[0]]
    for shift, far in far_all.items():
        far += [from_group(cells, shift) for cells in mine[1:]]
    theirs = [from_sibling(cells) for cells in mine]
    half = half_index.astype(jnp.int32)
    goal = atom_index * groups // atom_count

    if rows_dev == modes and groups == 2:
        place = jnp.stack([half, (atom_index & 1).astype(jnp.int32)])

        def next_door(some_mine, some_theirs, after=(), parts=1):
            keep, *sends = products_of(
                chunks, place, partners, some_mine, some_theirs, after, EARLY_US if after else LATE_US, parts
            )
            return keep, [lax.ppermute(send, "atoms", pairs) for send in sends]

        far = far_all[1]
        early = next_door(mine, theirs, far[:2])
        third, kept = lax.optimization_barrier((far[2], early[0]))
        early = (kept, early[1])
        far = [far[0], far[1], third]
        parts = 2
        span = modes // parts
        late = next_door(far, [from_sibling(cells) for cells in far], parts=parts)
        swapped = []
        for part, got in enumerate(late[1]):
            at = slice(part * span, (part + 1) * span)
            if part:
                got, _ = lax.optimization_barrier((got, sent))
            sent = jnp.where(
                group_index == goal,
                late[0][at] + got.astype(jnp.float32),
                early[0][at] + early[1][0][at].astype(jnp.float32),
            ).astype(jnp.bfloat16)
            swapped.append(lax.ppermute(sent, "atoms", [(z, z ^ 2) for z in range(atom_count)]))
        early, late = [[early[0]], early[1], swapped], [[late[0]], late[1], swapped]
    else:

        def settled(some_mine, some_theirs, shift):
            cells = all_products(chunks, half, partners, some_mine, some_theirs)
            cells, bit = settle(cells.reshape(-1, rows_dev, part_cols), 0, rows_dev)
            return collected([cells], bit, shift)

        early, late = settled(mine, theirs, 0), None
        for shift, far in far_all.items():
            terms = settled(far, [from_sibling(cells) for cells in far], shift)
            if late is None:
                late = terms
            else:
                here = (group_index ^ shift) == goal
                late = [jnp.where(here, new, old) for new, old in zip(terms, late)]
        early, late = [[term] for term in early], [[term] for term in late]

    my_freq = lax.dynamic_slice_in_dim(panel_freq, atom_index * rows_dev, rows_dev, 0)
    flag = jnp.stack(
        [
            (group_index == goal).astype(jnp.int32),
            (column_index * part_cols).astype(jnp.int32),
            atom_index.astype(jnp.int32),
        ]
    )
    elements, numerator = finish(
        flag,
        early,
        late,
        win_start.reshape(atom_count, rows_dev),
        win_len.reshape(atom_count, rows_dev),
        panel_freq.reshape(atom_count, rows_dev),
        partner_freq[None, :],
        1.0 / math.sqrt(3 * atom_rows * atom_count),
    )
    numerator = numerator + lax.ppermute(numerator, "sub", [(0, 1), (1, 0)])
    step = 1
    while step < groups:
        numerator = numerator + lax.ppermute(numerator, "modes", [(m, m ^ step) for m in range(groups)])
        step *= 2
    diffusivity = math.pi / 3.0 * numerator[0] / (my_freq * my_freq)
    return (elements, diffusivity)


def solution(mesh):
    return jax.shard_map(
        body,
        mesh=mesh,
        in_specs=(
            P(None, ("dom", "atoms"), ("modes", "sub")),
            P(None, ("dom", "atoms"), ("modes", "sub")),
            P(None, ("dom", "atoms"), None),
            P(("dom", "atoms"), None),
            P(("dom", "atoms")),
            P("dom"),
            P(("dom", "modes", "sub")),
            P("dom"),
            P("dom"),
        ),
        out_specs=(P(("dom", "atoms"), ("modes", "sub")), P(("dom", "atoms"))),
        check_vma=False,
    )
```

```python
import math

import jax
import jax.numpy as jnp
from jax import lax
from jax.experimental import pallas as pl
from jax.experimental.pallas import tpu as pltpu
from jax.sharding import PartitionSpec as P

HALO = 96
BONDS = 16
LANES = 128
SPAN = LANES + 2 * HALO
GROUP = 16
VMEM_BYTES = 14 * 1024 * 1024

lorentz_width = 0.05

EARLY_US = 6.0
LATE_US = 0.1

HBM = pl.BlockSpec(memory_space=pltpu.HBM)
ANY = pl.BlockSpec(memory_space=pl.ANY)
VMEM = pl.BlockSpec(memory_space=pltpu.VMEM)
SMEM = pl.BlockSpec(memory_space=pltpu.SMEM)


def call(kernel, name, in_specs, out_specs, out_shape, operands, busy_us, scratch=()):
    operands = [
        pltpu.with_memory_space_constraint(x, spec.memory_space) if spec is VMEM or spec is HBM else x
        for spec, x in zip(in_specs, operands)
    ]
    return pl.pallas_call(
        kernel,
        in_specs=in_specs,
        out_specs=out_specs,
        out_shape=out_shape,
        scratch_shapes=list(scratch),
        compiler_params=pltpu.CompilerParams(vmem_limit_bytes=VMEM_BYTES),
        cost_estimate=pl.CostEstimate(
            flops=int(busy_us * 1.1e9), bytes_accessed=int(busy_us * 1e5), transcendentals=0
        ),
        name=name,
    )(*operands)


def runs_of(blocks):
    runs = []
    for place, block in enumerate(blocks):
        if runs and runs[-1][1] + runs[-1][2] == block:
            runs[-1][2] += 1
        else:
            runs.append([place, block, 1])
    return runs


def build_block(first, base, nbr_ref, coef_ref, count_ref, dense_ref):
    lanes = pl.ds(first, LANES)
    target = nbr_ref[:, lanes] - (base + (first - HALO))
    slot_ids = lax.broadcasted_iota(jnp.int32, (BONDS, LANES), 0)
    live = slot_ids < count_ref[lanes].reshape(1, LANES)
    coefs = [jnp.where(live, coef_ref[e, :, lanes], 0.0) for e in range(9)]
    halves = [(target[h : h + 8], slot_ids[h : h + 8]) for h in (0, 8)]
    merged = [[jnp.zeros((8, LANES), jnp.float32) for _ in range(9)] for _ in range(2)]
    named = [jnp.broadcast_to(target[k : k + 1], (8, LANES)) for k in range(BONDS)]
    for k in range(BONDS):
        rows = [jnp.broadcast_to(coefs[e][k : k + 1], (8, LANES)) for e in range(9)]
        for h in range(k // 8, 2):
            same = (halves[h][0] == named[k]) & (halves[h][1] >= k)
            for e in range(9):
                merged[h][e] = merged[h][e] + jnp.where(same, rows[e], 0.0)
    row_ids = lax.broadcasted_iota(jnp.int32, (8, LANES), 0)

    def group_step(g, carry):
        cells = [[] for _ in range(9)]
        for tile in range(GROUP // 8):
            here = row_ids + (g * GROUP + tile * 8)
            slot = jnp.full((8, LANES), -1, jnp.int32)
            for k in range(BONDS):
                slot = jnp.where(named[k] == here, k, slot)
            place = slot & 7
            early, live_cell = slot < 8, slot >= 0
            for e in range(9):
                picks = [
                    jnp.take_along_axis(merged[h][e], place, axis=0, mode="promise_in_bounds")
                    for h in range(2)
                ]
                cells[e].append(jnp.where(live_cell, jnp.where(early, picks[0], picks[1]), 0.0))
        for r in range(3):
            for c in range(3):
                value = jnp.concatenate(cells[3 * r + c], axis=0)
                high = value.astype(jnp.bfloat16)
                low = (value - high.astype(jnp.float32)).astype(jnp.bfloat16)
                at = pl.ds(pl.multiple_of(c * SPAN + g * GROUP, GROUP), GROUP)
                dense_ref[at, 2 * r * LANES : (2 * r + 1) * LANES] = high
                dense_ref[at, (2 * r + 1) * LANES : (2 * r + 2) * LANES] = low
        return carry

    lax.fori_loop(0, SPAN // GROUP, group_step, 0)


def images_of(blocks, spot, panel, nbr, coef, count, halos=(), before=(), edges=False):
    rows, modes = panel.shape[1:]
    loads = len(before) == 0
    operands = [spot, nbr, count, coef, panel, *halos, *before]
    in_specs = [SMEM] + [HBM if loads else VMEM] * 4 + [VMEM] * len(halos) + [ANY] * len(before)
    width = len(blocks) * LANES
    out_shape = [pltpu.VMEM((modes, 3 * width), jnp.bfloat16)]
    out_specs = [VMEM]
    if edges:
        out_shape += [jax.ShapeDtypeStruct((3, HALO, modes), jnp.bfloat16)] * 2
        out_specs += [ANY] * 2
    n_in, n_out = len(operands), len(out_shape)

    def pieces_of(block):
        begin, end = block * LANES - HALO, (block + 1) * LANES + HALO
        found = []
        if begin < 0:
            found.append((1, HALO + begin, 0, -begin))
        low, high = max(begin, 0), min(end, rows)
        found.append((0, low, low - begin, high - low))
        if end > rows:
            found.append((2, 0, rows - begin, end - rows))
        return found

    def kernel(*refs):
        spot_ref, nbr_ref, count_ref, coef_ref, panel_ref = refs[:5]
        odd = spot_ref[1]
        outs = refs[n_in : n_in + n_out]
        window_ref, dense_ref, *scratch_refs = refs[n_in + n_out :]
        window_copies = []
        if loads:
            sources = (nbr_ref, count_ref, coef_ref)
            nbr_ref, count_ref, coef_ref, sems = scratch_refs
            copies = []

            def start(source, target, kept):
                copy = pltpu.make_async_copy(source, target, sems.at[len(copies) + len(window_copies)])
                copy.start()
                kept.append(copy)

            start(sources[0], nbr_ref, copies)
            start(sources[1], count_ref, copies)
            for _, block, length in runs_of(blocks):
                at = pl.ds(block * LANES, length * LANES)
                start(sources[2].at[:, :, at], coef_ref.at[:, :, at], copies)
            for place, block in enumerate(blocks):
                for _, source, at, length in pieces_of(block):
                    start(
                        panel_ref.at[:, pl.ds(source, length)], window_ref.at[place, :, pl.ds(at, length)], window_copies
                    )
            if edges:
                for turn, out in enumerate(outs[1:3]):
                    at = pl.multiple_of(jnp.where(odd == turn, rows - HALO, 0), 32)
                    start(panel_ref.at[:, pl.ds(at, HALO)], out, window_copies)
            for copy in copies:
                copy.wait()
        else:
            for place, block in enumerate(blocks):
                for which, source, at, length in pieces_of(block):
                    there = slice(source, source + length)
                    if which == 0:
                        found = panel_ref[:, there, :]
                    else:
                        found = jnp.where((odd == 1) == (which == 1), refs[5][:, there, :], refs[6][:, there, :])
                    window_ref[place, :, at : at + length, :] = found

        for place, block in enumerate(blocks):
            build_block(block * LANES, spot_ref[0], nbr_ref, coef_ref, count_ref, dense_ref)
            if loads and place == 0:
                for copy in window_copies:
                    copy.wait()
            both = lax.dot_general(
                window_ref[place].reshape(3 * SPAN, modes),
                dense_ref[...],
                (((0,), (0,)), ((), ())),
                preferred_element_type=jnp.float32,
            )
            for r in range(3):
                image = both[:, 2 * r * LANES : (2 * r + 1) * LANES]
                image = image + both[:, (2 * r + 1) * LANES : (2 * r + 2) * LANES]
                at = r * width + place * LANES
                outs[0][:, at : at + LANES] = image.astype(jnp.bfloat16)

    scratch = [
        pltpu.VMEM((len(blocks), 3, SPAN, modes), jnp.bfloat16),
        pltpu.VMEM((3 * SPAN, 6 * LANES), jnp.bfloat16),
    ]
    if loads:
        scratch += [
            pltpu.VMEM((BONDS, rows), jnp.int32),
            pltpu.VMEM((rows,), jnp.int32),
            pltpu.VMEM((9, BONDS, rows), jnp.float32),
            pltpu.SemaphoreType.DMA((4 + 3 * len(blocks) + 2,)),
        ]
    return call(kernel, "images", in_specs, out_specs, out_shape, operands, 0.8 + 1.2 * len(blocks), scratch)


def products_of(chunks, place, partners, mine, theirs, after=(), busy_us=2.0, cuts=()):
    rows, cols = mine[0].shape[0], partners.shape[2]
    count = len(chunks)
    spans = list(zip([0, *cuts], [*cuts, rows]))
    depth = partners.shape[1]

    def kernel(place_ref, partners_hbm, *refs):
        keep_ref, *send_refs = refs[-4 - len(spans) : -3]
        left_ref, partners_ref, sems = refs[-3:]
        copies = [
            pltpu.make_async_copy(partners_hbm.at[r], partners_ref.at[r], sems.at[r]) for r in range(3)
        ]
        for copy in copies:
            copy.start()
        kept = place_ref[0] == place_ref[1]
        for who in range(2):
            at_rows = pl.ds(pl.multiple_of(jnp.where(kept == (who == 0), 0, rows), rows), rows)
            for i, blocks in enumerate(chunks):
                image_ref = refs[who * count + i]
                width = len(blocks) * LANES
                for r in range(3):
                    for spot, block, length in runs_of(blocks):
                        at, to = r * width + spot * LANES, r * depth + block * LANES
                        left_ref[at_rows, to : to + length * LANES] = image_ref[:, at : at + length * LANES]
        total = None
        for r, copy in enumerate(copies):
            copy.wait()
            part = jnp.dot(
                left_ref[:, r * depth : (r + 1) * depth], partners_ref[r], preferred_element_type=jnp.float32
            )
            total = part if total is None else total + part
        keep_ref[...] = total[:rows]
        for (begin, end), send_ref in zip(spans, send_refs):
            send_ref[...] = total[rows + begin : rows + end].astype(jnp.bfloat16)

    return call(
        kernel,
        "products",
        [SMEM, HBM] + [VMEM] * (2 * count) + [ANY] * len(after),
        [VMEM] * (1 + len(spans)),
        [pltpu.VMEM((rows, cols), jnp.float32)]
        + [pltpu.VMEM((end - begin, cols), jnp.bfloat16) for begin, end in spans],
        (place, partners, *mine, *theirs, *after),
        busy_us,
        [
            pltpu.VMEM((2 * rows, 3 * depth), jnp.bfloat16),
            pltpu.VMEM((3, depth, cols), jnp.bfloat16),
            pltpu.SemaphoreType.DMA((3,)),
        ],
    )


def all_products(chunks, half, partners, mine, theirs):
    place = jnp.stack([half, jnp.zeros((), jnp.int32)])
    low = products_of(chunks, place, partners, mine, theirs)[0]
    high = products_of(chunks, place + jnp.array([0, 1], jnp.int32), partners, mine, theirs)[0]
    return jnp.stack([low, high])


def settle(cells, bit, rows_dev):
    depth = lax.axis_size("atoms")
    place = lax.axis_index("atoms")
    while cells.shape[0] > 1:
        pairs = cells.reshape(cells.shape[0] // 2, 2, rows_dev, -1)
        own = (place >> bit) & 1
        keep = lax.dynamic_index_in_dim(pairs, own, 1, keepdims=False)
        send = lax.dynamic_index_in_dim(pairs, 1 - own, 1, keepdims=False)
        step = 1 << bit
        got = lax.ppermute(send.astype(jnp.bfloat16), "atoms", [(z, z ^ step) for z in range(depth)])
        cells = keep + got.astype(jnp.float32)
        bit += 1
    return cells[0], bit


def collected(terms, bit, shift):
    groups, depth = lax.axis_size("modes"), lax.axis_size("atoms")
    level = 0
    while (1 << level) < groups:
        moves = []
        for z in range(depth):
            for m in range(groups):
                goal = m ^ shift
                settled = all(((z >> (bit + u)) ^ (goal >> u)) & 1 == 0 for u in range(level))
                if settled and ((z >> (bit + level)) ^ (goal >> level)) & 1:
                    moves.append((z * groups + m, (z ^ (1 << (bit + level))) * groups + m))
        sent = sum(term.astype(jnp.float32) for term in terms).astype(jnp.bfloat16)
        terms = terms + [lax.ppermute(sent, ("atoms", "modes"), moves)]
        level += 1
    return terms


def finish(flag, early, late, starts, lengths, freqs, partner_freq, norm_scale):
    rows, cols = early[0][0].shape
    terms = early + late
    operands = [flag, starts, lengths, freqs, partner_freq, *[piece for term in terms for piece in term]]
    step = 16

    def kernel(flag_ref, starts_ref, lengths_ref, freqs_ref, partner_ref, *refs):
        out_ref, sum_ref, start_ref, end_ref, freq_ref, folded_ref = refs[-6:]
        pieces = iter(refs[:-6])
        grouped = [[next(pieces) for _ in term] for term in terms]

        def add_up(some):
            out_ref[...] = some[0][0][...]
            for term in some[1:]:
                begin = 0
                for ref in term:
                    at = slice(begin, begin + ref.shape[0])
                    out_ref[at, :] = out_ref[at, :] + ref[...].astype(jnp.float32)
                    begin += ref.shape[0]

        @pl.when(flag_ref[0] == 1)
        def _():
            add_up(grouped[: len(early)])

        @pl.when(flag_ref[0] == 0)
        def _():
            add_up(grouped[len(early) :])

        def turned(row):
            return jnp.broadcast_to(row, (LANES, rows)).T

        mine = pl.ds(flag_ref[2], 1)
        start_row = starts_ref[mine, :].astype(jnp.float32)
        start_ref[...] = turned(start_row)
        end_ref[...] = turned(start_row + lengths_ref[mine, :].astype(jnp.float32))
        freq_ref[...] = turned(freqs_ref[mine, :])
        lane_ids = lax.broadcasted_iota(jnp.int32, (step, LANES), 1)

        def row_step(i, carry):
            at_rows = pl.ds(pl.multiple_of(i * step, step), step)
            start, end, freq = start_ref[at_rows, :], end_ref[at_rows, :], freq_ref[at_rows, :]
            folded = jnp.zeros((step, LANES), jnp.float32)
            for at in range(0, cols, LANES):
                columns = (lane_ids + (flag_ref[1] + at)).astype(jnp.float32)
                inside = (columns >= start) & (columns < end)
                elements = jnp.where(inside, out_ref[at_rows, at : at + LANES] * norm_scale, 0.0)
                out_ref[at_rows, at : at + LANES] = elements
                offset = freq - partner_ref[:, at : at + LANES]
                lorentz = lorentz_width / (math.pi * (offset * offset + lorentz_width * lorentz_width))
                folded = folded + jnp.where(inside, lorentz, 0.0) * elements * elements
            folded_ref[at_rows, :] = folded
            return carry

        lax.fori_loop(0, rows // step, row_step, 0)
        sum_ref[...] = jnp.sum(folded_ref[...].T, axis=0, keepdims=True)

    return call(
        kernel,
        "finish",
        [SMEM] + [VMEM] * (len(operands) - 1),
        [VMEM, VMEM],
        [jax.ShapeDtypeStruct((rows, cols), jnp.float32), jax.ShapeDtypeStruct((1, rows), jnp.float32)],
        operands,
        2.0,
        [pltpu.VMEM((rows, LANES), jnp.float32)] * 4,
    )


def body(
    mode_panel,
    partners,
    bond_blocks,
    neighbors,
    bond_count,
    panel_freq,
    partner_freq,
    win_start,
    win_len,
):
    atom_rows, modes = mode_panel.shape[1:]
    atom_index = lax.axis_index("atoms")
    atom_count = lax.axis_size("atoms")
    groups = lax.axis_size("modes")
    group_index = lax.axis_index("modes")
    half_index = lax.axis_index("sub")
    column_index = lax.axis_index(("modes", "sub"))
    part_cols = partners.shape[2]
    panel_total = win_start.shape[0]
    rows_dev = panel_total // atom_count

    nbr = neighbors.T
    coef = bond_blocks.transpose(0, 2, 1)
    spot = jnp.stack([(atom_index * atom_rows).astype(jnp.int32), (atom_index & 1).astype(jnp.int32)])

    last = atom_rows // LANES - 1
    middle = list(range(1, last))
    cut = len(middle) // 2
    chunks = [middle[:cut], middle[cut:], [last, 0]]
    shared = (spot, mode_panel, nbr, coef, bond_count)
    near, edge_one, edge_two = images_of(chunks[0], *shared, edges=True)
    pairs = [(z, z ^ 1) for z in range(atom_count)]
    others = [(z, (z + 1 if z & 1 else z - 1) % atom_count) for z in range(atom_count)]
    halos = (lax.ppermute(edge_one, "atoms", pairs), lax.ppermute(edge_two, "atoms", others))

    def from_group(cells, shift):
        return lax.ppermute(cells, "modes", [(m ^ shift, m) for m in range(groups)])

    def from_sibling(cells):
        return lax.ppermute(cells, "sub", [(0, 1), (1, 0)])

    far_all = {shift: [from_group(near, shift)] for shift in range(1, groups)}
    middle_images = images_of(chunks[1], *shared, before=[near])[0]
    before = [middle_images, *[far[0] for far in far_all.values()]]
    mine = [near, middle_images, images_of(chunks[2], *shared, halos=halos, before=before)[0]]
    for shift, far in far_all.items():
        far += [from_group(cells, shift) for cells in mine[1:]]
    theirs = [from_sibling(cells) for cells in mine]
    half = half_index.astype(jnp.int32)
    goal = atom_index * groups // atom_count

    if rows_dev == modes and groups == 2:
        place = jnp.stack([half, (atom_index & 1).astype(jnp.int32)])

        def next_door(some_mine, some_theirs, after=(), cuts=()):
            keep, *sends = products_of(
                chunks, place, partners, some_mine, some_theirs, after, EARLY_US if after else LATE_US, cuts
            )
            return keep, [lax.ppermute(send, "atoms", pairs) for send in sends]

        far = far_all[1]
        early = next_door(mine, theirs, far[:2])
        third, kept = lax.optimization_barrier((far[2], early[0]))
        early = (kept, early[1])
        far = [far[0], far[1], third]
        late = next_door(far, [from_sibling(cells) for cells in far], cuts=(modes // 4,))
        swapped = []
        for got in late[1]:
            begin = sum(piece.shape[0] for piece in swapped)
            at = slice(begin, begin + got.shape[0])
            if swapped:
                got, _ = lax.optimization_barrier((got, sent))
            sent = jnp.where(
                group_index == goal,
                late[0][at] + got.astype(jnp.float32),
                early[0][at] + early[1][0][at].astype(jnp.float32),
            ).astype(jnp.bfloat16)
            swapped.append(lax.ppermute(sent, "atoms", [(z, z ^ 2) for z in range(atom_count)]))
        early, late = [[early[0]], early[1], swapped], [[late[0]], late[1], swapped]
    else:

        def settled(some_mine, some_theirs, shift):
            cells = all_products(chunks, half, partners, some_mine, some_theirs)
            cells, bit = settle(cells.reshape(-1, rows_dev, part_cols), 0, rows_dev)
            return collected([cells], bit, shift)

        early, late = settled(mine, theirs, 0), None
        for shift, far in far_all.items():
            terms = settled(far, [from_sibling(cells) for cells in far], shift)
            if late is None:
                late = terms
            else:
                here = (group_index ^ shift) == goal
                late = [jnp.where(here, new, old) for new, old in zip(terms, late)]
        early, late = [[term] for term in early], [[term] for term in late]

    my_freq = lax.dynamic_slice_in_dim(panel_freq, atom_index * rows_dev, rows_dev, 0)
    flag = jnp.stack(
        [
            (group_index == goal).astype(jnp.int32),
            (column_index * part_cols).astype(jnp.int32),
            atom_index.astype(jnp.int32),
        ]
    )
    elements, numerator = finish(
        flag,
        early,
        late,
        win_start.reshape(atom_count, rows_dev),
        win_len.reshape(atom_count, rows_dev),
        panel_freq.reshape(atom_count, rows_dev),
        partner_freq[None, :],
        1.0 / math.sqrt(3 * atom_rows * atom_count),
    )
    numerator = numerator + lax.ppermute(numerator, "sub", [(0, 1), (1, 0)])
    step = 1
    while step < groups:
        numerator = numerator + lax.ppermute(numerator, "modes", [(m, m ^ step) for m in range(groups)])
        step *= 2
    diffusivity = math.pi / 3.0 * numerator[0] / (my_freq * my_freq)
    return (elements, diffusivity)


def solution(mesh):
    return jax.shard_map(
        body,
        mesh=mesh,
        in_specs=(
            P(None, ("dom", "atoms"), ("modes", "sub")),
            P(None, ("dom", "atoms"), ("modes", "sub")),
            P(None, ("dom", "atoms"), None),
            P(("dom", "atoms"), None),
            P(("dom", "atoms")),
            P("dom"),
            P(("dom", "modes", "sub")),
            P("dom"),
            P("dom"),
        ),
        out_specs=(P(("dom", "atoms"), ("modes", "sub")), P(("dom", "atoms"))),
        check_vma=False,
    )
```

```python
import math

import jax
import jax.numpy as jnp
from jax import lax
from jax.experimental import pallas as pl
from jax.experimental.pallas import tpu as pltpu
from jax.sharding import PartitionSpec as P

HALO = 96
BONDS = 16
LANES = 128
SPAN = LANES + 2 * HALO
GROUP = 16
VMEM_BYTES = 14 * 1024 * 1024

lorentz_width = 0.05

EARLY_US = 6.0
LATE_US = 0.1

HBM = pl.BlockSpec(memory_space=pltpu.HBM)
ANY = pl.BlockSpec(memory_space=pl.ANY)
VMEM = pl.BlockSpec(memory_space=pltpu.VMEM)
SMEM = pl.BlockSpec(memory_space=pltpu.SMEM)


def call(kernel, name, in_specs, out_specs, out_shape, operands, busy_us, scratch=()):
    operands = [
        pltpu.with_memory_space_constraint(x, spec.memory_space) if spec is VMEM or spec is HBM else x
        for spec, x in zip(in_specs, operands)
    ]
    return pl.pallas_call(
        kernel,
        in_specs=in_specs,
        out_specs=out_specs,
        out_shape=out_shape,
        scratch_shapes=list(scratch),
        compiler_params=pltpu.CompilerParams(vmem_limit_bytes=VMEM_BYTES),
        cost_estimate=pl.CostEstimate(
            flops=int(busy_us * 1.1e9), bytes_accessed=int(busy_us * 1e5), transcendentals=0
        ),
        name=name,
    )(*operands)


def runs_of(blocks):
    runs = []
    for place, block in enumerate(blocks):
        if runs and runs[-1][1] + runs[-1][2] == block:
            runs[-1][2] += 1
        else:
            runs.append([place, block, 1])
    return runs


def build_block(first, base, nbr_ref, coef_ref, count_ref, dense_ref):
    lanes = pl.ds(first, LANES)
    target = nbr_ref[:, lanes] - (base + (first - HALO))
    slot_ids = lax.broadcasted_iota(jnp.int32, (BONDS, LANES), 0)
    live = slot_ids < count_ref[lanes].reshape(1, LANES)
    coefs = [jnp.where(live, coef_ref[e, :, lanes], 0.0) for e in range(9)]
    halves = [(target[h : h + 8], slot_ids[h : h + 8]) for h in (0, 8)]
    merged = [[jnp.zeros((8, LANES), jnp.float32) for _ in range(9)] for _ in range(2)]
    named = [jnp.broadcast_to(target[k : k + 1], (8, LANES)) for k in range(BONDS)]
    for k in range(BONDS):
        rows = [jnp.broadcast_to(coefs[e][k : k + 1], (8, LANES)) for e in range(9)]
        for h in range(k // 8, 2):
            same = (halves[h][0] == named[k]) & (halves[h][1] >= k)
            for e in range(9):
                merged[h][e] = merged[h][e] + jnp.where(same, rows[e], 0.0)
    row_ids = lax.broadcasted_iota(jnp.int32, (8, LANES), 0)

    def group_step(g, carry):
        cells = [[] for _ in range(9)]
        for tile in range(GROUP // 8):
            here = row_ids + (g * GROUP + tile * 8)
            slot = jnp.full((8, LANES), -1, jnp.int32)
            for k in range(BONDS):
                slot = jnp.where(named[k] == here, k, slot)
            place = slot & 7
            early, live_cell = slot < 8, slot >= 0
            for e in range(9):
                picks = [
                    jnp.take_along_axis(merged[h][e], place, axis=0, mode="promise_in_bounds")
                    for h in range(2)
                ]
                cells[e].append(jnp.where(live_cell, jnp.where(early, picks[0], picks[1]), 0.0))
        for r in range(3):
            for c in range(3):
                value = jnp.concatenate(cells[3 * r + c], axis=0)
                high = value.astype(jnp.bfloat16)
                low = (value - high.astype(jnp.float32)).astype(jnp.bfloat16)
                at = pl.ds(pl.multiple_of(c * SPAN + g * GROUP, GROUP), GROUP)
                dense_ref[at, 2 * r * LANES : (2 * r + 1) * LANES] = high
                dense_ref[at, (2 * r + 1) * LANES : (2 * r + 2) * LANES] = low
        return carry

    lax.fori_loop(0, SPAN // GROUP, group_step, 0)


def images_of(blocks, spot, panel, nbr, coef, count, halos=(), before=(), edges=False):
    rows, modes = panel.shape[1:]
    loads = len(before) == 0
    operands = [spot, nbr, count, coef, panel, *halos, *before]
    in_specs = [SMEM] + [HBM if loads else VMEM] * 4 + [VMEM] * len(halos) + [ANY] * len(before)
    width = len(blocks) * LANES
    out_shape = [pltpu.VMEM((modes, 3 * width), jnp.bfloat16)]
    out_specs = [VMEM]
    if edges:
        out_shape += [jax.ShapeDtypeStruct((3, HALO, modes), jnp.bfloat16)] * 2
        out_specs += [ANY] * 2
    n_in, n_out = len(operands), len(out_shape)

    def pieces_of(block):
        begin, end = block * LANES - HALO, (block + 1) * LANES + HALO
        found = []
        if begin < 0:
            found.append((1, HALO + begin, 0, -begin))
        low, high = max(begin, 0), min(end, rows)
        found.append((0, low, low - begin, high - low))
        if end > rows:
            found.append((2, 0, rows - begin, end - rows))
        return found

    def kernel(*refs):
        spot_ref, nbr_ref, count_ref, coef_ref, panel_ref = refs[:5]
        odd = spot_ref[1]
        outs = refs[n_in : n_in + n_out]
        window_ref, dense_ref, *scratch_refs = refs[n_in + n_out :]
        window_copies = []
        if loads:
            sources = (nbr_ref, count_ref, coef_ref)
            nbr_ref, count_ref, coef_ref, sems = scratch_refs
            copies = []

            def start(source, target, kept):
                copy = pltpu.make_async_copy(source, target, sems.at[len(copies) + len(window_copies)])
                copy.start()
                kept.append(copy)

            start(sources[0], nbr_ref, copies)
            start(sources[1], count_ref, copies)
            for _, block, length in runs_of(blocks):
                at = pl.ds(block * LANES, length * LANES)
                start(sources[2].at[:, :, at], coef_ref.at[:, :, at], copies)
            for place, block in enumerate(blocks):
                for _, source, at, length in pieces_of(block):
                    start(
                        panel_ref.at[:, pl.ds(source, length)], window_ref.at[place, :, pl.ds(at, length)], window_copies
                    )
            if edges:
                for turn, out in enumerate(outs[1:3]):
                    at = pl.multiple_of(jnp.where(odd == turn, rows - HALO, 0), 32)
                    start(panel_ref.at[:, pl.ds(at, HALO)], out, window_copies)
            for copy in copies:
                copy.wait()
        else:
            for place, block in enumerate(blocks):
                for which, source, at, length in pieces_of(block):
                    there = slice(source, source + length)
                    if which == 0:
                        found = panel_ref[:, there, :]
                    else:
                        found = jnp.where((odd == 1) == (which == 1), refs[5][:, there, :], refs[6][:, there, :])
                    window_ref[place, :, at : at + length, :] = found

        for place, block in enumerate(blocks):
            build_block(block * LANES, spot_ref[0], nbr_ref, coef_ref, count_ref, dense_ref)
            if loads and place == 0:
                for copy in window_copies:
                    copy.wait()
            both = lax.dot_general(
                window_ref[place].reshape(3 * SPAN, modes),
                dense_ref[...],
                (((0,), (0,)), ((), ())),
                preferred_element_type=jnp.float32,
            )
            for r in range(3):
                image = both[:, 2 * r * LANES : (2 * r + 1) * LANES]
                image = image + both[:, (2 * r + 1) * LANES : (2 * r + 2) * LANES]
                at = r * width + place * LANES
                outs[0][:, at : at + LANES] = image.astype(jnp.bfloat16)

    scratch = [
        pltpu.VMEM((len(blocks), 3, SPAN, modes), jnp.bfloat16),
        pltpu.VMEM((3 * SPAN, 6 * LANES), jnp.bfloat16),
    ]
    if loads:
        scratch += [
            pltpu.VMEM((BONDS, rows), jnp.int32),
            pltpu.VMEM((rows,), jnp.int32),
            pltpu.VMEM((9, BONDS, rows), jnp.float32),
            pltpu.SemaphoreType.DMA((4 + 3 * len(blocks) + 2,)),
        ]
    return call(kernel, "images", in_specs, out_specs, out_shape, operands, 0.8 + 1.2 * len(blocks), scratch)


def products_of(chunks, place, partners, mine, theirs, after=(), busy_us=2.0, parts=1):
    rows, cols = mine[0].shape[0], partners.shape[2]
    count = len(chunks)
    depth = partners.shape[1]

    def kernel(place_ref, partners_hbm, *refs):
        keep_ref, *send_refs = refs[-4 - parts : -3]
        left_ref, partners_ref, sems = refs[-3:]
        copies = [
            pltpu.make_async_copy(partners_hbm.at[r], partners_ref.at[r], sems.at[r]) for r in range(3)
        ]
        for copy in copies:
            copy.start()
        kept = place_ref[0] == place_ref[1]
        for who in range(2):
            at_rows = pl.ds(pl.multiple_of(jnp.where(kept == (who == 0), 0, rows), rows), rows)
            for i, blocks in enumerate(chunks):
                image_ref = refs[who * count + i]
                width = len(blocks) * LANES
                for r in range(3):
                    for spot, block, length in runs_of(blocks):
                        at, to = r * width + spot * LANES, r * depth + block * LANES
                        left_ref[at_rows, to : to + length * LANES] = image_ref[:, at : at + length * LANES]
        total = None
        for r, copy in enumerate(copies):
            copy.wait()
            part = jnp.dot(
                left_ref[:, r * depth : (r + 1) * depth], partners_ref[r], preferred_element_type=jnp.float32
            )
            total = part if total is None else total + part
        keep_ref[...] = total[:rows]
        for part, send_ref in enumerate(send_refs):
            at = rows + part * (rows // parts)
            send_ref[...] = total[at : at + rows // parts].astype(jnp.bfloat16)

    return call(
        kernel,
        "products",
        [SMEM, HBM] + [VMEM] * (2 * count) + [ANY] * len(after),
        [VMEM] * (1 + parts),
        [pltpu.VMEM((rows, cols), jnp.float32)] + [pltpu.VMEM((rows // parts, cols), jnp.bfloat16)] * parts,
        (place, partners, *mine, *theirs, *after),
        busy_us,
        [
            pltpu.VMEM((2 * rows, 3 * depth), jnp.bfloat16),
            pltpu.VMEM((3, depth, cols), jnp.bfloat16),
            pltpu.SemaphoreType.DMA((3,)),
        ],
    )


def all_products(chunks, half, partners, mine, theirs):
    place = jnp.stack([half, jnp.zeros((), jnp.int32)])
    low = products_of(chunks, place, partners, mine, theirs)[0]
    high = products_of(chunks, place + jnp.array([0, 1], jnp.int32), partners, mine, theirs)[0]
    return jnp.stack([low, high])


def settle(cells, bit, rows_dev):
    depth = lax.axis_size("atoms")
    place = lax.axis_index("atoms")
    while cells.shape[0] > 1:
        pairs = cells.reshape(cells.shape[0] // 2, 2, rows_dev, -1)
        own = (place >> bit) & 1
        keep = lax.dynamic_index_in_dim(pairs, own, 1, keepdims=False)
        send = lax.dynamic_index_in_dim(pairs, 1 - own, 1, keepdims=False)
        step = 1 << bit
        got = lax.ppermute(send.astype(jnp.bfloat16), "atoms", [(z, z ^ step) for z in range(depth)])
        cells = keep + got.astype(jnp.float32)
        bit += 1
    return cells[0], bit


def collected(terms, bit, shift):
    groups, depth = lax.axis_size("modes"), lax.axis_size("atoms")
    level = 0
    while (1 << level) < groups:
        moves = []
        for z in range(depth):
            for m in range(groups):
                goal = m ^ shift
                settled = all(((z >> (bit + u)) ^ (goal >> u)) & 1 == 0 for u in range(level))
                if settled and ((z >> (bit + level)) ^ (goal >> level)) & 1:
                    moves.append((z * groups + m, (z ^ (1 << (bit + level))) * groups + m))
        sent = sum(term.astype(jnp.float32) for term in terms).astype(jnp.bfloat16)
        terms = terms + [lax.ppermute(sent, ("atoms", "modes"), moves)]
        level += 1
    return terms


def finish(flag, early, late, starts, lengths, freqs, partner_freq, norm_scale):
    rows, cols = early[0][0].shape
    terms = early + late
    operands = [flag, starts, lengths, freqs, partner_freq, *[piece for term in terms for piece in term]]
    step = 16

    def kernel(flag_ref, starts_ref, lengths_ref, freqs_ref, partner_ref, *refs):
        out_ref, sum_ref, start_ref, end_ref, freq_ref, folded_ref = refs[-6:]
        pieces = iter(refs[:-6])
        grouped = [[next(pieces) for _ in term] for term in terms]

        def add_up(some):
            out_ref[...] = some[0][0][...]
            for term in some[1:]:
                span = rows // len(term)
                for i, ref in enumerate(term):
                    at = slice(i * span, (i + 1) * span)
                    out_ref[at, :] = out_ref[at, :] + ref[...].astype(jnp.float32)

        @pl.when(flag_ref[0] == 1)
        def _():
            add_up(grouped[: len(early)])

        @pl.when(flag_ref[0] == 0)
        def _():
            add_up(grouped[len(early) :])

        def turned(row):
            return jnp.broadcast_to(row, (LANES, rows)).T

        mine = pl.ds(flag_ref[2], 1)
        start_row = starts_ref[mine, :].astype(jnp.float32)
        start_ref[...] = turned(start_row)
        end_ref[...] = turned(start_row + lengths_ref[mine, :].astype(jnp.float32))
        freq_ref[...] = turned(freqs_ref[mine, :])
        lane_ids = lax.broadcasted_iota(jnp.int32, (step, LANES), 1)

        def row_step(i, carry):
            at_rows = pl.ds(pl.multiple_of(i * step, step), step)
            start, end, freq = start_ref[at_rows, :], end_ref[at_rows, :], freq_ref[at_rows, :]
            folded = jnp.zeros((step, LANES), jnp.float32)
            for at in range(0, cols, LANES):
                columns = (lane_ids + (flag_ref[1] + at)).astype(jnp.float32)
                inside = (columns >= start) & (columns < end)
                elements = jnp.where(inside, out_ref[at_rows, at : at + LANES] * norm_scale, 0.0)
                out_ref[at_rows, at : at + LANES] = elements
                offset = freq - partner_ref[:, at : at + LANES]
                lorentz = lorentz_width / (math.pi * (offset * offset + lorentz_width * lorentz_width))
                folded = folded + jnp.where(inside, lorentz, 0.0) * elements * elements
            folded_ref[at_rows, :] = folded
            return carry

        lax.fori_loop(0, rows // step, row_step, 0)
        sum_ref[...] = jnp.sum(folded_ref[...].T, axis=0, keepdims=True)

    return call(
        kernel,
        "finish",
        [SMEM] + [VMEM] * (len(operands) - 1),
        [VMEM, VMEM],
        [jax.ShapeDtypeStruct((rows, cols), jnp.float32), jax.ShapeDtypeStruct((1, rows), jnp.float32)],
        operands,
        2.0,
        [pltpu.VMEM((rows, LANES), jnp.float32)] * 4,
    )


def body(
    mode_panel,
    partners,
    bond_blocks,
    neighbors,
    bond_count,
    panel_freq,
    partner_freq,
    win_start,
    win_len,
):
    atom_rows, modes = mode_panel.shape[1:]
    atom_index = lax.axis_index("atoms")
    atom_count = lax.axis_size("atoms")
    groups = lax.axis_size("modes")
    group_index = lax.axis_index("modes")
    half_index = lax.axis_index("sub")
    column_index = lax.axis_index(("modes", "sub"))
    part_cols = partners.shape[2]
    panel_total = win_start.shape[0]
    rows_dev = panel_total // atom_count

    nbr = neighbors.T
    coef = bond_blocks.transpose(0, 2, 1)
    spot = jnp.stack([(atom_index * atom_rows).astype(jnp.int32), (atom_index & 1).astype(jnp.int32)])

    last = atom_rows // LANES - 1
    middle = list(range(1, last))
    cut = len(middle) // 2
    chunks = [middle[:cut], middle[cut:], [last, 0]]
    shared = (spot, mode_panel, nbr, coef, bond_count)
    near, edge_one, edge_two = images_of(chunks[0], *shared, edges=True)
    pairs = [(z, z ^ 1) for z in range(atom_count)]
    others = [(z, min(max(z + 1 if z & 1 else z - 1, 0), atom_count - 1)) for z in range(atom_count)]
    halos = (lax.ppermute(edge_one, "atoms", pairs), lax.ppermute(edge_two, "atoms", others))

    def from_group(cells, shift):
        return lax.ppermute(cells, "modes", [(m ^ shift, m) for m in range(groups)])

    def from_sibling(cells):
        return lax.ppermute(cells, "sub", [(0, 1), (1, 0)])

    far_all = {shift: [from_group(near, shift)] for shift in range(1, groups)}
    middle_images = images_of(chunks[1], *shared, before=[near])[0]
    before = [middle_images, *[far[0] for far in far_all.values()]]
    mine = [near, middle_images, images_of(chunks[2], *shared, halos=halos, before=before)[0]]
    for shift, far in far_all.items():
        far += [from_group(cells, shift) for cells in mine[1:]]
    theirs = [from_sibling(cells) for cells in mine]
    half = half_index.astype(jnp.int32)
    goal = atom_index * groups // atom_count

    if rows_dev == modes and groups == 2:
        place = jnp.stack([half, (atom_index & 1).astype(jnp.int32)])

        def next_door(some_mine, some_theirs, after=(), parts=1):
            keep, *sends = products_of(
                chunks, place, partners, some_mine, some_theirs, after, EARLY_US if after else LATE_US, parts
            )
            return keep, [lax.ppermute(send, "atoms", pairs) for send in sends]

        far = far_all[1]
        early = next_door(mine, theirs, far[:2])
        third, kept = lax.optimization_barrier((far[2], early[0]))
        early = (kept, early[1])
        far = [far[0], far[1], third]
        parts = 2
        span = modes // parts
        late = next_door(far, [from_sibling(cells) for cells in far], parts=parts)
        swapped = []
        for part, got in enumerate(late[1]):
            at = slice(part * span, (part + 1) * span)
            if part:
                got, _ = lax.optimization_barrier((got, sent))
            sent = jnp.where(
                group_index == goal,
                late[0][at] + got.astype(jnp.float32),
                early[0][at] + early[1][0][at].astype(jnp.float32),
            ).astype(jnp.bfloat16)
            swapped.append(lax.ppermute(sent, "atoms", [(z, z ^ 2) for z in range(atom_count)]))
        early, late = [[early[0]], early[1], swapped], [[late[0]], late[1], swapped]
    else:

        def settled(some_mine, some_theirs, shift):
            cells = all_products(chunks, half, partners, some_mine, some_theirs)
            cells, bit = settle(cells.reshape(-1, rows_dev, part_cols), 0, rows_dev)
            return collected([cells], bit, shift)

        early, late = settled(mine, theirs, 0), None
        for shift, far in far_all.items():
            terms = settled(far, [from_sibling(cells) for cells in far], shift)
            if late is None:
                late = terms
            else:
                here = (group_index ^ shift) == goal
                late = [jnp.where(here, new, old) for new, old in zip(terms, late)]
        early, late = [[term] for term in early], [[term] for term in late]

    my_freq = lax.dynamic_slice_in_dim(panel_freq, atom_index * rows_dev, rows_dev, 0)
    flag = jnp.stack(
        [
            (group_index == goal).astype(jnp.int32),
            (column_index * part_cols).astype(jnp.int32),
            atom_index.astype(jnp.int32),
        ]
    )
    elements, numerator = finish(
        flag,
        early,
        late,
        win_start.reshape(atom_count, rows_dev),
        win_len.reshape(atom_count, rows_dev),
        panel_freq.reshape(atom_count, rows_dev),
        partner_freq[None, :],
        1.0 / math.sqrt(3 * atom_rows * atom_count),
    )
    numerator = numerator + lax.ppermute(numerator, "sub", [(0, 1), (1, 0)])
    step = 1
    while step < groups:
        numerator = numerator + lax.ppermute(numerator, "modes", [(m, m ^ step) for m in range(groups)])
        step *= 2
    diffusivity = math.pi / 3.0 * numerator[0] / (my_freq * my_freq)
    return (elements, diffusivity)


def solution(mesh):
    return jax.shard_map(
        body,
        mesh=mesh,
        in_specs=(
            P(None, ("dom", "atoms"), ("modes", "sub")),
            P(None, ("dom", "atoms"), ("modes", "sub")),
            P(None, ("dom", "atoms"), None),
            P(("dom", "atoms"), None),
            P(("dom", "atoms")),
            P("dom"),
            P(("dom", "modes", "sub")),
            P("dom"),
            P("dom"),
        ),
        out_specs=(P(("dom", "atoms"), ("modes", "sub")), P(("dom", "atoms"))),
        check_vma=False,
    )
```

```python
import math

import jax
import jax.numpy as jnp
from jax import lax
from jax.experimental import pallas as pl
from jax.experimental.pallas import tpu as pltpu
from jax.sharding import PartitionSpec as P

HALO = 96
BONDS = 16
LANES = 128
SPAN = LANES + 2 * HALO
GROUP = 16
VMEM_BYTES = 14 * 1024 * 1024

lorentz_width = 0.05

EARLY_US = 6.0
LATE_US = 0.1

HBM = pl.BlockSpec(memory_space=pltpu.HBM)
ANY = pl.BlockSpec(memory_space=pl.ANY)
VMEM = pl.BlockSpec(memory_space=pltpu.VMEM)
SMEM = pl.BlockSpec(memory_space=pltpu.SMEM)


def call(kernel, name, in_specs, out_specs, out_shape, operands, busy_us, scratch=()):
    operands = [
        pltpu.with_memory_space_constraint(x, spec.memory_space) if spec is VMEM or spec is HBM else x
        for spec, x in zip(in_specs, operands)
    ]
    return pl.pallas_call(
        kernel,
        in_specs=in_specs,
        out_specs=out_specs,
        out_shape=out_shape,
        scratch_shapes=list(scratch),
        compiler_params=pltpu.CompilerParams(vmem_limit_bytes=VMEM_BYTES),
        cost_estimate=pl.CostEstimate(
            flops=int(busy_us * 1.1e9), bytes_accessed=int(busy_us * 1e5), transcendentals=0
        ),
        name=name,
    )(*operands)


def runs_of(blocks):
    runs = []
    for place, block in enumerate(blocks):
        if runs and runs[-1][1] + runs[-1][2] == block:
            runs[-1][2] += 1
        else:
            runs.append([place, block, 1])
    return runs


def build_block(first, base, nbr_ref, coef_ref, count_ref, dense_ref):
    lanes = pl.ds(first, LANES)
    target = nbr_ref[:, lanes] - (base + (first - HALO))
    slot_ids = lax.broadcasted_iota(jnp.int32, (BONDS, LANES), 0)
    live = slot_ids < count_ref[lanes].reshape(1, LANES)
    coefs = [jnp.where(live, coef_ref[e, :, lanes], 0.0) for e in range(9)]
    halves = [(target[h : h + 8], slot_ids[h : h + 8]) for h in (0, 8)]
    merged = [[jnp.zeros((8, LANES), jnp.float32) for _ in range(9)] for _ in range(2)]
    named = [jnp.broadcast_to(target[k : k + 1], (8, LANES)) for k in range(BONDS)]
    for k in range(BONDS):
        rows = [jnp.broadcast_to(coefs[e][k : k + 1], (8, LANES)) for e in range(9)]
        for h in range(k // 8, 2):
            same = (halves[h][0] == named[k]) & (halves[h][1] >= k)
            for e in range(9):
                merged[h][e] = merged[h][e] + jnp.where(same, rows[e], 0.0)
    row_ids = lax.broadcasted_iota(jnp.int32, (8, LANES), 0)

    def group_step(g, carry):
        cells = [[] for _ in range(9)]
        for tile in range(GROUP // 8):
            here = row_ids + (g * GROUP + tile * 8)
            slot = jnp.full((8, LANES), -1, jnp.int32)
            for k in range(BONDS):
                slot = jnp.where(named[k] == here, k, slot)
            place = slot & 7
            early, live_cell = slot < 8, slot >= 0
            for e in range(9):
                picks = [
                    jnp.take_along_axis(merged[h][e], place, axis=0, mode="promise_in_bounds")
                    for h in range(2)
                ]
                cells[e].append(jnp.where(live_cell, jnp.where(early, picks[0], picks[1]), 0.0))
        for r in range(3):
            for c in range(3):
                value = jnp.concatenate(cells[3 * r + c], axis=0)
                high = value.astype(jnp.bfloat16)
                low = (value - high.astype(jnp.float32)).astype(jnp.bfloat16)
                at = pl.ds(pl.multiple_of(c * SPAN + g * GROUP, GROUP), GROUP)
                dense_ref[at, 2 * r * LANES : (2 * r + 1) * LANES] = high
                dense_ref[at, (2 * r + 1) * LANES : (2 * r + 2) * LANES] = low
        return carry

    lax.fori_loop(0, SPAN // GROUP, group_step, 0)


def images_of(blocks, spot, panel, nbr, coef, count, halos=(), before=(), edges=False):
    rows, modes = panel.shape[1:]
    loads = len(before) == 0
    operands = [spot, nbr, count, coef, panel, *halos, *before]
    in_specs = [SMEM] + [HBM if loads else VMEM] * 4 + [VMEM] * len(halos) + [ANY] * len(before)
    width = len(blocks) * LANES
    out_shape = [pltpu.VMEM((modes, 3 * width), jnp.bfloat16)]
    out_specs = [VMEM]
    if edges:
        out_shape += [jax.ShapeDtypeStruct((3, HALO, modes), jnp.bfloat16)] * 2
        out_specs += [ANY] * 2
    n_in, n_out = len(operands), len(out_shape)

    def pieces_of(block):
        begin, end = block * LANES - HALO, (block + 1) * LANES + HALO
        found = []
        if begin < 0:
            found.append((1, HALO + begin, 0, -begin))
        low, high = max(begin, 0), min(end, rows)
        found.append((0, low, low - begin, high - low))
        if end > rows:
            found.append((2, 0, rows - begin, end - rows))
        return found

    def kernel(*refs):
        spot_ref, nbr_ref, count_ref, coef_ref, panel_ref = refs[:5]
        odd = spot_ref[1]
        outs = refs[n_in : n_in + n_out]
        window_ref, dense_ref, *scratch_refs = refs[n_in + n_out :]
        window_copies = []
        if loads:
            sources = (nbr_ref, count_ref, coef_ref)
            nbr_ref, count_ref, coef_ref, sems = scratch_refs
            copies = []

            def start(source, target, kept):
                copy = pltpu.make_async_copy(source, target, sems.at[len(copies) + len(window_copies)])
                copy.start()
                kept.append(copy)

            start(sources[0], nbr_ref, copies)
            start(sources[1], count_ref, copies)
            for _, block, length in runs_of(blocks):
                at = pl.ds(block * LANES, length * LANES)
                start(sources[2].at[:, :, at], coef_ref.at[:, :, at], copies)
            for place, block in enumerate(blocks):
                for _, source, at, length in pieces_of(block):
                    start(
                        panel_ref.at[:, pl.ds(source, length)], window_ref.at[place, :, pl.ds(at, length)], window_copies
                    )
            if edges:
                for turn, out in enumerate(outs[1:3]):
                    at = pl.multiple_of(jnp.where(odd == turn, rows - HALO, 0), 32)
                    start(panel_ref.at[:, pl.ds(at, HALO)], out, window_copies)
            for copy in copies:
                copy.wait()
        else:
            for place, block in enumerate(blocks):
                for which, source, at, length in pieces_of(block):
                    there = slice(source, source + length)
                    if which == 0:
                        found = panel_ref[:, there, :]
                    else:
                        found = jnp.where((odd == 1) == (which == 1), refs[5][:, there, :], refs[6][:, there, :])
                    window_ref[place, :, at : at + length, :] = found

        for place, block in enumerate(blocks):
            build_block(block * LANES, spot_ref[0], nbr_ref, coef_ref, count_ref, dense_ref)
            if loads and place == 0:
                for copy in window_copies:
                    copy.wait()
            both = lax.dot_general(
                window_ref[place].reshape(3 * SPAN, modes),
                dense_ref[...],
                (((0,), (0,)), ((), ())),
                preferred_element_type=jnp.float32,
            )
            for r in range(3):
                image = both[:, 2 * r * LANES : (2 * r + 1) * LANES]
                image = image + both[:, (2 * r + 1) * LANES : (2 * r + 2) * LANES]
                at = r * width + place * LANES
                outs[0][:, at : at + LANES] = image.astype(jnp.bfloat16)

    scratch = [
        pltpu.VMEM((len(blocks), 3, SPAN, modes), jnp.bfloat16),
        pltpu.VMEM((3 * SPAN, 6 * LANES), jnp.bfloat16),
    ]
    if loads:
        scratch += [
            pltpu.VMEM((BONDS, rows), jnp.int32),
            pltpu.VMEM((rows,), jnp.int32),
            pltpu.VMEM((9, BONDS, rows), jnp.float32),
            pltpu.SemaphoreType.DMA((4 + 3 * len(blocks) + 2,)),
        ]
    return call(kernel, "images", in_specs, out_specs, out_shape, operands, 0.8 + 1.2 * len(blocks), scratch)


def products_of(chunks, place, partners, mine, theirs, after=(), busy_us=2.0, parts=1):
    rows, cols = mine[0].shape[0], partners.shape[2]
    count = len(chunks)
    depth = partners.shape[1]
    pieces = [(r, pl.ds(h * (depth // 2), depth // 2)) for r in range(3) for h in range(2)]

    def kernel(place_ref, partners_hbm, *refs):
        keep_ref, *send_refs = refs[-4 - parts : -3]
        left_ref, partners_ref, sems = refs[-3:]
        copies = [
            pltpu.make_async_copy(partners_hbm.at[r, at], partners_ref.at[r, at], sems.at[i])
            for i, (r, at) in enumerate(pieces)
        ]
        for copy in copies:
            copy.start()
        kept = place_ref[0] == place_ref[1]
        for who in range(2):
            at_rows = pl.ds(pl.multiple_of(jnp.where(kept == (who == 0), 0, rows), rows), rows)
            for i, blocks in enumerate(chunks):
                image_ref = refs[who * count + i]
                width = len(blocks) * LANES
                for r in range(3):
                    for spot, block, length in runs_of(blocks):
                        at, to = r * width + spot * LANES, r * depth + block * LANES
                        left_ref[at_rows, to : to + length * LANES] = image_ref[:, at : at + length * LANES]
        total = None
        for (r, at), copy in zip(pieces, copies):
            copy.wait()
            from_row = r * depth + at.start
            part = jnp.dot(
                left_ref[:, from_row : from_row + at.size],
                partners_ref[r, at],
                preferred_element_type=jnp.float32,
            )
            total = part if total is None else total + part
        keep_ref[...] = total[:rows]
        for part, send_ref in enumerate(send_refs):
            at = rows + part * (rows // parts)
            send_ref[...] = total[at : at + rows // parts].astype(jnp.bfloat16)

    return call(
        kernel,
        "products",
        [SMEM, HBM] + [VMEM] * (2 * count) + [ANY] * len(after),
        [VMEM] * (1 + parts),
        [pltpu.VMEM((rows, cols), jnp.float32)] + [pltpu.VMEM((rows // parts, cols), jnp.bfloat16)] * parts,
        (place, partners, *mine, *theirs, *after),
        busy_us,
        [
            pltpu.VMEM((2 * rows, 3 * depth), jnp.bfloat16),
            pltpu.VMEM((3, depth, cols), jnp.bfloat16),
            pltpu.SemaphoreType.DMA((len(pieces),)),
        ],
    )


def all_products(chunks, half, partners, mine, theirs):
    place = jnp.stack([half, jnp.zeros((), jnp.int32)])
    low = products_of(chunks, place, partners, mine, theirs)[0]
    high = products_of(chunks, place + jnp.array([0, 1], jnp.int32), partners, mine, theirs)[0]
    return jnp.stack([low, high])


def settle(cells, bit, rows_dev):
    depth = lax.axis_size("atoms")
    place = lax.axis_index("atoms")
    while cells.shape[0] > 1:
        pairs = cells.reshape(cells.shape[0] // 2, 2, rows_dev, -1)
        own = (place >> bit) & 1
        keep = lax.dynamic_index_in_dim(pairs, own, 1, keepdims=False)
        send = lax.dynamic_index_in_dim(pairs, 1 - own, 1, keepdims=False)
        step = 1 << bit
        got = lax.ppermute(send.astype(jnp.bfloat16), "atoms", [(z, z ^ step) for z in range(depth)])
        cells = keep + got.astype(jnp.float32)
        bit += 1
    return cells[0], bit


def collected(terms, bit, shift):
    groups, depth = lax.axis_size("modes"), lax.axis_size("atoms")
    level = 0
    while (1 << level) < groups:
        moves = []
        for z in range(depth):
            for m in range(groups):
                goal = m ^ shift
                settled = all(((z >> (bit + u)) ^ (goal >> u)) & 1 == 0 for u in range(level))
                if settled and ((z >> (bit + level)) ^ (goal >> level)) & 1:
                    moves.append((z * groups + m, (z ^ (1 << (bit + level))) * groups + m))
        sent = sum(term.astype(jnp.float32) for term in terms).astype(jnp.bfloat16)
        terms = terms + [lax.ppermute(sent, ("atoms", "modes"), moves)]
        level += 1
    return terms


def finish(flag, early, late, starts, lengths, freqs, partner_freq, norm_scale):
    rows, cols = early[0][0].shape
    terms = early + late
    operands = [flag, starts, lengths, freqs, partner_freq, *[piece for term in terms for piece in term]]
    step = 16

    def kernel(flag_ref, starts_ref, lengths_ref, freqs_ref, partner_ref, *refs):
        out_ref, sum_ref, start_ref, end_ref, freq_ref, folded_ref = refs[-6:]
        pieces = iter(refs[:-6])
        grouped = [[next(pieces) for _ in term] for term in terms]

        def add_up(some):
            out_ref[...] = some[0][0][...]
            for term in some[1:]:
                span = rows // len(term)
                for i, ref in enumerate(term):
                    at = slice(i * span, (i + 1) * span)
                    out_ref[at, :] = out_ref[at, :] + ref[...].astype(jnp.float32)

        @pl.when(flag_ref[0] == 1)
        def _():
            add_up(grouped[: len(early)])

        @pl.when(flag_ref[0] == 0)
        def _():
            add_up(grouped[len(early) :])

        def turned(row):
            return jnp.broadcast_to(row, (LANES, rows)).T

        mine = pl.ds(flag_ref[2], 1)
        start_row = starts_ref[mine, :].astype(jnp.float32)
        start_ref[...] = turned(start_row)
        end_ref[...] = turned(start_row + lengths_ref[mine, :].astype(jnp.float32))
        freq_ref[...] = turned(freqs_ref[mine, :])
        lane_ids = lax.broadcasted_iota(jnp.int32, (step, LANES), 1)

        def row_step(i, carry):
            at_rows = pl.ds(pl.multiple_of(i * step, step), step)
            start, end, freq = start_ref[at_rows, :], end_ref[at_rows, :], freq_ref[at_rows, :]
            folded = jnp.zeros((step, LANES), jnp.float32)
            for at in range(0, cols, LANES):
                columns = (lane_ids + (flag_ref[1] + at)).astype(jnp.float32)
                inside = (columns >= start) & (columns < end)
                elements = jnp.where(inside, out_ref[at_rows, at : at + LANES] * norm_scale, 0.0)
                out_ref[at_rows, at : at + LANES] = elements
                offset = freq - partner_ref[:, at : at + LANES]
                lorentz = lorentz_width / (math.pi * (offset * offset + lorentz_width * lorentz_width))
                folded = folded + jnp.where(inside, lorentz, 0.0) * elements * elements
            folded_ref[at_rows, :] = folded
            return carry

        lax.fori_loop(0, rows // step, row_step, 0)
        sum_ref[...] = jnp.sum(folded_ref[...].T, axis=0, keepdims=True)

    return call(
        kernel,
        "finish",
        [SMEM] + [VMEM] * (len(operands) - 1),
        [VMEM, VMEM],
        [jax.ShapeDtypeStruct((rows, cols), jnp.float32), jax.ShapeDtypeStruct((1, rows), jnp.float32)],
        operands,
        2.0,
        [pltpu.VMEM((rows, LANES), jnp.float32)] * 4,
    )


def body(
    mode_panel,
    partners,
    bond_blocks,
    neighbors,
    bond_count,
    panel_freq,
    partner_freq,
    win_start,
    win_len,
):
    atom_rows, modes = mode_panel.shape[1:]
    atom_index = lax.axis_index("atoms")
    atom_count = lax.axis_size("atoms")
    groups = lax.axis_size("modes")
    group_index = lax.axis_index("modes")
    half_index = lax.axis_index("sub")
    column_index = lax.axis_index(("modes", "sub"))
    part_cols = partners.shape[2]
    panel_total = win_start.shape[0]
    rows_dev = panel_total // atom_count

    nbr = neighbors.T
    coef = bond_blocks.transpose(0, 2, 1)
    spot = jnp.stack([(atom_index * atom_rows).astype(jnp.int32), (atom_index & 1).astype(jnp.int32)])

    last = atom_rows // LANES - 1
    middle = list(range(1, last))
    cut = len(middle) // 2
    chunks = [middle[:cut], middle[cut:], [last, 0]]
    shared = (spot, mode_panel, nbr, coef, bond_count)
    near, edge_one, edge_two = images_of(chunks[0], *shared, edges=True)
    pairs = [(z, z ^ 1) for z in range(atom_count)]
    others = [(z, (z + 1 if z & 1 else z - 1) % atom_count) for z in range(atom_count)]
    halos = (lax.ppermute(edge_one, "atoms", pairs), lax.ppermute(edge_two, "atoms", others))

    def from_group(cells, shift):
        return lax.ppermute(cells, "modes", [(m ^ shift, m) for m in range(groups)])

    def from_sibling(cells):
        return lax.ppermute(cells, "sub", [(0, 1), (1, 0)])

    far_all = {shift: [from_group(near, shift)] for shift in range(1, groups)}
    middle_images = images_of(chunks[1], *shared, before=[near])[0]
    before = [middle_images, *[far[0] for far in far_all.values()]]
    mine = [near, middle_images, images_of(chunks[2], *shared, halos=halos, before=before)[0]]
    for shift, far in far_all.items():
        far += [from_group(cells, shift) for cells in mine[1:]]
    theirs = [from_sibling(cells) for cells in mine]
    half = half_index.astype(jnp.int32)
    goal = atom_index * groups // atom_count

    if rows_dev == modes and groups == 2:
        place = jnp.stack([half, (atom_index & 1).astype(jnp.int32)])

        def next_door(some_mine, some_theirs, after=(), parts=1):
            keep, *sends = products_of(
                chunks, place, partners, some_mine, some_theirs, after, EARLY_US if after else LATE_US, parts
            )
            return keep, [lax.ppermute(send, "atoms", pairs) for send in sends]

        far = far_all[1]
        early = next_door(mine, theirs, far[:2])
        third, kept = lax.optimization_barrier((far[2], early[0]))
        early = (kept, early[1])
        far = [far[0], far[1], third]
        parts = 2
        span = modes // parts
        late = next_door(far, [from_sibling(cells) for cells in far], parts=parts)
        swapped = []
        for part, got in enumerate(late[1]):
            at = slice(part * span, (part + 1) * span)
            if part:
                got, _ = lax.optimization_barrier((got, sent))
            sent = jnp.where(
                group_index == goal,
                late[0][at] + got.astype(jnp.float32),
                early[0][at] + early[1][0][at].astype(jnp.float32),
            ).astype(jnp.bfloat16)
            swapped.append(lax.ppermute(sent, "atoms", [(z, z ^ 2) for z in range(atom_count)]))
        early, late = [[early[0]], early[1], swapped], [[late[0]], late[1], swapped]
    else:

        def settled(some_mine, some_theirs, shift):
            cells = all_products(chunks, half, partners, some_mine, some_theirs)
            cells, bit = settle(cells.reshape(-1, rows_dev, part_cols), 0, rows_dev)
            return collected([cells], bit, shift)

        early, late = settled(mine, theirs, 0), None
        for shift, far in far_all.items():
            terms = settled(far, [from_sibling(cells) for cells in far], shift)
            if late is None:
                late = terms
            else:
                here = (group_index ^ shift) == goal
                late = [jnp.where(here, new, old) for new, old in zip(terms, late)]
        early, late = [[term] for term in early], [[term] for term in late]

    my_freq = lax.dynamic_slice_in_dim(panel_freq, atom_index * rows_dev, rows_dev, 0)
    flag = jnp.stack(
        [
            (group_index == goal).astype(jnp.int32),
            (column_index * part_cols).astype(jnp.int32),
            atom_index.astype(jnp.int32),
        ]
    )
    elements, numerator = finish(
        flag,
        early,
        late,
        win_start.reshape(atom_count, rows_dev),
        win_len.reshape(atom_count, rows_dev),
        panel_freq.reshape(atom_count, rows_dev),
        partner_freq[None, :],
        1.0 / math.sqrt(3 * atom_rows * atom_count),
    )
    numerator = numerator + lax.ppermute(numerator, "sub", [(0, 1), (1, 0)])
    step = 1
    while step < groups:
        numerator = numerator + lax.ppermute(numerator, "modes", [(m, m ^ step) for m in range(groups)])
        step *= 2
    diffusivity = math.pi / 3.0 * numerator[0] / (my_freq * my_freq)
    return (elements, diffusivity)


def solution(mesh):
    return jax.shard_map(
        body,
        mesh=mesh,
        in_specs=(
            P(None, ("dom", "atoms"), ("modes", "sub")),
            P(None, ("dom", "atoms"), ("modes", "sub")),
            P(None, ("dom", "atoms"), None),
            P(("dom", "atoms"), None),
            P(("dom", "atoms")),
            P("dom"),
            P(("dom", "modes", "sub")),
            P("dom"),
            P("dom"),
        ),
        out_specs=(P(("dom", "atoms"), ("modes", "sub")), P(("dom", "atoms"))),
        check_vma=False,
    )
```

```python
import math

import jax
import jax.numpy as jnp
from jax import lax
from jax.experimental import pallas as pl
from jax.experimental.pallas import tpu as pltpu
from jax.sharding import PartitionSpec as P

HALO = 96
BONDS = 16
LANES = 128
SPAN = LANES + 2 * HALO
GROUP = 16
VMEM_BYTES = 14 * 1024 * 1024

lorentz_width = 0.05

EARLY_US = 6.0
LATE_US = 0.1

HBM = pl.BlockSpec(memory_space=pltpu.HBM)
ANY = pl.BlockSpec(memory_space=pl.ANY)
VMEM = pl.BlockSpec(memory_space=pltpu.VMEM)
SMEM = pl.BlockSpec(memory_space=pltpu.SMEM)


def call(kernel, name, in_specs, out_specs, out_shape, operands, busy_us, scratch=()):
    operands = [
        pltpu.with_memory_space_constraint(x, spec.memory_space) if spec is VMEM or spec is HBM else x
        for spec, x in zip(in_specs, operands)
    ]
    return pl.pallas_call(
        kernel,
        in_specs=in_specs,
        out_specs=out_specs,
        out_shape=out_shape,
        scratch_shapes=list(scratch),
        compiler_params=pltpu.CompilerParams(vmem_limit_bytes=VMEM_BYTES),
        cost_estimate=pl.CostEstimate(
            flops=int(busy_us * 1.1e9), bytes_accessed=int(busy_us * 1e5), transcendentals=0
        ),
        name=name,
    )(*operands)


def runs_of(blocks):
    runs = []
    for place, block in enumerate(blocks):
        if runs and runs[-1][1] + runs[-1][2] == block:
            runs[-1][2] += 1
        else:
            runs.append([place, block, 1])
    return runs


def build_block(first, base, nbr_ref, coef_ref, count_ref, dense_ref):
    lanes = pl.ds(first, LANES)
    target = nbr_ref[:, lanes] - (base + (first - HALO))
    slot_ids = lax.broadcasted_iota(jnp.int32, (BONDS, LANES), 0)
    live = slot_ids < count_ref[lanes].reshape(1, LANES)
    coefs = [jnp.where(live, coef_ref[e, :, lanes], 0.0) for e in range(9)]
    halves = [(target[h : h + 8], slot_ids[h : h + 8]) for h in (0, 8)]
    merged = [[jnp.zeros((8, LANES), jnp.float32) for _ in range(9)] for _ in range(2)]
    named = [jnp.broadcast_to(target[k : k + 1], (8, LANES)) for k in range(BONDS)]
    for k in range(BONDS):
        rows = [jnp.broadcast_to(coefs[e][k : k + 1], (8, LANES)) for e in range(9)]
        for h in range(k // 8, 2):
            same = (halves[h][0] == named[k]) & (halves[h][1] >= k)
            for e in range(9):
                merged[h][e] = merged[h][e] + jnp.where(same, rows[e], 0.0)
    row_ids = lax.broadcasted_iota(jnp.int32, (8, LANES), 0)

    def group_step(g, carry):
        cells = [[] for _ in range(9)]
        for tile in range(GROUP // 8):
            here = row_ids + (g * GROUP + tile * 8)
            slot = jnp.full((8, LANES), -1, jnp.int32)
            for k in range(BONDS):
                slot = jnp.where(named[k] == here, k, slot)
            place = slot & 7
            early, live_cell = slot < 8, slot >= 0
            for e in range(9):
                picks = [
                    jnp.take_along_axis(merged[h][e], place, axis=0, mode="promise_in_bounds")
                    for h in range(2)
                ]
                cells[e].append(jnp.where(live_cell, jnp.where(early, picks[0], picks[1]), 0.0))
        for r in range(3):
            for c in range(3):
                value = jnp.concatenate(cells[3 * r + c], axis=0)
                high = value.astype(jnp.bfloat16)
                low = (value - high.astype(jnp.float32)).astype(jnp.bfloat16)
                at = pl.ds(pl.multiple_of(c * SPAN + g * GROUP, GROUP), GROUP)
                dense_ref[at, 2 * r * LANES : (2 * r + 1) * LANES] = high
                dense_ref[at, (2 * r + 1) * LANES : (2 * r + 2) * LANES] = low
        return carry

    lax.fori_loop(0, SPAN // GROUP, group_step, 0)


def images_of(blocks, spot, panel, nbr, coef, count, halos=(), before=(), edges=False):
    rows, modes = panel.shape[1:]
    loads = len(before) == 0
    operands = [spot, nbr, count, coef, panel, *halos, *before]
    in_specs = [SMEM] + [HBM if loads else VMEM] * 4 + [VMEM] * len(halos) + [ANY] * len(before)
    width = len(blocks) * LANES
    out_shape = [pltpu.VMEM((modes, 3 * width), jnp.bfloat16)]
    out_specs = [VMEM]
    if edges:
        out_shape += [jax.ShapeDtypeStruct((3, HALO, modes), jnp.bfloat16)] * 2
        out_specs += [ANY] * 2
    n_in, n_out = len(operands), len(out_shape)

    def pieces_of(block):
        begin, end = block * LANES - HALO, (block + 1) * LANES + HALO
        found = []
        if begin < 0:
            found.append((1, HALO + begin, 0, -begin))
        low, high = max(begin, 0), min(end, rows)
        found.append((0, low, low - begin, high - low))
        if end > rows:
            found.append((2, 0, rows - begin, end - rows))
        return found

    def kernel(*refs):
        spot_ref, nbr_ref, count_ref, coef_ref, panel_ref = refs[:5]
        odd = spot_ref[1]
        outs = refs[n_in : n_in + n_out]
        window_ref, dense_ref, *scratch_refs = refs[n_in + n_out :]
        window_copies = []
        if loads:
            sources = (nbr_ref, count_ref, coef_ref)
            nbr_ref, count_ref, coef_ref, sems = scratch_refs
            copies = []

            def start(source, target, kept):
                copy = pltpu.make_async_copy(source, target, sems.at[len(copies) + len(window_copies)])
                copy.start()
                kept.append(copy)

            start(sources[0], nbr_ref, copies)
            start(sources[1], count_ref, copies)
            for _, block, length in runs_of(blocks):
                at = pl.ds(block * LANES, length * LANES)
                start(sources[2].at[:, :, at], coef_ref.at[:, :, at], copies)
            for place, block in enumerate(blocks):
                for _, source, at, length in pieces_of(block):
                    start(
                        panel_ref.at[:, pl.ds(source, length)], window_ref.at[place, :, pl.ds(at, length)], window_copies
                    )
            if edges:
                for turn, out in enumerate(outs[1:3]):
                    at = pl.multiple_of(jnp.where(odd == turn, rows - HALO, 0), 32)
                    start(panel_ref.at[:, pl.ds(at, HALO)], out, window_copies)
            for copy in copies:
                copy.wait()
        else:
            for place, block in enumerate(blocks):
                for which, source, at, length in pieces_of(block):
                    there = slice(source, source + length)
                    if which == 0:
                        found = panel_ref[:, there, :]
                    else:
                        found = jnp.where((odd == 1) == (which == 1), refs[5][:, there, :], refs[6][:, there, :])
                    window_ref[place, :, at : at + length, :] = found

        for place, block in enumerate(blocks):
            build_block(block * LANES, spot_ref[0], nbr_ref, coef_ref, count_ref, dense_ref)
            if loads and place == 0:
                for copy in window_copies:
                    copy.wait()
            both = lax.dot_general(
                window_ref[place].reshape(3 * SPAN, modes),
                dense_ref[...],
                (((0,), (0,)), ((), ())),
                preferred_element_type=jnp.float32,
            )
            for r in range(3):
                image = both[:, 2 * r * LANES : (2 * r + 1) * LANES]
                image = image + both[:, (2 * r + 1) * LANES : (2 * r + 2) * LANES]
                at = r * width + place * LANES
                outs[0][:, at : at + LANES] = image.astype(jnp.bfloat16)

    scratch = [
        pltpu.VMEM((len(blocks), 3, SPAN, modes), jnp.bfloat16),
        pltpu.VMEM((3 * SPAN, 6 * LANES), jnp.bfloat16),
    ]
    if loads:
        scratch += [
            pltpu.VMEM((BONDS, rows), jnp.int32),
            pltpu.VMEM((rows,), jnp.int32),
            pltpu.VMEM((9, BONDS, rows), jnp.float32),
            pltpu.SemaphoreType.DMA((4 + 3 * len(blocks) + 2,)),
        ]
    return call(kernel, "images", in_specs, out_specs, out_shape, operands, 0.8 + 1.2 * len(blocks), scratch)


def products_of(chunks, place, partners, mine, theirs, after=(), busy_us=2.0, parts=1):
    rows, cols = mine[0].shape[0], partners.shape[2]
    count = len(chunks)
    depth = partners.shape[1]

    def kernel(place_ref, partners_hbm, *refs):
        keep_ref, *send_refs = refs[-4 - parts : -3]
        left_ref, partners_ref, sems = refs[-3:]
        copies = [
            pltpu.make_async_copy(partners_hbm.at[r], partners_ref.at[r], sems.at[r]) for r in range(3)
        ]
        for copy in copies:
            copy.start()
        kept = place_ref[0] == place_ref[1]
        for who in range(2):
            at_rows = pl.ds(pl.multiple_of(jnp.where(kept == (who == 0), 0, rows), rows), rows)
            for i, blocks in enumerate(chunks):
                image_ref = refs[who * count + i]
                width = len(blocks) * LANES
                for r in range(3):
                    for spot, block, length in runs_of(blocks):
                        at, to = r * width + spot * LANES, r * depth + block * LANES
                        left_ref[at_rows, to : to + length * LANES] = image_ref[:, at : at + length * LANES]
        total = None
        for r, copy in enumerate(copies):
            copy.wait()
            part = jnp.dot(
                left_ref[:, r * depth : (r + 1) * depth], partners_ref[r], preferred_element_type=jnp.float32
            )
            total = part if total is None else total + part
        keep_ref[...] = total[:rows]
        for part, send_ref in enumerate(send_refs):
            at = rows + part * (rows // parts)
            send_ref[...] = total[at : at + rows // parts].astype(jnp.bfloat16)

    return call(
        kernel,
        "products",
        [SMEM, HBM] + [VMEM] * (2 * count) + [ANY] * len(after),
        [VMEM] * (1 + parts),
        [pltpu.VMEM((rows, cols), jnp.float32)] + [pltpu.VMEM((rows // parts, cols), jnp.bfloat16)] * parts,
        (place, partners, *mine, *theirs, *after),
        busy_us,
        [
            pltpu.VMEM((2 * rows, 3 * depth), jnp.bfloat16),
            pltpu.VMEM((3, depth, cols), jnp.bfloat16),
            pltpu.SemaphoreType.DMA((3,)),
        ],
    )


def all_products(chunks, half, partners, mine, theirs):
    place = jnp.stack([half, jnp.zeros((), jnp.int32)])
    low = products_of(chunks, place, partners, mine, theirs)[0]
    high = products_of(chunks, place + jnp.array([0, 1], jnp.int32), partners, mine, theirs)[0]
    return jnp.stack([low, high])


def settle(cells, bit, rows_dev):
    depth = lax.axis_size("atoms")
    place = lax.axis_index("atoms")
    while cells.shape[0] > 1:
        pairs = cells.reshape(cells.shape[0] // 2, 2, rows_dev, -1)
        own = (place >> bit) & 1
        keep = lax.dynamic_index_in_dim(pairs, own, 1, keepdims=False)
        send = lax.dynamic_index_in_dim(pairs, 1 - own, 1, keepdims=False)
        step = 1 << bit
        got = lax.ppermute(send.astype(jnp.bfloat16), "atoms", [(z, z ^ step) for z in range(depth)])
        cells = keep + got.astype(jnp.float32)
        bit += 1
    return cells[0], bit


def collected(terms, bit, shift):
    groups, depth = lax.axis_size("modes"), lax.axis_size("atoms")
    level = 0
    while (1 << level) < groups:
        moves = []
        for z in range(depth):
            for m in range(groups):
                goal = m ^ shift
                settled = all(((z >> (bit + u)) ^ (goal >> u)) & 1 == 0 for u in range(level))
                if settled and ((z >> (bit + level)) ^ (goal >> level)) & 1:
                    moves.append((z * groups + m, (z ^ (1 << (bit + level))) * groups + m))
        sent = sum(term.astype(jnp.float32) for term in terms).astype(jnp.bfloat16)
        terms = terms + [lax.ppermute(sent, ("atoms", "modes"), moves)]
        level += 1
    return terms


def finish(flag, early, late, starts, lengths, freqs, partner_freq, norm_scale):
    rows, cols = early[0][0].shape
    terms = early + late
    operands = [flag, starts, lengths, freqs, partner_freq, *[piece for term in terms for piece in term]]
    step = 16

    def kernel(flag_ref, starts_ref, lengths_ref, freqs_ref, partner_ref, *refs):
        out_ref, sum_ref, start_ref, end_ref, freq_ref, folded_ref = refs[-6:]
        pieces = iter(refs[:-6])
        grouped = [[next(pieces) for _ in term] for term in terms]

        def add_up(some):
            out_ref[...] = some[0][0][...]
            for term in some[1:]:
                span = rows // len(term)
                for i, ref in enumerate(term):
                    at = slice(i * span, (i + 1) * span)
                    out_ref[at, :] = out_ref[at, :] + ref[...].astype(jnp.float32)

        @pl.when(flag_ref[0] == 1)
        def _():
            add_up(grouped[: len(early)])

        @pl.when(flag_ref[0] == 0)
        def _():
            add_up(grouped[len(early) :])

        def turned(row):
            return jnp.broadcast_to(row, (LANES, rows)).T

        mine = pl.ds(flag_ref[2], 1)
        start_row = starts_ref[mine, :].astype(jnp.float32)
        start_ref[...] = turned(start_row)
        end_ref[...] = turned(start_row + lengths_ref[mine, :].astype(jnp.float32))
        freq_ref[...] = turned(freqs_ref[mine, :])
        lane_ids = lax.broadcasted_iota(jnp.int32, (step, LANES), 1)

        def row_step(i, carry):
            at_rows = pl.ds(pl.multiple_of(i * step, step), step)
            start, end, freq = start_ref[at_rows, :], end_ref[at_rows, :], freq_ref[at_rows, :]
            folded = jnp.zeros((step, LANES), jnp.float32)
            for at in range(0, cols, LANES):
                columns = (lane_ids + (flag_ref[1] + at)).astype(jnp.float32)
                inside = (columns >= start) & (columns < end)
                elements = jnp.where(inside, out_ref[at_rows, at : at + LANES] * norm_scale, 0.0)
                out_ref[at_rows, at : at + LANES] = elements
                offset = freq - partner_ref[:, at : at + LANES]
                lorentz = lorentz_width / (math.pi * (offset * offset + lorentz_width * lorentz_width))
                folded = folded + jnp.where(inside, lorentz, 0.0) * elements * elements
            folded_ref[at_rows, :] = folded
            return carry

        lax.fori_loop(0, rows // step, row_step, 0)
        sum_ref[...] = jnp.sum(folded_ref[...].T, axis=0, keepdims=True)

    return call(
        kernel,
        "finish",
        [SMEM] + [VMEM] * (len(operands) - 1),
        [VMEM, VMEM],
        [jax.ShapeDtypeStruct((rows, cols), jnp.float32), jax.ShapeDtypeStruct((1, rows), jnp.float32)],
        operands,
        2.0,
        [pltpu.VMEM((rows, LANES), jnp.float32)] * 4,
    )


def body(
    mode_panel,
    partners,
    bond_blocks,
    neighbors,
    bond_count,
    panel_freq,
    partner_freq,
    win_start,
    win_len,
):
    atom_rows, modes = mode_panel.shape[1:]
    atom_index = lax.axis_index("atoms")
    atom_count = lax.axis_size("atoms")
    groups = lax.axis_size("modes")
    group_index = lax.axis_index("modes")
    half_index = lax.axis_index("sub")
    column_index = lax.axis_index(("modes", "sub"))
    part_cols = partners.shape[2]
    panel_total = win_start.shape[0]
    rows_dev = panel_total // atom_count

    nbr = neighbors.T
    coef = bond_blocks.transpose(0, 2, 1)
    spot = jnp.stack([(atom_index * atom_rows).astype(jnp.int32), (atom_index & 1).astype(jnp.int32)])

    last = atom_rows // LANES - 1
    middle = list(range(1, last))
    cut = len(middle) // 2
    chunks = [middle[:cut], middle[cut:], [last, 0]]
    shared = (spot, mode_panel, nbr, coef, bond_count)
    near, edge_one, edge_two = images_of(chunks[0], *shared, edges=True)
    pairs = [(z, z ^ 1) for z in range(atom_count)]
    others = [(z, (z + 1 if z & 1 else z - 1) % atom_count) for z in range(atom_count)]
    halos = (lax.ppermute(edge_one, "atoms", pairs), lax.ppermute(edge_two, "atoms", others))

    def from_group(cells, shift):
        return lax.ppermute(cells, "modes", [(m ^ shift, m) for m in range(groups)])

    def from_sibling(cells):
        return lax.ppermute(cells, "sub", [(0, 1), (1, 0)])

    far_all = {shift: [from_group(near, shift)] for shift in range(1, groups)}
    middle_images = images_of(chunks[1], *shared, before=[near])[0]
    before = [middle_images, *[far[0] for far in far_all.values()]]
    mine = [near, middle_images, images_of(chunks[2], *shared, halos=halos, before=before)[0]]
    for shift, far in far_all.items():
        far += [from_group(cells, shift) for cells in mine[1:]]
    late_near, late_middle, late_edge = lax.optimization_barrier(tuple(mine))
    theirs = [from_sibling(cells) for cells in (late_near, late_middle, late_edge)]
    half = half_index.astype(jnp.int32)
    goal = atom_index * groups // atom_count

    if rows_dev == modes and groups == 2:
        place = jnp.stack([half, (atom_index & 1).astype(jnp.int32)])

        def next_door(some_mine, some_theirs, after=(), parts=1):
            keep, *sends = products_of(
                chunks, place, partners, some_mine, some_theirs, after, EARLY_US if after else LATE_US, parts
            )
            return keep, [lax.ppermute(send, "atoms", pairs) for send in sends]

        far = far_all[1]
        early = next_door(mine, theirs, far[:2])
        third, kept = lax.optimization_barrier((far[2], early[0]))
        early = (kept, early[1])
        far = [far[0], far[1], third]
        parts = 2
        span = modes // parts
        late = next_door(far, [from_sibling(cells) for cells in far], parts=parts)
        swapped = []
        for part, got in enumerate(late[1]):
            at = slice(part * span, (part + 1) * span)
            if part:
                got, _ = lax.optimization_barrier((got, sent))
            sent = jnp.where(
                group_index == goal,
                late[0][at] + got.astype(jnp.float32),
                early[0][at] + early[1][0][at].astype(jnp.float32),
            ).astype(jnp.bfloat16)
            swapped.append(lax.ppermute(sent, "atoms", [(z, z ^ 2) for z in range(atom_count)]))
        early, late = [[early[0]], early[1], swapped], [[late[0]], late[1], swapped]
    else:

        def settled(some_mine, some_theirs, shift):
            cells = all_products(chunks, half, partners, some_mine, some_theirs)
            cells, bit = settle(cells.reshape(-1, rows_dev, part_cols), 0, rows_dev)
            return collected([cells], bit, shift)

        early, late = settled(mine, theirs, 0), None
        for shift, far in far_all.items():
            terms = settled(far, [from_sibling(cells) for cells in far], shift)
            if late is None:
                late = terms
            else:
                here = (group_index ^ shift) == goal
                late = [jnp.where(here, new, old) for new, old in zip(terms, late)]
        early, late = [[term] for term in early], [[term] for term in late]

    my_freq = lax.dynamic_slice_in_dim(panel_freq, atom_index * rows_dev, rows_dev, 0)
    flag = jnp.stack(
        [
            (group_index == goal).astype(jnp.int32),
            (column_index * part_cols).astype(jnp.int32),
            atom_index.astype(jnp.int32),
        ]
    )
    elements, numerator = finish(
        flag,
        early,
        late,
        win_start.reshape(atom_count, rows_dev),
        win_len.reshape(atom_count, rows_dev),
        panel_freq.reshape(atom_count, rows_dev),
        partner_freq[None, :],
        1.0 / math.sqrt(3 * atom_rows * atom_count),
    )
    numerator = numerator + lax.ppermute(numerator, "sub", [(0, 1), (1, 0)])
    step = 1
    while step < groups:
        numerator = numerator + lax.ppermute(numerator, "modes", [(m, m ^ step) for m in range(groups)])
        step *= 2
    diffusivity = math.pi / 3.0 * numerator[0] / (my_freq * my_freq)
    return (elements, diffusivity)


def solution(mesh):
    return jax.shard_map(
        body,
        mesh=mesh,
        in_specs=(
            P(None, ("dom", "atoms"), ("modes", "sub")),
            P(None, ("dom", "atoms"), ("modes", "sub")),
            P(None, ("dom", "atoms"), None),
            P(("dom", "atoms"), None),
            P(("dom", "atoms")),
            P("dom"),
            P(("dom", "modes", "sub")),
            P("dom"),
            P("dom"),
        ),
        out_specs=(P(("dom", "atoms"), ("modes", "sub")), P(("dom", "atoms"))),
        check_vma=False,
    )
```
